32 devices in a mesh: section: 4 (over x, core), dp: 8 (over z, y).
Axes of the slice: x: 2, y: 2, z: 4, core: 2. Of those that a mesh axis runs over, the one named last changes fastest.
Arguments:
- inputs: bfloat16 [4, 128, 64, 512], P(None, 'dp'), may hold values from -6 to 6
- cotangent: bfloat16 [4, 128, 64, 512], P(None, 'dp'), may hold values from -6 to 6
- segments: int32 [4, 128, 64], P(None, 'dp'), may hold values from 0 to 1, as said below
- observed: int32 [4, 128, 64], P(None, 'dp'), may hold values from 0 to 1, as said below
- q_weight: bfloat16 [2, 512, 384], P(None, 'dp'), may hold values from -0.0625 to 0.0625
- k_weight: bfloat16 [2, 512, 384], P(None, 'dp'), may hold values from -0.25 to 0.25
- v_weight: bfloat16 [2, 512, 384], P(None, 'dp'), may hold values from -0.25 to 0.25
- o_weight: bfloat16 [2, 384, 512], P(None, 'dp'), may hold values from -0.875 to 0.875
- gate_weight: bfloat16 [2, 512, 1024], P(None, 'dp'), may hold values from -0.25 to 0.25
- up_weight: bfloat16 [2, 512, 1024], P(None, 'dp'), may hold values from -0.25 to 0.25
- down_weight: bfloat16 [2, 1024, 512], P(None, 'dp'), may hold values from -0.25 to 0.25
- gains: bfloat16 [2, 2, 512], P(None, None, 'dp'), may hold values from 0.5 to 1.5
- position_table: bfloat16 [32, 6], replicated, may hold values from -4 to 4
Outputs:
- section_outputs: bfloat16 [4, 4, 128, 64, 512], P('section', None, 'dp')
- section_grads: bfloat16 [4, 4, 128, 64, 512], P('section', None, 'dp')
- q_grad: float32 [2, 512, 384], P(None, 'dp')
- k_grad: float32 [2, 512, 384], P(None, 'dp')
- v_grad: float32 [2, 512, 384], P(None, 'dp')
- o_grad: float32 [2, 384, 512], P(None, 'dp')
- gate_grad: float32 [2, 512, 1024], P(None, 'dp')
- up_grad: float32 [2, 512, 1024], P(None, 'dp')
- down_grad: float32 [2, 1024, 512], P(None, 'dp')
- gains_grad: float32 [2, 2, 512], P(None, None, 'dp')
- table_grad: float32 [32, 6], replicated
The draws below stay inside these ranges and needn't reach their ends.
Inputs may be any that keep to these rules, and one draw needn't show every extreme that they name: `segments`: each row holds either one series of 64 patches, all numbered 0, or two series of 32 patches, numbered 0 then 1. Patches 0 and 32 of every row are observed.
All inputs are finite; a program needn't handle non-finite values.
Results may differ from the reference program's by a relative error of at most 0.03.
Values may be sent and summed in bfloat16 or wider, within the bound.
No kernel may reach another device: no remote copies, remote signals or barrier semaphores. Data moves between devices by JAX's collectives and lax.ppermute only.
A program may use at most 256 MiB of HBM per device.

```python
import jax
import jax.numpy as jnp
from jax import lax

D = 512
HEADS = 6
INNER = 384
FF = 1024
BUCKETS = 32
SEQ = 64
MICRO = 4
ROWS_DEV = 16
LAYERS = 2
BATCH = 128
N_DP = 8


def draw_segments(key, part):
    key = jax.random.fold_in(key, 11)
    series_flag = jax.random.randint(key, (MICRO, BATCH, 1), 0, 2)
    position = jnp.arange(SEQ, dtype=jnp.int32)
    later_half = (position >= SEQ // 2).astype(jnp.int32)
    return (series_flag * later_half[None, None, :]).astype(jnp.int32)


def draw_observed(key, part):
    key = jax.random.fold_in(key, 23)
    random_bits = (jax.random.randint(key, (MICRO, BATCH, SEQ), 0, 5) > 0).astype(jnp.int32)
    position = jnp.arange(SEQ, dtype=jnp.int32)
    forced = ((position == 0) | (position == SEQ // 2)).astype(jnp.int32)
    return jnp.maximum(random_bits, forced[None, None, :]).astype(jnp.int32)


def raised(values, stream_key, source, target, shards_of, factor):
    owner, partner = [(jnp.arange(values.shape[axis_at]) // (values.shape[axis_at] // shards_of)).reshape([-1 if axis == axis_at else 1 for axis in range(values.ndim)]) for axis_at in (source, target)]
    chosen = jax.random.permutation(stream_key, shards_of)[partner]
    strong = (owner == chosen) | (owner == (partner + shards_of // 2) % shards_of)
    return jnp.where(strong, factor * values, values)


def level_of(rng, extent, shards, smallest, high):
    def one(dim, parts):
        steps = jax.random.uniform(jax.random.fold_in(jax.random.fold_in(rng, 6), dim), (parts,), jnp.float32, smallest / len(shards), high / len(shards))
        return jnp.repeat(jnp.exp(steps), extent[dim] // parts).reshape((-1,) + (1,) * (len(extent) - dim - 1))

    gain = one(*shards[0])
    for cut in shards[1:]:
        gain = gain * one(*cut)
    return gain


def bell_draw(own_key, dims, scale, most, pieces=(), kind=jnp.bfloat16):
    array = jax.random.normal(own_key, dims, jnp.float32) * scale
    if len(pieces) > 0:
        array = level_of(own_key, dims, pieces, -0.22, 0.18) * array
    return jnp.clip(array, min=-most, max=most).astype(kind)


def heavy_noise(key, shape, deviation, reach, cuts, heavy, kind=jnp.bfloat16):
    entries = deviation * jax.random.normal(key, shape, jnp.float32)
    if cuts:
        entries = entries * level_of(key, shape, cuts, -0.22, 0.18)
    return jnp.clip(raised(entries, jax.random.fold_in(key, 3), *heavy), -reach, reach).astype(kind)


def setup_inputs(seed: int = 0) -> dict:
    splits = jax.random.split(jax.random.key(seed), 14)
    inputs = heavy_noise(splits[0], (MICRO, BATCH, SEQ, D), 1.0, 6.0, ((1, 8),), (1, 3, 8, 2.0))
    cotangent = bell_draw(splits[1], (MICRO, BATCH, SEQ, D), 1.0, 6.0, ((1, 8),))
    segments = draw_segments(jax.random.fold_in(splits[13], 71), 0)
    observed = draw_observed(jax.random.fold_in(splits[13], 71), 0)
    q_weight = bell_draw(splits[4], (LAYERS, D, INNER), (16 * D) ** -0.5, 0.0625, ((1, 8),))
    k_weight = bell_draw(splits[5], (LAYERS, D, INNER), D ** -0.5, 0.25, ((1, 8),))
    v_weight = bell_draw(splits[6], (LAYERS, D, INNER), D ** -0.5, 0.25, ((1, 8),))
    o_weight = bell_draw(splits[7], (LAYERS, INNER, D), (INNER // 8) ** -0.5, 0.875, ((1, 8),))
    gate_weight = bell_draw(splits[8], (LAYERS, D, FF), D ** -0.5, 0.25, ((1, 8),))
    up_weight = bell_draw(splits[9], (LAYERS, D, FF), D ** -0.5, 0.25, ((1, 8),))
    down_weight = bell_draw(splits[10], (LAYERS, FF, D), (FF // 2) ** -0.5, 0.25, ((1, 8),))
    gains = jnp.clip(1.0 + 0.1 * jax.random.normal(splits[11], (LAYERS, 2, D), jnp.float32), 0.5, 1.5).astype(jnp.bfloat16)
    position_table = bell_draw(splits[12], (BUCKETS, HEADS), 1.0, 4.0)
    return dict(inputs=inputs, cotangent=cotangent, segments=segments, observed=observed, q_weight=q_weight, k_weight=k_weight, v_weight=v_weight, o_weight=o_weight, gate_weight=gate_weight, up_weight=up_weight, down_weight=down_weight, gains=gains, position_table=position_table)


@jax.custom_vjp
def low(v):
    return lax.optimization_barrier(v.astype(jnp.bfloat16)).astype(jnp.float32)

@jax.custom_vjp
def low_back(v):
    return v

def low_keep(v):
    return (low(v), None)

def low_pass(kept, grad):
    return (grad,)

def back_keep(v):
    return (v, None)

def back_low(kept, grad):
    return (low(grad),)
low.defvjp(low_keep, low_pass)
low_back.defvjp(back_keep, back_low)
eps_norm = 1e-06
limits = (12, 16, 23, 32, 46, 64, 91)
masked = -1e+30
highest = lax.Precision.HIGHEST

def bucket_onehot(seq_count, bucket_count):
    position = jnp.arange(seq_count, dtype=jnp.int32)
    offset = position[None, :] - position[:, None]
    distance = jnp.abs(offset)
    far_bucket = jnp.full(distance.shape, 8, jnp.int32)
    for threshold in limits:
        far_bucket = far_bucket + (distance >= threshold).astype(jnp.int32)
    bucket = jnp.where(distance < 8, distance, jnp.minimum(far_bucket, 15)) + 16 * (offset > 0).astype(jnp.int32)
    return (bucket[:, :, None] == jnp.arange(bucket_count, dtype=jnp.int32)[None, None, :]).astype(jnp.float32)

def normalize(values):
    return values * lax.rsqrt(lax.optimization_barrier(jnp.mean(values * values, axis=-1, keepdims=True)) + eps_norm)

def project(operand, matrix):
    return jnp.einsum('rsd,de->rse', operand, matrix, precision=highest)

def attention_sublayer(stream, weights, position_bias, allowed):
    q_weight, k_weight, v_weight, o_weight, gain_row = weights
    row_count, seq_count, model_width = stream.shape
    head_count = position_bias.shape[0]
    attn_in = low(normalize(stream) * gain_row)
    query_low = low(low_back(project(attn_in, q_weight))).reshape(row_count, seq_count, head_count, -1)
    key_low = low(low_back(project(attn_in, k_weight))).reshape(row_count, seq_count, head_count, -1)
    value_low = low(low_back(project(attn_in, v_weight))).reshape(row_count, seq_count, head_count, -1)
    scores = jnp.einsum('rihd,rjhd->rhij', query_low, key_low, precision=highest) + position_bias[None]
    scores = jnp.where(allowed[:, None], low_back(scores), masked)
    prob_low = low(jax.nn.softmax(scores, axis=-1))
    attended = jnp.einsum('rhij,rjhd->rihd', prob_low, value_low, precision=highest).reshape(row_count, seq_count, -1)
    attended = low(low_back(attended))
    return stream + low_back(project(attended, o_weight))

def ffn_sublayer(stream, weights):
    gate_weight, up_weight, down_weight, gain_row = weights
    ffn_in = low(normalize(stream) * gain_row)
    gate_act = low_back(project(ffn_in, gate_weight))
    up_act = low_back(project(ffn_in, up_weight))
    hidden = low(jax.nn.gelu(gate_act, approximate=True) * up_act)
    return stream + low_back(project(hidden, down_weight))

def encoder(stream, shifts, params, bias_table, onehot, allowed):
    q_weight, k_weight, v_weight, o_weight, gate_weight, up_weight, down_weight, gains = params
    position_bias = jnp.einsum('ijb,bh->hij', onehot, bias_table, precision=highest)
    states = []
    for section_index in range(2 * LAYERS):
        layer_index = section_index // 2
        stream = low_back(stream) + shifts[section_index]
        if section_index % 2 == 0:
            weights = (q_weight[layer_index], k_weight[layer_index], v_weight[layer_index], o_weight[layer_index], gains[layer_index, 0])
            stream = low(attention_sublayer(stream, weights, position_bias, allowed))
        else:
            weights = (gate_weight[layer_index], up_weight[layer_index], down_weight[layer_index], gains[layer_index, 1])
            stream = low(ffn_sublayer(stream, weights))
        states.append(stream)
    return jnp.stack(states)

def reference(inputs, cotangent, segments, observed, q_weight, k_weight, v_weight, o_weight, gate_weight, up_weight, down_weight, gains, position_table):
    params = tuple((weight_set.astype(jnp.float32) for weight_set in (q_weight, k_weight, v_weight, o_weight, gate_weight, up_weight, down_weight, gains)))
    bias_table = position_table.astype(jnp.float32)
    onehot = bucket_onehot(SEQ, BUCKETS)
    block_count = MICRO * N_DP
    block_inputs = inputs.reshape(block_count, ROWS_DEV, SEQ, D)
    block_cot = cotangent.reshape(block_count, ROWS_DEV, SEQ, D)
    block_segments = segments.reshape(block_count, ROWS_DEV, SEQ)
    block_observed = observed.reshape(block_count, ROWS_DEV, SEQ)

    def scan_step(totals, block_data):
        block_in, block_grad, block_seg, block_obs = block_data
        allowed = (block_seg[:, :, None] == block_seg[:, None, :]) & (block_obs[:, None, :] == 1)
        zero_shift = jnp.zeros((2 * LAYERS,) + block_in.shape, jnp.float32)

        def forward(stream, shifts, weight_sets, table_values):
            return encoder(stream, shifts, weight_sets, table_values, onehot, allowed)
        states, pullback = jax.vjp(forward, block_in.astype(jnp.float32), zero_shift, params, bias_table)
        cot_full = jnp.zeros_like(states).at[2 * LAYERS - 1].set(block_grad.astype(jnp.float32))
        unused, shift_grads, param_grads, table_part = pullback(cot_full)
        totals = jax.tree.map(jnp.add, totals, (param_grads, table_part))
        return (totals, (states.astype(jnp.bfloat16), shift_grads.astype(jnp.bfloat16)))
    initial = (jax.tree.map(jnp.zeros_like, params), jnp.zeros_like(bias_table))
    (param_grads, table_grad), (states, shift_grads) = lax.scan(scan_step, initial, (block_inputs, block_cot, block_segments, block_observed))
    section_outputs = states.reshape(MICRO, N_DP, 2 * LAYERS, ROWS_DEV, SEQ, D).transpose(2, 0, 1, 3, 4, 5).reshape(2 * LAYERS, MICRO, BATCH, SEQ, D)
    section_grads = shift_grads.reshape(MICRO, N_DP, 2 * LAYERS, ROWS_DEV, SEQ, D).transpose(2, 0, 1, 3, 4, 5).reshape(2 * LAYERS, MICRO, BATCH, SEQ, D)
    return (section_outputs, section_grads, param_grads[0], param_grads[1], param_grads[2], param_grads[3], param_grads[4], param_grads[5], param_grads[6], param_grads[7], table_grad)
```

```python
import jax
import jax.numpy as jnp
from jax import lax
from jax.experimental import pallas as pl
from jax.experimental.pallas import tpu as pltpu
from jax.sharding import PartitionSpec as P

eps_norm = 1e-06
limits = (12, 16, 23, 32, 46, 64, 91)
masked = -1e30
bf = jnp.bfloat16
f32 = jnp.float32
vmem_limit = 60 * 1024 * 1024


def dot_nn(a, b):
    return lax.dot_general(a, b, (((1,), (0,)), ((), ())), preferred_element_type=f32)


def dot_nt(a, b):
    return lax.dot_general(a, b, (((1,), (1,)), ((), ())), preferred_element_type=f32)


def dot_tn(a, b):
    return lax.dot_general(a, b, (((0,), (0,)), ((), ())), preferred_element_type=f32)


def row_scale(x):
    return lax.rsqrt(jnp.mean(x * x, axis=-1, keepdims=True) + eps_norm)


def pair_parts(values):
    lane = lax.broadcasted_iota(jnp.int32, values.shape, 1)
    zero = jnp.zeros_like(values)
    return jnp.concatenate(
        [jnp.where(lane < 64, values, zero), jnp.where(lane < 64, zero, values)], axis=0
    )


def pair_pick(values):
    half = values.shape[0] // 2
    lane = lax.broadcasted_iota(jnp.int32, (half, values.shape[1]), 1)
    return jnp.where(lane < 64, values[:half], values[half:])


def pair_max(values):
    lane = lax.broadcasted_iota(jnp.int32, values.shape, 1)
    low = jnp.max(jnp.where(lane < 64, values, -jnp.inf), axis=-1, keepdims=True)
    high = jnp.max(jnp.where(lane < 64, -jnp.inf, values), axis=-1, keepdims=True)
    return jnp.where(lane < 64, low, high)


def pair_sum(values):
    lane = lax.broadcasted_iota(jnp.int32, values.shape, 1)
    low = jnp.sum(jnp.where(lane < 64, values, 0.0), axis=-1, keepdims=True)
    high = jnp.sum(jnp.where(lane < 64, 0.0, values), axis=-1, keepdims=True)
    return jnp.where(lane < 64, low, high)


def attn_fwd_kernel(x_ref, mask_ref, bias_ref, gain_ref, wq_ref, wk_ref, wv_ref, wo_ref,
                    out_ref, q_ref, k_ref, v_ref, p_ref, att_ref):
    x = x_ref[...].astype(f32)
    a = (x * row_scale(x) * gain_ref[...]).astype(bf)
    q = dot_nn(a, wq_ref[...]).astype(bf)
    k = dot_nn(a, wk_ref[...]).astype(bf)
    v = dot_nn(a, wv_ref[...]).astype(bf)
    q_ref[...] = q
    k_ref[...] = k
    v_ref[...] = v
    rows = x.shape[0] // 64
    units = [(r, h) for r in range(rows) for h in range(3)]
    at = lambda arr, r, h: arr[r * 64:r * 64 + 64, h * 128:h * 128 + 128]
    scores = [dot_nt(at(k, r, h), pair_parts(at(q, r, h))) for r, h in units]
    probs = []
    for (r, h), s in zip(units, scores):
        s = s + (bias_ref[:, h * 128:h * 128 + 128] + mask_ref[r])
        e = jnp.exp(s - jnp.max(s, axis=0, keepdims=True))
        p = (e * (1.0 / jnp.sum(e, axis=0, keepdims=True))).astype(bf)
        p_ref[r * 64:r * 64 + 64, h * 128:h * 128 + 128] = p
        probs.append(p)
    full_att = [dot_tn(p, at(v, r, h)) for (r, h), p in zip(units, probs)]
    att = {unit: pair_pick(part).astype(bf) for unit, part in zip(units, full_att)}
    att = jnp.concatenate([jnp.concatenate([att[r, h] for h in range(3)], axis=1) for r in range(rows)], axis=0)
    att_ref[...] = att
    out_ref[...] = (x + dot_nn(att, wo_ref[...])).astype(bf)


def attn_bwd_kernel(x_ref, q_ref, k_ref, v_ref, p_ref, att_ref, g_ref, gain_ref,
                    wq_ref, wk_ref, wv_ref, wo_ref,
                    gin_ref, dwq_ref, dwk_ref, dwv_ref, dwo_ref, dgain_ref, dbias_ref,
                    a_s, dq_s, dk_s, dv_s, att_s, g_s, dgain_s, dbias_s):
    step = pl.program_id(0)
    last = pl.num_programs(0) - 1
    block = x_ref.shape[0]

    @pl.when(step == 0)
    def _():
        dgain_s[...] = jnp.zeros_like(dgain_s)
        dbias_s[...] = jnp.zeros_like(dbias_s)

    here = pl.ds(pl.multiple_of(step * block, block), block)
    g_low = g_ref[...]
    da = dot_nt(g_low, wo_ref[...]).astype(bf)
    att_s[here, :] = att_ref[...]
    g_s[here, :] = g_low
    rows = block // 64
    units = [(r, h) for r in range(rows) for h in range(3)]
    at = lambda arr, r, h: arr[r * 64:r * 64 + 64, h * 128:h * 128 + 128]
    db = [None] * 3
    da_bds = [pair_parts(at(da, r, h)) for r, h in units]
    dps = [dot_nt(at(v_ref, r, h), da_bd) for (r, h), da_bd in zip(units, da_bds)]
    dv_u = {(r, h): dot_nn(at(p_ref, r, h), da_bd).astype(bf) for (r, h), da_bd in zip(units, da_bds)}
    dss = []
    for (r, h), dp in zip(units, dps):
        pf = at(p_ref, r, h).astype(f32)
        ds = pf * (dp - jnp.sum(pf * dp, axis=0, keepdims=True))
        db[h] = ds if db[h] is None else db[h] + ds
        dss.append(ds.astype(bf))
    dk_u = {(r, h): dot_nn(ds, pair_parts(at(q_ref, r, h))).astype(bf) for (r, h), ds in zip(units, dss)}
    full_dq = [dot_tn(ds, at(k_ref, r, h)) for (r, h), ds in zip(units, dss)]
    dq_u = {unit: pair_pick(part).astype(bf) for unit, part in zip(units, full_dq)}
    join = lambda u: jnp.concatenate([jnp.concatenate([u[r, h] for h in range(3)], axis=1) for r in range(rows)], axis=0)
    dq, dk, dv = join(dq_u), join(dk_u), join(dv_u)
    dq_s[here, :] = dq
    dk_s[here, :] = dk
    dv_s[here, :] = dv
    for h in range(3):
        dbias_s[:, h * 128:h * 128 + 128] += db[h]
    gx = dot_nt(dq, wq_ref[...]) + dot_nt(dk, wk_ref[...]) + dot_nt(dv, wv_ref[...])
    x = x_ref[...].astype(f32)
    r_ = row_scale(x)
    n = x * r_
    a_s[here, :] = (n * gain_ref[...]).astype(bf)
    dgain_s[...] += jnp.sum(gx * n, axis=0, keepdims=True)
    e = gx * gain_ref[...]
    dx = r_ * (e - n * jnp.mean(e * n, axis=-1, keepdims=True))
    gin_ref[...] = (g_low.astype(f32) + dx).astype(bf)

    @pl.when(step == last)
    def _():
        dwq_ref[...] = dot_tn(a_s[...], dq_s[...]).astype(bf)
        dwk_ref[...] = dot_tn(a_s[...], dk_s[...]).astype(bf)
        dwv_ref[...] = dot_tn(a_s[...], dv_s[...]).astype(bf)
        dwo_ref[...] = dot_tn(att_s[...], g_s[...]).astype(bf)
        dgain_ref[...] = dgain_s[...]
        dbias_ref[...] = dbias_s[...]


def gelu_parts(u):
    c = 0.7978845608028654
    u2 = u * u
    t = jnp.tanh(u * (c + (c * 0.044715) * u2))
    half = 0.5 + 0.5 * t
    act = u * half
    slope = half + (0.5 * u) * (1.0 - t * t) * (c + (3.0 * c * 0.044715) * u2)
    return act, slope


def gelu(u):
    c = 0.7978845608028654
    t = jnp.tanh(u * (c + (c * 0.044715) * (u * u)))
    return u * (0.5 + 0.5 * t)


def ffn_fwd_kernel(x_ref, gain_ref, wg_ref, wu_ref, wd_ref, out_ref, gate_ref, up_ref):
    x = x_ref[...].astype(f32)
    a = (x * row_scale(x) * gain_ref[...]).astype(bf)
    gate = dot_nn(a, wg_ref[...])
    up = dot_nn(a, wu_ref[...])
    gate_ref[...] = gate.astype(bf)
    up_ref[...] = up.astype(bf)
    hidden = (gelu(gate) * up).astype(bf)
    out_ref[...] = (x + dot_nn(hidden, wd_ref[...])).astype(bf)


def ffn_bwd_kernel(x_ref, gate_ref, up_ref, g_ref, gain_ref, wg_ref, wu_ref, wd_ref,
                   gin_ref, dwg_ref, dwu_ref, dwd_ref, dgain_ref,
                   a_s, gb_s, ub_s, hid_s, g_s, dgain_s):
    step = pl.program_id(0)
    last = pl.num_programs(0) - 1
    block = x_ref.shape[0]

    @pl.when(step == 0)
    def _():
        dgain_s[...] = jnp.zeros_like(dgain_s)

    here = pl.ds(pl.multiple_of(step * block, block), block)
    g_low = g_ref[...]
    g_s[here, :] = g_low
    hg = dot_nt(g_low, wd_ref[...])
    gate = gate_ref[...].astype(f32)
    up = up_ref[...].astype(f32)
    act, slope = gelu_parts(gate)
    hid_s[here, :] = (act * up).astype(bf)
    gb = (hg * up * slope).astype(bf)
    ub = (hg * act).astype(bf)
    gb_s[here, :] = gb
    ub_s[here, :] = ub
    gx = dot_nt(gb, wg_ref[...]) + dot_nt(ub, wu_ref[...])
    x = x_ref[...].astype(f32)
    r_ = row_scale(x)
    n = x * r_
    a_s[here, :] = (n * gain_ref[...]).astype(bf)
    dgain_s[...] += jnp.sum(gx * n, axis=0, keepdims=True)
    e = gx * gain_ref[...]
    dx = r_ * (e - n * jnp.mean(e * n, axis=-1, keepdims=True))
    gin_ref[...] = (g_low.astype(f32) + dx).astype(bf)

    @pl.when(step == last)
    def _():
        dwg_ref[...] = dot_tn(a_s[...], gb_s[...]).astype(bf)
        dwu_ref[...] = dot_tn(a_s[...], ub_s[...]).astype(bf)
        dwd_ref[...] = dot_tn(hid_s[...], g_s[...]).astype(bf)
        dgain_ref[...] = dgain_s[...]


def tok(block, width):
    return pl.BlockSpec((block, width), lambda i: (i, 0))


def full(shape):
    zero = (0,) * len(shape)
    return pl.BlockSpec(shape, lambda i: zero)


def sds(shape, dtype):
    return jax.ShapeDtypeStruct(shape, dtype)


def call(kernel, grid, in_specs, out_specs, out_shape, scratch, flops, byts, name):
    return pl.pallas_call(
        kernel, grid=(grid,), in_specs=in_specs, out_specs=out_specs, out_shape=out_shape,
        scratch_shapes=scratch, name=name,
        compiler_params=pltpu.CompilerParams(vmem_limit_bytes=vmem_limit),
        cost_estimate=pl.CostEstimate(flops=flops, bytes_accessed=byts, transcendentals=0),
    )


def attn_fwd(x, mask, bias, gain, wq, wk, wv, wo, block=256):
    t, d = x.shape
    inner = wq.shape[1]
    return call(attn_fwd_kernel, t // block,
        [tok(block, d), pl.BlockSpec((block // 64, 64, 128), lambda i: (i, 0, 0)), full(bias.shape),
         full((1, d)), full(wq.shape), full(wk.shape), full(wv.shape), full(wo.shape)],
        [tok(block, d)] + [tok(block, inner)] * 5,
        [sds((t, d), bf)] + [sds((t, inner), bf)] * 5, [],
        2 * t * d * inner * 4, 4 * t * d, "attn_fwd")(x, mask, bias, gain, wq, wk, wv, wo)


def attn_bwd(x, q, k, v, p, att, g, gain, wq, wk, wv, wo, block=256):
    t, d = x.shape
    inner = wq.shape[1]
    return call(attn_bwd_kernel, t // block,
        [tok(block, d)] + [tok(block, inner)] * 5 + [tok(block, d), full((1, d)),
         full(wq.shape), full(wk.shape), full(wv.shape), full(wo.shape)],
        [tok(block, d), full(wq.shape), full(wk.shape), full(wv.shape), full(wo.shape),
         full((1, d)), full((64, inner))],
        [sds((t, d), bf), sds(wq.shape, bf), sds(wk.shape, bf), sds(wv.shape, bf), sds(wo.shape, bf),
         sds((1, d), f32), sds((64, inner), f32)],
        [pltpu.VMEM((t, d), bf)] + [pltpu.VMEM((t, inner), bf)] * 4 + [pltpu.VMEM((t, d), bf),
         pltpu.VMEM((1, d), f32), pltpu.VMEM((64, inner), f32)],
        2 * t * d * inner * 8, 12 * t * d, "attn_bwd")(x, q, k, v, p, att, g, gain, wq, wk, wv, wo)


def ffn_fwd(x, gain, wg, wu, wd, block=256):
    t, d = x.shape
    ff = wg.shape[1]
    return call(ffn_fwd_kernel, t // block,
        [tok(block, d), full((1, d)), full(wg.shape), full(wu.shape), full(wd.shape)],
        [tok(block, d), tok(block, ff), tok(block, ff)],
        [sds((t, d), bf), sds((t, ff), bf), sds((t, ff), bf)], [],
        2 * t * d * ff * 3, 4 * t * d, "ffn_fwd")(x, gain, wg, wu, wd)


def ffn_bwd(x, gate, up, g, gain, wg, wu, wd, block=256):
    t, d = x.shape
    ff = wg.shape[1]
    return call(ffn_bwd_kernel, t // block,
        [tok(block, d), tok(block, ff), tok(block, ff), tok(block, d), full((1, d)),
         full(wg.shape), full(wu.shape), full(wd.shape)],
        [tok(block, d), full(wg.shape), full(wu.shape), full(wd.shape), full((1, d))],
        [sds((t, d), bf), sds(wg.shape, bf), sds(wu.shape, bf), sds(wd.shape, bf), sds((1, d), f32)],
        [pltpu.VMEM((t, d), bf)] + [pltpu.VMEM((t, ff), bf)] * 3 + [pltpu.VMEM((t, d), bf),
         pltpu.VMEM((1, d), f32)],
        2 * t * d * ff * 6, 12 * t * d, "ffn_bwd")(x, gate, up, g, gain, wg, wu, wd)


def z_shift(values, by):
    half = lax.axis_size("dp") // 2
    pairs = [(z * 2 + y, ((z + by) % half) * 2 + y) for z in range(half) for y in range(2)]
    return lax.ppermute(values, "dp", pairs)


def swapped(values, axis, bit):
    return lax.ppermute(values, axis, [(i, i ^ bit) for i in range(lax.axis_size(axis))])


def after(values, *others):
    return lax.optimization_barrier((values,) + others)[0]


def by_core(core, arrays):
    return jnp.where(core == 0, arrays[0], arrays[1])


def half_rows(core, matrix):
    half = matrix.shape[0] // 2
    return lax.dynamic_slice_in_dim(matrix, core * half, half, 0)


def fold_rows(matrix, unit):
    return jnp.concatenate(
        [matrix[at:at + unit] for at in range(0, matrix.shape[0], unit)], axis=1
    )


def gather_part(piece, place):
    z, y, core = place
    half = lax.axis_size("dp") // 2
    got = [piece] + [z_shift(piece, by) for by in range(1, half)]
    column = jnp.stack([lax.select_n((z - at) % half, *got) for at in range(half)])
    other = swapped(column, "dp", 1)
    both = jnp.stack([by_core(y, (column, other)), by_core(y, (other, column))], axis=1)
    peer = swapped(both, "section", 1)
    whole = jnp.stack([by_core(core, (both, peer)), by_core(core, (peer, both))], axis=2)
    return whole, got[-1]


def reduce_part(packed, place):
    z, y, core = place
    half = lax.axis_size("dp") // 2

    def added(*terms):
        total = terms[0].astype(f32)
        for term in terms[1:]:
            total = total + term.astype(f32)
        return total.astype(bf)

    def exchanged(values, index, axis):
        keep = lax.dynamic_index_in_dim(values, index, 0, keepdims=False)
        give = lax.dynamic_index_in_dim(values, 1 - index, 0, keepdims=False)
        return added(keep, swapped(give, axis, 1))

    chip = exchanged(packed, core, "section")
    column = exchanged(chip, y, "dp")
    terms = [lax.dynamic_index_in_dim(column, z, 0, keepdims=False)]
    for by in range(1, half):
        terms.append(
            z_shift(lax.dynamic_index_in_dim(column, (z + by) % half, 0, keepdims=False), by)
        )
    mine = added(*terms)
    return added(mine, swapped(mine, "section", 2))


def split_last(values, widths):
    parts, at = [], 0
    for width in widths:
        parts.append(values[..., at:at + width])
        at += width
    return parts


def pack_rows(grad, half, unit):
    rows, width = grad.shape
    tiles = rows // (4 * half * unit)
    split = grad.reshape(half, 2, 2, tiles, unit, width)
    return split.transpose(2, 1, 0, 4, 3, 5).reshape(2, 2, half, unit, tiles * width)


def pack_columns(grad, half, unit):
    rows, width = grad.shape
    tiles = rows // (2 * half * unit)
    split = grad.reshape(half, 2, tiles, unit, 2, width // 2)
    return split.transpose(4, 1, 0, 3, 2, 5).reshape(2, 2, half, unit, tiles * (width // 2))


def open_rows(packed, width):
    half, _, _, unit, n = packed.shape
    split = packed.reshape(half, 2, 2, unit, n // width, width)
    return split.transpose(0, 1, 2, 4, 3, 5).reshape(-1, width)


def open_columns(packed, width):
    half, _, _, unit, n = packed.shape
    tiles = n // (width // 2)
    split = packed.reshape(half, 2, 2, unit, tiles, width // 2)
    return split.transpose(0, 1, 4, 3, 2, 5).reshape(-1, width)


def bucket_onehot(seq_count, bucket_count):
    position = jnp.arange(seq_count, dtype=jnp.int32)
    offset = position[None, :] - position[:, None]
    distance = jnp.abs(offset)
    far_bucket = jnp.full(distance.shape, 8, jnp.int32)
    for threshold in limits:
        far_bucket = far_bucket + (distance >= threshold).astype(jnp.int32)
    bucket = jnp.where(distance < 8, distance, jnp.minimum(far_bucket, 15)) + 16 * (
        offset > 0
    ).astype(jnp.int32)
    return (bucket[:, :, None] == jnp.arange(bucket_count, dtype=jnp.int32)[None, None, :]).astype(f32)


def body(inputs, cotangent, segments, observed, q_weight, k_weight, v_weight, o_weight,
         gate_weight, up_weight, down_weight, gains, position_table):
    section = lax.axis_index("section")
    core = section % 2
    chip = section // 2
    dp = lax.axis_index("dp")
    half = lax.axis_size("dp") // 2
    place = (dp // 2, dp % 2, core)
    micro_count, row_count, seq_count, width = inputs.shape
    layers = q_weight.shape[0]
    inner, wide = q_weight.shape[2], gate_weight.shape[2]
    unit = q_weight.shape[1] // 4
    heads = position_table.shape[1]
    tokens = row_count * seq_count

    attn_n, ffn_n = 8 * inner + 0, 6 * wide
    attn_widths = (2 * inner,) * 3 + (3 * (width // 2),)
    ffn_widths = (2 * wide, 2 * wide, 4 * width)

    weights = []
    previous = None
    for layer in range(layers):
        o_half = lax.dynamic_slice_in_dim(o_weight[layer], core * (width // 2), width // 2, 1)
        piece = jnp.concatenate(
            [fold_rows(half_rows(core, w[layer]), unit) for w in (q_weight, k_weight, v_weight)]
            + [fold_rows(o_half, unit)], axis=1)
        if previous is not None:
            piece = after(piece, previous)
        whole, previous = gather_part(piece, place)
        parts = split_last(whole, attn_widths)
        attn = tuple(open_rows(part, inner) for part in parts[:3]) + (open_columns(parts[3], width),)
        piece = jnp.concatenate(
            [fold_rows(half_rows(core, w[layer]), unit) for w in (gate_weight, up_weight, down_weight)],
            axis=1)
        piece = after(piece, previous)
        whole, previous = gather_part(piece, place)
        parts = split_last(whole, ffn_widths)
        ffn = (open_rows(parts[0], wide), open_rows(parts[1], wide), open_rows(parts[2], width))
        weights.append((attn, ffn))

    gains_all = lax.all_gather(gains, "dp", axis=2, tiled=True).astype(f32)

    x = lax.dynamic_index_in_dim(inputs, section, 0, keepdims=False).reshape(tokens, width)
    grad = lax.dynamic_index_in_dim(cotangent, section, 0, keepdims=False).reshape(tokens, width)
    seg = lax.dynamic_index_in_dim(segments, section, 0, keepdims=False)
    obs = lax.dynamic_index_in_dim(observed, section, 0, keepdims=False)
    allowed = (seg[:, :, None] == seg[:, None, :]) & (obs[:, :, None] == 1)
    mask = jnp.where(allowed, 0.0, masked).astype(f32)
    mask = jnp.concatenate([mask, mask], axis=2)
    onehot = bucket_onehot(seq_count, position_table.shape[0])
    bias = jnp.einsum("ijb,bh->jhi", onehot, position_table.astype(f32), precision=lax.Precision.HIGHEST)
    bias = bias.reshape(seq_count, heads * seq_count)

    states, kept = [x], []
    for layer in range(layers):
        attn, ffn = weights[layer]
        out, *saved = attn_fwd(states[-1], mask, bias, gains_all[layer, 0][None], *attn, block=512)
        states.append(out)
        kept.append(saved)
        out, *saved = ffn_fwd(states[-1], gains_all[layer, 1][None], *ffn, block=512)
        states.append(out)
        kept.append(saved)
    outs = states[1:]

    grads = [None] * 4
    reduced = [None] * 4
    gain_terms = [None] * 4
    bias_terms = []
    for layer in reversed(range(layers)):
        attn, ffn = weights[layer]
        s = 2 * layer + 1
        grad, dg, du, dd, gain_terms[s] = ffn_bwd(
            states[s], *kept[s], grad, gains_all[layer, 1][None], *ffn, block=512)
        grads[s] = grad
        packed = jnp.concatenate([pack_rows(t, half, unit) for t in (dg, du, dd)], axis=-1)
        reduced[s] = reduce_part(packed, place)
        s = 2 * layer
        grad, dq, dk, dv, do, gain_terms[s], bias_term = attn_bwd(
            states[s], *kept[s], grad, gains_all[layer, 0][None], *attn, block=512)
        grads[s] = grad
        bias_terms.append(bias_term)
        packed = jnp.concatenate(
            [pack_rows(t, half, unit) for t in (dq, dk, dv)] + [pack_columns(do, half, unit)], axis=-1)
        reduced[s] = reduce_part(packed, place)

    def across(value, s):
        pairs = [(0, 2), (1, 3)] if s >= 2 else [(2, 0), (3, 1)]
        return lax.ppermute(value, "section", pairs)

    def placed(values, received):
        own = lax.select_n(section, *values)
        far = lax.select_n(section, *received)
        swap = lambda arrays: lax.select_n(section, arrays[1], arrays[0], arrays[3], arrays[2])
        near = swapped(jnp.stack([swap(values), swap(received)]), "section", 1)
        pool = (own, near[0], far, near[1])
        full = jnp.stack([lax.select_n(section ^ m, *pool) for m in range(micro_count)])
        return full.reshape(1, micro_count, row_count, seq_count, width)

    section_outputs = placed(outs, [across(outs[s], s) for s in range(4)])
    section_grads = placed(grads, [across(grads[s], s) for s in range(4)])

    both = [jnp.stack([by_core(core, (r, p)), by_core(core, (p, r))])
            for r, p in ((r, swapped(r, "section", 1)) for r in reduced)]

    def rows_out(part, columns):
        split = part.reshape(2, unit, part.shape[2] // columns, columns)
        return split.transpose(0, 2, 1, 3).reshape(-1, columns).astype(f32)

    def columns_out(part, columns):
        tiles = part.shape[2] // (columns // 2)
        split = part.reshape(2, unit, tiles, columns // 2)
        return split.transpose(2, 1, 0, 3).reshape(-1, columns).astype(f32)

    attn_parts = [split_last(both[s], attn_widths) for s in (0, 2)]
    ffn_parts = [split_last(both[s], ffn_widths) for s in (1, 3)]
    q_grad, k_grad, v_grad = (jnp.stack([rows_out(p[i], inner) for p in attn_parts]) for i in range(3))
    o_grad = jnp.stack([columns_out(p[3], width) for p in attn_parts])
    gate_grad, up_grad = (jnp.stack([rows_out(p[i], wide) for p in ffn_parts]) for i in range(2))
    down_grad = jnp.stack([rows_out(p[2], width) for p in ffn_parts])

    bias_sum = (bias_terms[0] + bias_terms[1]).reshape(seq_count, heads, seq_count)
    table = jnp.einsum("ijb,jhi->bh", onehot, bias_sum, precision=lax.Precision.HIGHEST)
    gain_flat = jnp.concatenate([t.reshape(-1) for t in gain_terms])
    small = jnp.concatenate([gain_flat, table.reshape(-1)])
    pad = -small.shape[0] % 1024
    small = jnp.pad(small, (0, pad)).reshape(-1, 128)
    bit = 1
    while bit < lax.axis_size("dp"):
        small = small + swapped(small, "dp", bit)
        bit *= 2
    small = small + swapped(small, "section", 1)
    small = small + swapped(small, "section", 2)
    small = small.reshape(-1)
    shard = gains.shape[2]
    gains_grad = lax.dynamic_slice_in_dim(
        small[:gain_flat.shape[0]].reshape(layers, 2, width), dp * shard, shard, 2)
    table_grad = small[gain_flat.shape[0]:gain_flat.shape[0] + table.size].reshape(table.shape)
    return (section_outputs, section_grads, q_grad, k_grad, v_grad, o_grad, gate_grad, up_grad,
            down_grad, gains_grad, table_grad)


def solution(mesh):
    rows4 = P(None, "dp", None, None)
    rows3 = P(None, "dp", None)
    staged = P("section", None, "dp", None, None)
    return jax.shard_map(
        body,
        mesh=mesh,
        in_specs=(rows4, rows4) + (rows3,) * 9 + (P(None, None, "dp"), P()),
        out_specs=(staged, staged) + (rows3,) * 7 + (P(None, None, "dp"), P()),
        check_vma=False,
    )
```

```python
import jax
import jax.numpy as jnp
from jax import lax
from jax.experimental import pallas as pl
from jax.experimental.pallas import tpu as pltpu
from jax.sharding import PartitionSpec as P

eps_norm = 1e-06
limits = (12, 16, 23, 32, 46, 64, 91)
masked = -1e30
bf = jnp.bfloat16
f32 = jnp.float32
vmem_limit = 60 * 1024 * 1024


def dot_nn(a, b):
    return lax.dot_general(a, b, (((1,), (0,)), ((), ())), preferred_element_type=f32)


def dot_nt(a, b):
    return lax.dot_general(a, b, (((1,), (1,)), ((), ())), preferred_element_type=f32)


def dot_tn(a, b):
    return lax.dot_general(a, b, (((0,), (0,)), ((), ())), preferred_element_type=f32)


def row_scale(x):
    return lax.rsqrt(jnp.mean(x * x, axis=-1, keepdims=True) + eps_norm)


def pair_parts(values):
    lane = lax.broadcasted_iota(jnp.int32, values.shape, 1)
    zero = jnp.zeros_like(values)
    return jnp.concatenate(
        [jnp.where(lane < 64, values, zero), jnp.where(lane < 64, zero, values)], axis=0
    )


def pair_pick(values):
    half = values.shape[0] // 2
    lane = lax.broadcasted_iota(jnp.int32, (half, values.shape[1]), 1)
    return jnp.where(lane < 64, values[:half], values[half:])


blocks = 16
block_rows = 32


def order_of(ids, z, other_y, other_core):
    return (z * 2 + (ids[1] ^ other_y)) * 2 + (ids[2] ^ other_core)


def open_attn(ids, parts, wqkv, wo):
    for at, ref in enumerate(parts):
        other_y, other_core = at % 2, at // 2
        for z in range(4):
            place = order_of(ids, z, other_y, other_core)
            wqkv[pl.ds(pl.multiple_of(place * 32, 32), 32), :] = ref[z, :, :1152]
            shard = z * 2 + (ids[1] ^ other_y)
            core = ids[2] ^ other_core
            for i in range(3):
                rows = pl.ds(pl.multiple_of(shard * 48 + i * 16, 16), 16)
                for j in range(2):
                    columns = pl.ds(pl.multiple_of(core * 256 + j * 128, 128), 128)
                    wo[rows, columns] = ref[z, j * 16:j * 16 + 16, 1152 + i * 128:1280 + i * 128]


def open_ffn(ids, parts, wgu, wd):
    for at, ref in enumerate(parts):
        other_y, other_core = at % 2, at // 2
        for z in range(4):
            place = order_of(ids, z, other_y, other_core)
            wgu[pl.ds(pl.multiple_of(place * 32, 32), 32), :] = ref[z, :, :2048]
            for i in range(2):
                wd[pl.ds(pl.multiple_of(place * 64 + i * 32, 32), 32), :] = (
                    ref[z, :, 2048 + i * 512:2560 + i * 512])


def hand_out(ids, packed, keep_ref, give_ref):
    for other_core, ref in enumerate((keep_ref, give_ref)):
        for other_y in range(2):
            for by in range(4):
                place = order_of(ids, (ids[0] + by) & 3, other_y, other_core)
                ref[other_y, by] = packed[pl.ds(pl.multiple_of(place * 32, 32), 32), :]


def attn_fwd_kernel(ids, x_ref, mask_ref, bias_ref, gain_ref, w0, w1, w2, w3,
                    out_ref, q_ref, k_ref, v_ref, p_ref, att_ref, wqkv, wo):
    @pl.when(pl.program_id(0) == 0)
    def _():
        open_attn(ids, (w0, w1, w2, w3), wqkv, wo)

    x = x_ref[...].astype(f32)
    a = (x * row_scale(x) * gain_ref[...]).astype(bf)
    q = dot_nn(a, wqkv[:, :384]).astype(bf)
    k = dot_nn(a, wqkv[:, 384:768]).astype(bf)
    v = dot_nn(a, wqkv[:, 768:]).astype(bf)
    q_ref[...] = q
    k_ref[...] = k
    v_ref[...] = v
    rows = x.shape[0] // 64
    units = [(r, h) for r in range(rows) for h in range(3)]
    at = lambda arr, r, h: arr[r * 64:r * 64 + 64, h * 128:h * 128 + 128]
    scores = [dot_nt(at(k, r, h), pair_parts(at(q, r, h))) for r, h in units]
    probs = []
    for (r, h), s in zip(units, scores):
        s = s + (bias_ref[:, h * 128:h * 128 + 128] + mask_ref[r])
        e = jnp.exp(s - jnp.max(s, axis=0, keepdims=True))
        p = (e * (1.0 / jnp.sum(e, axis=0, keepdims=True))).astype(bf)
        p_ref[r * 64:r * 64 + 64, h * 128:h * 128 + 128] = p
        probs.append(p)
    full_att = [dot_tn(p, at(v, r, h)) for (r, h), p in zip(units, probs)]
    att = {unit: pair_pick(part).astype(bf) for unit, part in zip(units, full_att)}
    att = jnp.concatenate(
        [jnp.concatenate([att[r, h] for h in range(3)], axis=1) for r in range(rows)], axis=0)
    att_ref[...] = att
    out_ref[...] = (x + dot_nn(att, wo[...])).astype(bf)


def norm_back(x_ref, gain_ref, gx, g_low, a_ref, dgain):
    x = x_ref[...].astype(f32)
    scale = row_scale(x)
    n = x * scale
    a_ref[...] = (n * gain_ref[...]).astype(bf)
    dgain[...] += jnp.sum(gx * n, axis=0, keepdims=True)
    e = gx * gain_ref[...]
    dx = scale * (e - n * jnp.mean(e * n, axis=-1, keepdims=True))
    return (g_low.astype(f32) + dx).astype(bf)


def bucket_of(key, query):
    offset = key - query
    distance = jnp.abs(offset)
    far = jnp.full(distance.shape, 8, jnp.int32)
    for threshold in limits:
        far = far + (distance >= threshold).astype(jnp.int32)
    near = jnp.where(distance < 8, distance, jnp.minimum(far, 15))
    return near + 16 * (offset > 0).astype(jnp.int32)


def table_terms(bias_grad):
    key = lax.broadcasted_iota(jnp.int32, (64, 128), 0)
    query = lax.broadcasted_iota(jnp.int32, (64, 128), 1) & 63
    bucket = bucket_of(key, query)
    pieces = [bias_grad[:, h * 128:h * 128 + 128] for h in range(3)]
    sums = [[], [], []]
    for b in range(32):
        hit = bucket == b
        for h in range(3):
            sums[h].append(jnp.sum(jnp.where(hit, pieces[h], 0.0), axis=0, keepdims=True))
    lane = lax.broadcasted_iota(jnp.int32, (32, 128), 1)
    table = jnp.zeros((32, 128), f32)
    for h in range(3):
        part = jnp.concatenate(sums[h], axis=0)
        low = jnp.sum(jnp.where(lane < 64, part, 0.0), axis=1, keepdims=True)
        high = jnp.sum(jnp.where(lane < 64, 0.0, part), axis=1, keepdims=True)
        table = jnp.where(lane == 2 * h, low, jnp.where(lane == 2 * h + 1, high, table))
    return table


def attn_bwd_kernel(ids, x_ref, q_ref, k_ref, v_ref, p_ref, att_ref, g_ref, gain_ref, w0, w1, w2, w3,
                    gains_in, bias_in, gin_ref, keep_ref, give_ref, dgain_ref, dbias_ref,
                    wqkv, wo, a_s, dqkv_s, att_s, g_s, dgain_s, dbias_s, packed):
    step = pl.program_id(0)
    last = pl.num_programs(0) - 1
    block = x_ref.shape[0]
    with_small = keep_ref.shape[3] > 1536

    @pl.when(step == 0)
    def _():
        open_attn(ids, (w0, w1, w2, w3), wqkv, wo)
        dgain_s[...] = jnp.zeros_like(dgain_s)
        dbias_s[...] = bias_in[...]

    here = pl.ds(pl.multiple_of(step * block, block), block)
    g_low = g_ref[...]
    da = dot_nt(g_low, wo[...]).astype(bf)
    att_s[here, :] = att_ref[...]
    g_s[here, :] = g_low
    rows = block // 64
    units = [(r, h) for r in range(rows) for h in range(3)]
    at = lambda arr, r, h: arr[r * 64:r * 64 + 64, h * 128:h * 128 + 128]
    db = [None] * 3
    da_bds = [pair_parts(at(da, r, h)) for r, h in units]
    dps = [dot_nt(at(v_ref, r, h), da_bd) for (r, h), da_bd in zip(units, da_bds)]
    dv_u = {(r, h): dot_nn(at(p_ref, r, h), da_bd).astype(bf) for (r, h), da_bd in zip(units, da_bds)}
    dss = []
    for (r, h), dp in zip(units, dps):
        pf = at(p_ref, r, h).astype(f32)
        ds = pf * (dp - jnp.sum(pf * dp, axis=0, keepdims=True))
        db[h] = ds if db[h] is None else db[h] + ds
        dss.append(ds.astype(bf))
    dk_u = {(r, h): dot_nn(ds, pair_parts(at(q_ref, r, h))).astype(bf) for (r, h), ds in zip(units, dss)}
    full_dq = [dot_tn(ds, at(k_ref, r, h)) for (r, h), ds in zip(units, dss)]
    dq_u = {unit: pair_pick(part).astype(bf) for unit, part in zip(units, full_dq)}
    dqkv = jnp.concatenate(
        [jnp.concatenate([u[r, h] for u in (dq_u, dk_u, dv_u) for h in range(3)], axis=1)
         for r in range(rows)], axis=0)
    dqkv_s[here, :] = dqkv
    for h in range(3):
        dbias_s[:, h * 128:h * 128 + 128] += db[h]
    gx = dot_nt(dqkv, wqkv[...])
    gin_ref[...] = norm_back(x_ref, gain_ref, gx, g_low, a_s.at[here, :], dgain_s)

    @pl.when(step == last)
    def _():
        for h in range(3):
            columns = slice(h * 384, h * 384 + 384)
            packed[:, columns] = dot_tn(a_s[...], dqkv_s[:, columns]).astype(bf)
        dwo = dot_tn(att_s[...], g_s[...]).astype(bf)
        for shard in range(8):
            for core in range(2):
                for i in range(3):
                    for j in range(2):
                        packed[(shard * 2 + core) * 32 + j * 16:(shard * 2 + core) * 32 + j * 16 + 16,
                               1152 + i * 128:1280 + i * 128] = (
                            dwo[shard * 48 + i * 16:shard * 48 + i * 16 + 16,
                                core * 256 + j * 128:core * 256 + j * 128 + 128])
        dgain_ref[...] = dgain_s[...]
        dbias_ref[...] = dbias_s[...]
        if with_small:
            table = table_terms(dbias_s[...]).astype(bf)
            terms = jnp.concatenate([dgain_s[...], gains_in[...]], axis=0)
            row = lax.broadcasted_iota(jnp.int32, (32, 128), 0)
            for shard in range(8):
                spot = slice(shard * 64, shard * 64 + 64)
                first = jnp.concatenate([terms[0:1, spot], terms[1:2, spot]], axis=1)
                second = jnp.concatenate([terms[2:3, spot], terms[3:4, spot]], axis=1)
                small = jnp.where(row == 0, first, jnp.where(row == 1, second, 0.0)).astype(bf)
                packed[shard * 64:shard * 64 + 32, 1536:1664] = small
                packed[shard * 64 + 32:shard * 64 + 64, 1536:1664] = table
        hand_out(ids, packed, keep_ref, give_ref)


def gelu_parts(u):
    c = 0.7978845608028654
    u2 = u * u
    t = jnp.tanh(u * (c + (c * 0.044715) * u2))
    half = 0.5 + 0.5 * t
    act = u * half
    slope = half + (0.5 * u) * (1.0 - t * t) * (c + (3.0 * c * 0.044715) * u2)
    return act, slope


def gelu(u):
    c = 0.7978845608028654
    t = jnp.tanh(u * (c + (c * 0.044715) * (u * u)))
    return u * (0.5 + 0.5 * t)


def ffn_fwd_kernel(ids, x_ref, gain_ref, w0, w1, w2, w3, out_ref, gate_ref, up_ref, wgu, wd):
    @pl.when(pl.program_id(0) == 0)
    def _():
        open_ffn(ids, (w0, w1, w2, w3), wgu, wd)

    x = x_ref[...].astype(f32)
    a = (x * row_scale(x) * gain_ref[...]).astype(bf)
    gate = dot_nn(a, wgu[:, :1024])
    up = dot_nn(a, wgu[:, 1024:])
    gate_ref[...] = gate.astype(bf)
    up_ref[...] = up.astype(bf)
    hidden = (gelu(gate) * up).astype(bf)
    out_ref[...] = (x + dot_nn(hidden, wd[...])).astype(bf)


def ffn_bwd_kernel(ids, x_ref, gate_ref, up_ref, g_ref, gain_ref, w0, w1, w2, w3,
                   gin_ref, keep_ref, give_ref, dgain_ref,
                   wgu, wd, a_s, gub_s, hid_s, g_s, dgain_s, packed):
    step = pl.program_id(0)
    last = pl.num_programs(0) - 1
    block = x_ref.shape[0]

    @pl.when(step == 0)
    def _():
        open_ffn(ids, (w0, w1, w2, w3), wgu, wd)
        dgain_s[...] = jnp.zeros_like(dgain_s)

    here = pl.ds(pl.multiple_of(step * block, block), block)
    g_low = g_ref[...]
    g_s[here, :] = g_low
    hg = dot_nt(g_low, wd[...])
    gate = gate_ref[...].astype(f32)
    up = up_ref[...].astype(f32)
    act, slope = gelu_parts(gate)
    hid_s[here, :] = (act * up).astype(bf)
    gb = (hg * up * slope).astype(bf)
    ub = (hg * act).astype(bf)
    gub_s[here, :1024] = gb
    gub_s[here, 1024:] = ub
    gx = dot_nt(gb, wgu[:, :1024]) + dot_nt(ub, wgu[:, 1024:])
    gin_ref[...] = norm_back(x_ref, gain_ref, gx, g_low, a_s.at[here, :], dgain_s)

    @pl.when(step == last)
    def _():
        for h in range(4):
            columns = slice(h * 512, h * 512 + 512)
            packed[:, columns] = dot_tn(a_s[...], gub_s[:, columns]).astype(bf)
        for h in range(2):
            dwd = dot_tn(hid_s[:, h * 512:h * 512 + 512], g_s[...]).astype(bf)
            for at in range(8):
                for i in range(2):
                    packed[(h * 8 + at) * 32:(h * 8 + at) * 32 + 32, 2048 + i * 512:2560 + i * 512] = (
                        dwd[at * 64 + i * 32:at * 64 + i * 32 + 32])
        dgain_ref[...] = dgain_s[...]
        hand_out(ids, packed, keep_ref, give_ref)


def tok(block, width):
    return pl.BlockSpec((block, width), lambda i, ids: (i, 0))


def full(shape):
    zero = (0,) * len(shape)
    return pl.BlockSpec(shape, lambda i, ids: zero)


def sds(shape, dtype):
    return jax.ShapeDtypeStruct(shape, dtype)


def call(kernel, grid, in_specs, out_specs, out_shape, scratch, micros, name):
    return pl.pallas_call(
        kernel,
        grid_spec=pltpu.PrefetchScalarGridSpec(
            num_scalar_prefetch=1, grid=(grid,), in_specs=in_specs, out_specs=out_specs,
            scratch_shapes=scratch),
        out_shape=out_shape, name=name,
        compiler_params=pltpu.CompilerParams(vmem_limit_bytes=vmem_limit),
        cost_estimate=pl.CostEstimate(flops=int(micros * 1.1e9), bytes_accessed=0, transcendentals=0),
    )


token_block = 512


def attn_fwd(ids, x, mask, bias, gain, parts):
    t, d = x.shape
    block = token_block
    return call(
        attn_fwd_kernel, t // block,
        [tok(block, d), pl.BlockSpec((block // 64, 64, 128), lambda i, ids: (i, 0, 0)), full(bias.shape),
         full((1, d))] + [full(parts[0].shape)] * 4,
        [tok(block, d)] + [tok(block, 384)] * 5,
        [sds((t, d), bf)] + [sds((t, 384), bf)] * 5,
        [pltpu.VMEM((512, 1152), bf), pltpu.VMEM((384, 512), bf)],
        7, "attn_fwd")(ids, x, mask, bias, gain, *parts)


def attn_bwd(ids, x, q, k, v, p, att, g, gain, parts, gains_in, bias_in, with_small):
    t, d = x.shape
    block = token_block
    n = 1664 if with_small else 1536
    packed = (2, 4, 32, n)
    return call(
        attn_bwd_kernel, t // block,
        [tok(block, d)] + [tok(block, 384)] * 5 + [tok(block, d), full((1, d))]
        + [full(parts[0].shape)] * 4 + [full(gains_in.shape), full(bias_in.shape)],
        [tok(block, d), full(packed), full(packed), full((1, d)), full((64, 384))],
        [sds((t, d), bf), sds(packed, bf), sds(packed, bf), sds((1, d), f32), sds((64, 384), f32)],
        [pltpu.VMEM((512, 1152), bf), pltpu.VMEM((384, 512), bf), pltpu.VMEM((t, d), bf),
         pltpu.VMEM((t, 1152), bf), pltpu.VMEM((t, 384), bf), pltpu.VMEM((t, d), bf),
         pltpu.VMEM((1, d), f32), pltpu.VMEM((64, 384), f32), pltpu.VMEM((512, n), bf)],
        12, "attn_bwd")(ids, x, q, k, v, p, att, g, gain, *parts, gains_in, bias_in)


def ffn_fwd(ids, x, gain, parts):
    t, d = x.shape
    block = token_block
    return call(
        ffn_fwd_kernel, t // block,
        [tok(block, d), full((1, d))] + [full(parts[0].shape)] * 4,
        [tok(block, d), tok(block, 1024), tok(block, 1024)],
        [sds((t, d), bf), sds((t, 1024), bf), sds((t, 1024), bf)],
        [pltpu.VMEM((512, 2048), bf), pltpu.VMEM((1024, 512), bf)],
        7, "ffn_fwd")(ids, x, gain, *parts)


def ffn_bwd(ids, x, gate, up, g, gain, parts):
    t, d = x.shape
    block = token_block
    packed = (2, 4, 32, 3072)
    return call(
        ffn_bwd_kernel, t // block,
        [tok(block, d), tok(block, 1024), tok(block, 1024), tok(block, d), full((1, d))]
        + [full(parts[0].shape)] * 4,
        [tok(block, d), full(packed), full(packed), full((1, d))],
        [sds((t, d), bf), sds(packed, bf), sds(packed, bf), sds((1, d), f32)],
        [pltpu.VMEM((512, 2048), bf), pltpu.VMEM((1024, 512), bf), pltpu.VMEM((t, d), bf),
         pltpu.VMEM((t, 2048), bf), pltpu.VMEM((t, 1024), bf), pltpu.VMEM((t, d), bf),
         pltpu.VMEM((1, d), f32), pltpu.VMEM((512, 3072), bf)],
        15, "ffn_bwd")(ids, x, gate, up, g, gain, *parts)


def pack_kernel(ids, q, k, v, o, gate, up, down, a0, f0, a1, f1):
    core = ids[2]
    rows = pl.ds(pl.multiple_of(core * 32, 32), 32)
    for layer, a_ref, f_ref in ((0, a0, f0), (1, a1, f1)):
        for at, w in enumerate((q, k, v)):
            a_ref[:, at * 384:at * 384 + 384] = w[layer, rows, :]
        for i in range(3):
            for j in range(2):
                columns = pl.ds(pl.multiple_of(core * 256 + j * 128, 128), 128)
                a_ref[j * 16:j * 16 + 16, 1152 + i * 128:1280 + i * 128] = (
                    o[layer, i * 16:i * 16 + 16, columns])
        f_ref[:, :1024] = gate[layer, rows, :]
        f_ref[:, 1024:2048] = up[layer, rows, :]
        for i in range(2):
            f_ref[:, 2048 + i * 512:2560 + i * 512] = (
                down[layer, pl.ds(pl.multiple_of(core * 64 + i * 32, 32), 32), :])


def pack_weights(ids, *weights):
    return call(
        pack_kernel, 1, [full(w.shape) for w in weights],
        [full((32, 1536)), full((32, 3072))] * 2,
        [sds((32, 1536), bf), sds((32, 3072), bf)] * 2, [], 2, "pack_weights")(ids, *weights)


def unpack_kernel(ids, *refs):
    sums, outs = refs[:16], refs[16:]
    q, k, v, o, gate, up, down, gains, table = outs
    first = ids[2] == 0
    for s in range(4):
        own, near, far, cross = (ref[...].astype(f32) for ref in sums[s * 4:s * 4 + 4])
        mine, peer = own + far, near + cross
        halves = (jnp.where(first, mine, peer), jnp.where(first, peer, mine))
        layer = s // 2
        for core in range(2):
            part = halves[core]
            rows = slice(core * 32, core * 32 + 32)
            if s % 2 == 0:
                for at, w in enumerate((q, k, v)):
                    w[layer, rows, :] = part[:, at * 384:at * 384 + 384]
                for i in range(3):
                    for j in range(2):
                        o[layer, i * 16:i * 16 + 16, core * 256 + j * 128:core * 256 + j * 128 + 128] = (
                            part[j * 16:j * 16 + 16, 1152 + i * 128:1280 + i * 128])
            else:
                gate[layer, rows, :] = part[:, :1024]
                up[layer, rows, :] = part[:, 1024:2048]
                for i in range(2):
                    down[layer, core * 64 + i * 32:core * 64 + i * 32 + 32, :] = (
                        part[:, 2048 + i * 512:2560 + i * 512])
        if s == 0:
            for l in range(2):
                for n in range(2):
                    gains[l, n:n + 1, :] = halves[0][l:l + 1, 1536 + n * 64:1600 + n * 64]
            table[...] = halves[1][:, 1536:1542]


def unpack_grads(ids, sums, shapes):
    flat = [array for part in sums for array in part]
    return call(
        unpack_kernel, 1, [full(array.shape) for array in flat], [full(shape) for shape in shapes],
        [sds(shape, f32) for shape in shapes], [], 3, "unpack_grads")(ids, *flat)


def place_kernel(ids, own0, own1, own2, own3, near, far, cross, out, sems):
    section = ids[3]
    def copy(ref, slot, sem):
        return pltpu.make_async_copy(ref, out.at[slot], sems.at[sem])
    for at, ref in enumerate((own0, own1, own2, own3)):
        @pl.when(section == at)
        def _(ref=ref):
            copy(ref, section, 0).start()
    copy(near, section ^ 1, 1).start()
    copy(far, section ^ 2, 2).start()
    copy(cross, section ^ 3, 3).start()
    copy(near, section, 0).wait()
    copy(near, section ^ 1, 1).wait()
    copy(far, section ^ 2, 2).wait()
    copy(cross, section ^ 3, 3).wait()


def place(ids, own, others):
    t, d = own[0].shape
    anywhere = pl.BlockSpec(memory_space=pl.ANY)
    return pl.pallas_call(
        place_kernel,
        grid_spec=pltpu.PrefetchScalarGridSpec(
            num_scalar_prefetch=1, grid=(1,), in_specs=[anywhere] * 7, out_specs=anywhere,
            scratch_shapes=[pltpu.SemaphoreType.DMA((4,))]),
        out_shape=sds((4, t, d), bf), name="place",
        cost_estimate=pl.CostEstimate(flops=3_000_000_000, bytes_accessed=0, transcendentals=0),
    )(ids, *own, *others)


def z_shift(values, by):
    half = lax.axis_size("dp") // 2
    pairs = [(z * 2 + y, ((z + by) % half) * 2 + y) for z in range(half) for y in range(2)]
    return lax.ppermute(values, "dp", pairs)


def swapped(values, axis, bit):
    return lax.ppermute(values, axis, [(i, i ^ bit) for i in range(lax.axis_size(axis))])


def after(values, *others):
    return lax.optimization_barrier((values,) + others)[0]


def added(*terms):
    total = terms[0].astype(f32)
    for term in terms[1:]:
        total = total + term.astype(f32)
    return total.astype(bf)


def gather_part(piece, place_ids):
    z = place_ids[0]
    got = [piece] + [z_shift(piece, by) for by in range(1, 4)]
    column = jnp.stack([lax.select_n((z - at) % 4, *got) for at in range(4)])
    other = swapped(column, "dp", 1)
    return (column, other, swapped(column, "section", 1), swapped(other, "section", 1)), got[-1]


def reduce_part(keep, give):
    got = swapped(give, "section", 1)
    sent = swapped(added(keep[1], got[1]), "dp", 1)
    terms = [added(keep[0, by], got[0, by], sent[by]) for by in range(4)]
    mine = added(terms[0], *[z_shift(terms[by], by) for by in range(1, 4)])
    return (mine,) + tuple(swapped(mine, "section", bit) for bit in (1, 2, 3)), (got, sent)


def to_packed(q, k, v, o, gate, up, down):
    o_part = o.reshape(8, 3, 16, 2, 2, 128).transpose(0, 3, 4, 2, 1, 5).reshape(512, 384)
    d_part = down.reshape(16, 2, 32, 512).transpose(0, 2, 1, 3).reshape(512, 1024)
    return jnp.concatenate([q, k, v, o_part], axis=1), jnp.concatenate([gate, up, d_part], axis=1)


def from_packed(attn, ffn):
    q, k, v = (attn[:, at * 384:at * 384 + 384] for at in range(3))
    o = attn[:, 1152:1536].reshape(8, 2, 2, 16, 3, 128).transpose(0, 4, 3, 1, 2, 5).reshape(384, 512)
    down = ffn[:, 2048:].reshape(16, 32, 2, 512).transpose(0, 2, 1, 3).reshape(1024, 512)
    return q, k, v, o, ffn[:, :1024], ffn[:, 1024:2048], down


def parts_of(whole):
    split = whole.reshape(4, 2, 2, 32, whole.shape[1])
    return tuple(split[:, y, core] for core in range(2) for y in range(2))


def whole_of(keep, give):
    split = jnp.stack([keep, give]).transpose(2, 1, 0, 3, 4)
    return split.reshape(512, keep.shape[3])


def gather_small(gains):
    z = lax.axis_index("dp") // 2
    y = lax.axis_index("dp") % 2
    got = [gains] + [z_shift(gains, by) for by in range(1, 4)]
    column = jnp.stack([lax.select_n((z - at) % 4, *got) for at in range(4)])
    other = swapped(column, "dp", 1)
    pair = jnp.stack([jnp.where(y == 0, column, other), jnp.where(y == 0, other, column)], axis=1)
    return pair.transpose(2, 3, 0, 1, 4).reshape(gains.shape[0], gains.shape[1], -1).astype(f32)


def body(inputs, cotangent, segments, observed, q_weight, k_weight, v_weight, o_weight,
         gate_weight, up_weight, down_weight, gains, position_table):
    section = lax.axis_index("section")
    dp = lax.axis_index("dp")
    micro_count, row_count, seq_count, width = inputs.shape
    layers = q_weight.shape[0]
    heads = position_table.shape[1]
    tokens = row_count * seq_count
    shards = (q_weight, k_weight, v_weight, o_weight, gate_weight, up_weight, down_weight)
    eight = lax.axis_size("dp") == 8
    own_ids = jnp.stack([dp // 2, dp % 2, section % 2, section]).astype(jnp.int32)
    ids = own_ids if eight else jnp.stack([0 * dp, 0 * dp, 0 * dp, section]).astype(jnp.int32)

    weights = []
    if eight:
        pieces = pack_weights(own_ids, *shards)
        previous = None
        for piece in pieces:
            if previous is not None:
                piece = after(piece, previous)
            parts, previous = gather_part(piece, (dp // 2,))
            weights.append(parts)
        gains_all = gather_small(gains)
    else:
        whole = [lax.all_gather(w, "dp", axis=1, tiled=True) for w in shards]
        for layer in range(layers):
            weights.extend(parts_of(w) for w in to_packed(*(w[layer] for w in whole)))
        gains_all = lax.all_gather(gains, "dp", axis=2, tiled=True).astype(f32)

    x = lax.dynamic_index_in_dim(inputs, section, 0, keepdims=False).reshape(tokens, width)
    grad = lax.dynamic_index_in_dim(cotangent, section, 0, keepdims=False).reshape(tokens, width)
    seg = lax.dynamic_index_in_dim(segments, section, 0, keepdims=False)
    obs = lax.dynamic_index_in_dim(observed, section, 0, keepdims=False)
    allowed = (seg[:, :, None] == seg[:, None, :]) & (obs[:, :, None] == 1)
    mask = jnp.where(allowed, 0.0, masked).astype(f32)
    mask = jnp.concatenate([mask, mask], axis=2)
    position = jnp.arange(seq_count, dtype=jnp.int32)
    bucket = bucket_of(position[:, None], position[None, :])
    onehot = (bucket[:, :, None] == jnp.arange(position_table.shape[0])[None, None, :]).astype(f32)
    bias = jnp.einsum("jib,bh->jhi", onehot, position_table.astype(f32), precision=lax.Precision.HIGHEST)
    bias = bias.reshape(seq_count, heads * seq_count)

    states, kept = [x], []
    for s in range(4):
        gain = gains_all[s // 2, s % 2][None]
        if s % 2 == 0:
            out, *saved = attn_fwd(ids, states[-1], mask, bias, gain, weights[s])
        else:
            out, *saved = ffn_fwd(ids, states[-1], gain, weights[s])
        states.append(out)
        kept.append(saved)
    outs = states[1:]

    grads, reduced, gain_terms = [None] * 4, [None] * 4, [None] * 4
    packed, steps = [None] * 4, [None] * 4
    bias_sum = jnp.zeros((seq_count, heads * seq_count), f32)
    for s in (3, 2, 1, 0):
        gain = gains_all[s // 2, s % 2][None]
        if eight and s == 1:
            grad = after(grad, steps[3][0])
        if eight and s == 0:
            grad = after(grad, steps[3][1], steps[2][0])
        if s % 2 == 1:
            grad, keep, give, gain_terms[s] = ffn_bwd(
                ids, states[s], *kept[s], grad, gain, weights[s])
        else:
            earlier = jnp.concatenate(gain_terms[1:]) if s == 0 else jnp.zeros((3, width), f32)
            grad, keep, give, gain_terms[s], bias_sum = attn_bwd(
                ids, states[s], *kept[s], grad, gain, weights[s], earlier, bias_sum, eight and s == 0)
        grads[s] = grad
        if eight:
            reduced[s], steps[s] = reduce_part(keep, give)
        else:
            packed[s] = whole_of(keep, give)

    def sent(values, s):
        return [lax.ppermute(values[s], "section", [(s ^ bit, s)]) for bit in (1, 2, 3)]

    def placed(values):
        arrived = [sent(values, s) for s in range(4)]
        others = [lax.select_n(section, *[arrived[s][at] for s in range(4)]) for at in range(3)]
        full_set = place(ids, values, others)
        return full_set.reshape(1, micro_count, row_count, seq_count, width)

    section_outputs = placed(outs)
    section_grads = placed(grads)

    if eight:
        shapes = [w.shape for w in shards] + [gains.shape, position_table.shape]
        final = unpack_grads(ids, reduced, shapes)
        return (section_outputs, section_grads) + tuple(final)

    dense = [from_packed(packed[2 * layer], packed[2 * layer + 1]) for layer in range(layers)]
    final = []
    for at in range(7):
        both = jnp.stack([d[at] for d in dense])
        part = lax.psum_scatter(both, "dp", scatter_dimension=1, tiled=True)
        final.append(lax.psum(part, "section").astype(f32))
    bias_sum = bias_sum.reshape(seq_count, heads, seq_count)
    table = jnp.einsum("jib,jhi->bh", onehot, bias_sum, precision=lax.Precision.HIGHEST)
    gain_sum = jnp.concatenate(gain_terms).reshape(layers, 2, width)
    table, gain_sum = lax.psum((table, gain_sum), ("section", "dp"))
    shard = gains.shape[2]
    gain_sum = lax.dynamic_slice_in_dim(gain_sum, dp * shard, shard, 2)
    return (section_outputs, section_grads) + tuple(final) + (gain_sum, table)


def solution(mesh):
    rows4 = P(None, "dp", None, None)
    rows3 = P(None, "dp", None)
    staged = P("section", None, "dp", None, None)
    return jax.shard_map(
        body,
        mesh=mesh,
        in_specs=(rows4, rows4) + (rows3,) * 9 + (P(None, None, "dp"), P()),
        out_specs=(staged, staged) + (rows3,) * 7 + (P(None, None, "dp"), P()),
        check_vma=False,
    )
```

```python
import jax
import jax.numpy as jnp
from jax import lax
from jax.experimental import pallas as pl
from jax.experimental.pallas import tpu as pltpu
from jax.sharding import PartitionSpec as P

eps_norm = 1e-06
limits = (12, 16, 23, 32, 46, 64, 91)
masked = -1e30
bf = jnp.bfloat16
f32 = jnp.float32
vmem_limit = 60 * 1024 * 1024


def dot_nn(a, b):
    return lax.dot_general(a, b, (((1,), (0,)), ((), ())), preferred_element_type=f32)


def dot_nt(a, b):
    return lax.dot_general(a, b, (((1,), (1,)), ((), ())), preferred_element_type=f32)


def dot_tn(a, b):
    return lax.dot_general(a, b, (((0,), (0,)), ((), ())), preferred_element_type=f32)


def row_scale(x):
    return lax.rsqrt(jnp.mean(x * x, axis=-1, keepdims=True) + eps_norm)


def pair_parts(values):
    lane = lax.broadcasted_iota(jnp.int32, values.shape, 1)
    zero = jnp.zeros_like(values)
    return jnp.concatenate(
        [jnp.where(lane < 64, values, zero), jnp.where(lane < 64, zero, values)], axis=0
    )


def pair_pick(values):
    half = values.shape[0] // 2
    lane = lax.broadcasted_iota(jnp.int32, (half, values.shape[1]), 1)
    return jnp.where(lane < 64, values[:half], values[half:])


blocks = 16
block_rows = 32


def order_of(ids, z, other_y, other_core):
    return (z * 2 + (ids[1] ^ other_y)) * 2 + (ids[2] ^ other_core)


def open_attn(ids, parts, wqkv, wo):
    for at, ref in enumerate(parts):
        other_y, other_core = at % 2, at // 2
        for z in range(4):
            place = order_of(ids, z, other_y, other_core)
            if wqkv is not None:
                wqkv[pl.ds(pl.multiple_of(place * 32, 32), 32), :] = ref[z, :, :1152]
            shard = z * 2 + (ids[1] ^ other_y)
            core = ids[2] ^ other_core
            for i in range(3):
                rows = pl.ds(pl.multiple_of(shard * 48 + i * 16, 16), 16)
                for j in range(2):
                    columns = pl.ds(pl.multiple_of(core * 256 + j * 128, 128), 128)
                    wo[rows, columns] = ref[z, j * 16:j * 16 + 16, 1152 + i * 128:1280 + i * 128]


def open_ffn(ids, parts, wgu, wd):
    for at, ref in enumerate(parts):
        other_y, other_core = at % 2, at // 2
        for z in range(4):
            place = order_of(ids, z, other_y, other_core)
            if wgu is not None:
                wgu[pl.ds(pl.multiple_of(place * 32, 32), 32), :] = ref[z, :, :2048]
            for i in range(2):
                wd[pl.ds(pl.multiple_of(place * 64 + i * 32, 32), 32), :] = (
                    ref[z, :, 2048 + i * 512:2560 + i * 512])


def hand_out(ids, packed, keep_ref, give_ref):
    for other_core, ref in enumerate((keep_ref, give_ref)):
        for other_y in range(2):
            for by in range(4):
                place = order_of(ids, ids[0] ^ by, other_y, other_core)
                ref[other_y, by] = packed[pl.ds(pl.multiple_of(place * 32, 32), 32), :]


def attn_fwd_kernel(ids, x_ref, mask_ref, bias_ref, gain_ref, w0, w1, w2, w3,
                    out_ref, q_ref, k_ref, v_ref, p_ref, att_ref, wqkv, wo):
    @pl.when(pl.program_id(0) == 0)
    def _():
        open_attn(ids, (w0, w1, w2, w3), wqkv, wo)

    x = x_ref[...].astype(f32)
    a = (x * row_scale(x) * gain_ref[...]).astype(bf)
    q = dot_nn(a, wqkv[:, :384]).astype(bf)
    k = dot_nn(a, wqkv[:, 384:768]).astype(bf)
    v = dot_nn(a, wqkv[:, 768:]).astype(bf)
    q_ref[...] = q
    k_ref[...] = k
    v_ref[...] = v
    rows = x.shape[0] // 64
    units = [(r, h) for r in range(rows) for h in range(3)]
    at = lambda arr, r, h: arr[r * 64:r * 64 + 64, h * 128:h * 128 + 128]
    scores = [dot_nt(at(k, r, h), pair_parts(at(q, r, h))) for r, h in units]
    probs = []
    for (r, h), s in zip(units, scores):
        s = s + (bias_ref[:, h * 128:h * 128 + 128] + mask_ref[r])
        e = jnp.exp(s - jnp.max(s, axis=0, keepdims=True))
        p = (e * (1.0 / jnp.sum(e, axis=0, keepdims=True))).astype(bf)
        p_ref[r * 64:r * 64 + 64, h * 128:h * 128 + 128] = p
        probs.append(p)
    full_att = [dot_tn(p, at(v, r, h)) for (r, h), p in zip(units, probs)]
    att = {unit: pair_pick(part).astype(bf) for unit, part in zip(units, full_att)}
    att = jnp.concatenate(
        [jnp.concatenate([att[r, h] for h in range(3)], axis=1) for r in range(rows)], axis=0)
    att_ref[...] = att
    out_ref[...] = (x + dot_nn(att, wo[...])).astype(bf)


def normed(x_ref, gain_ref):
    x = x_ref[...].astype(f32)
    return (x * row_scale(x) * gain_ref[...]).astype(bf)


def input_grad_kernel(ids, x_ref, back_ref, g_ref, gain_ref, w0, w1, w2, w3, gin_ref, w_s):
    width = back_ref.shape[1]

    @pl.when(pl.program_id(0) == 0)
    def _():
        for at, ref in enumerate((w0, w1, w2, w3)):
            for z in range(4):
                place = order_of(ids, z, at % 2, at // 2)
                w_s[pl.ds(pl.multiple_of(place * 32, 32), 32), :] = ref[z, :, :width]

    gx = dot_nt(back_ref[...], w_s[...])
    x = x_ref[...].astype(f32)
    scale = row_scale(x)
    n = x * scale
    e = gx * gain_ref[...]
    dx = scale * (e - n * jnp.mean(e * n, axis=-1, keepdims=True))
    gin_ref[...] = (g_ref[...].astype(f32) + dx).astype(bf)


def bucket_of(key, query):
    offset = key - query
    distance = jnp.abs(offset)
    far = jnp.full(distance.shape, 8, jnp.int32)
    for threshold in limits:
        far = far + (distance >= threshold).astype(jnp.int32)
    near = jnp.where(distance < 8, distance, jnp.minimum(far, 15))
    return near + 16 * (offset > 0).astype(jnp.int32)


def table_terms(bias_grad):
    key = lax.broadcasted_iota(jnp.int32, (64, 128), 0)
    query = lax.broadcasted_iota(jnp.int32, (64, 128), 1) & 63
    bucket = bucket_of(key, query)
    pieces = [bias_grad[:, h * 128:h * 128 + 128] for h in range(3)]
    sums = [[], [], []]
    for b in range(32):
        hit = bucket == b
        for h in range(3):
            sums[h].append(jnp.sum(jnp.where(hit, pieces[h], 0.0), axis=0, keepdims=True))
    lane = lax.broadcasted_iota(jnp.int32, (32, 128), 1)
    table = jnp.zeros((32, 128), f32)
    for h in range(3):
        part = jnp.concatenate(sums[h], axis=0)
        low = jnp.sum(jnp.where(lane < 64, part, 0.0), axis=1, keepdims=True)
        high = jnp.sum(jnp.where(lane < 64, 0.0, part), axis=1, keepdims=True)
        table = jnp.where(lane == 2 * h, low, jnp.where(lane == 2 * h + 1, high, table))
    return table


def attn_bwd_kernel(ids, x_ref, q_ref, k_ref, v_ref, p_ref, att_ref, g_ref, gain_ref, w0, w1, w2, w3,
                    bias_in, back_ref, keep_ref, give_ref, dbias_ref,
                    wo, a_s, dqkv_s, att_s, g_s, dbias_s, packed):
    step = pl.program_id(0)
    last = pl.num_programs(0) - 1
    block = x_ref.shape[0]
    with_table = keep_ref.shape[3] > 1536

    @pl.when(step == 0)
    def _():
        open_attn(ids, (w0, w1, w2, w3), None, wo)
        dbias_s[...] = bias_in[...]

    here = pl.ds(pl.multiple_of(step * block, block), block)
    g_low = g_ref[...]
    da = dot_nt(g_low, wo[...]).astype(bf)
    att_s[here, :] = att_ref[...]
    g_s[here, :] = g_low
    a_s[here, :] = normed(x_ref, gain_ref)
    rows = block // 64
    units = [(r, h) for r in range(rows) for h in range(3)]
    at = lambda arr, r, h: arr[r * 64:r * 64 + 64, h * 128:h * 128 + 128]
    db = [None] * 3
    da_bds = [pair_parts(at(da, r, h)) for r, h in units]
    dps = [dot_nt(at(v_ref, r, h), da_bd) for (r, h), da_bd in zip(units, da_bds)]
    dv_u = {(r, h): dot_nn(at(p_ref, r, h), da_bd).astype(bf) for (r, h), da_bd in zip(units, da_bds)}
    dss = []
    for (r, h), dp in zip(units, dps):
        pf = at(p_ref, r, h).astype(f32)
        ds = pf * (dp - jnp.sum(pf * dp, axis=0, keepdims=True))
        db[h] = ds if db[h] is None else db[h] + ds
        dss.append(ds.astype(bf))
    dk_u = {(r, h): dot_nn(ds, pair_parts(at(q_ref, r, h))).astype(bf) for (r, h), ds in zip(units, dss)}
    full_dq = [dot_tn(ds, at(k_ref, r, h)) for (r, h), ds in zip(units, dss)]
    dq_u = {unit: pair_pick(part).astype(bf) for unit, part in zip(units, full_dq)}
    dqkv = jnp.concatenate(
        [jnp.concatenate([u[r, h] for u in (dq_u, dk_u, dv_u) for h in range(3)], axis=1)
         for r in range(rows)], axis=0)
    dqkv_s[here, :] = dqkv
    back_ref[...] = dqkv
    for h in range(3):
        dbias_s[:, h * 128:h * 128 + 128] += db[h]

    @pl.when(step == last)
    def _():
        for h in range(3):
            columns = slice(h * 384, h * 384 + 384)
            packed[:, columns] = dot_tn(a_s[...], dqkv_s[:, columns]).astype(bf)
        dwo = dot_tn(att_s[...], g_s[...]).astype(bf)
        for shard in range(8):
            for core in range(2):
                for i in range(3):
                    for j in range(2):
                        packed[(shard * 2 + core) * 32 + j * 16:(shard * 2 + core) * 32 + j * 16 + 16,
                               1152 + i * 128:1280 + i * 128] = (
                            dwo[shard * 48 + i * 16:shard * 48 + i * 16 + 16,
                                core * 256 + j * 128:core * 256 + j * 128 + 128])
        dbias_ref[...] = dbias_s[...]
        if with_table:
            table = table_terms(dbias_s[...]).astype(bf)
            for at in range(16):
                packed[at * 32:at * 32 + 32, 1536:1664] = table
        hand_out(ids, packed, keep_ref, give_ref)


def gelu_parts(u):
    c = 0.7978845608028654
    u2 = u * u
    t = jnp.tanh(u * (c + (c * 0.044715) * u2))
    half = 0.5 + 0.5 * t
    act = u * half
    slope = half + (0.5 * u) * (1.0 - t * t) * (c + (3.0 * c * 0.044715) * u2)
    return act, slope


def gelu(u):
    c = 0.7978845608028654
    t = jnp.tanh(u * (c + (c * 0.044715) * (u * u)))
    return u * (0.5 + 0.5 * t)


def ffn_fwd_kernel(ids, x_ref, gain_ref, w0, w1, w2, w3, out_ref, gate_ref, up_ref, wgu, wd):
    @pl.when(pl.program_id(0) == 0)
    def _():
        open_ffn(ids, (w0, w1, w2, w3), wgu, wd)

    x = x_ref[...].astype(f32)
    a = (x * row_scale(x) * gain_ref[...]).astype(bf)
    gate = dot_nn(a, wgu[:, :1024])
    up = dot_nn(a, wgu[:, 1024:])
    gate_ref[...] = gate.astype(bf)
    up_ref[...] = up.astype(bf)
    hidden = (gelu(gate) * up).astype(bf)
    out_ref[...] = (x + dot_nn(hidden, wd[...])).astype(bf)


def ffn_bwd_kernel(ids, x_ref, gate_ref, up_ref, g_ref, gain_ref, w0, w1, w2, w3,
                   back_ref, keep_ref, give_ref, wd, a_s, gub_s, hid_s, g_s, packed):
    step = pl.program_id(0)
    last = pl.num_programs(0) - 1
    block = x_ref.shape[0]

    @pl.when(step == 0)
    def _():
        open_ffn(ids, (w0, w1, w2, w3), None, wd)

    here = pl.ds(pl.multiple_of(step * block, block), block)
    g_low = g_ref[...]
    g_s[here, :] = g_low
    a_s[here, :] = normed(x_ref, gain_ref)
    hg = dot_nt(g_low, wd[...])
    gate = gate_ref[...].astype(f32)
    up = up_ref[...].astype(f32)
    act, slope = gelu_parts(gate)
    hid_s[here, :] = (act * up).astype(bf)
    gb = (hg * up * slope).astype(bf)
    ub = (hg * act).astype(bf)
    gub_s[here, :1024] = gb
    gub_s[here, 1024:] = ub
    back_ref[:, :1024] = gb
    back_ref[:, 1024:] = ub

    @pl.when(step == last)
    def _():
        for h in range(4):
            columns = slice(h * 512, h * 512 + 512)
            packed[:, columns] = dot_tn(a_s[...], gub_s[:, columns]).astype(bf)
        for h in range(2):
            dwd = dot_tn(hid_s[:, h * 512:h * 512 + 512], g_s[...]).astype(bf)
            for at in range(8):
                for i in range(2):
                    packed[(h * 8 + at) * 32:(h * 8 + at) * 32 + 32, 2048 + i * 512:2560 + i * 512] = (
                        dwd[at * 64 + i * 32:at * 64 + i * 32 + 32])
        hand_out(ids, packed, keep_ref, give_ref)


def tok(block, width):
    return pl.BlockSpec((block, width), lambda i, ids: (i, 0))


def full(shape):
    zero = (0,) * len(shape)
    return pl.BlockSpec(shape, lambda i, ids: zero)


def sds(shape, dtype):
    return jax.ShapeDtypeStruct(shape, dtype)


def call(kernel, grid, in_specs, out_specs, out_shape, scratch, micros, name):
    return pl.pallas_call(
        kernel,
        grid_spec=pltpu.PrefetchScalarGridSpec(
            num_scalar_prefetch=1, grid=(grid,), in_specs=in_specs, out_specs=out_specs,
            scratch_shapes=scratch),
        out_shape=out_shape, name=name,
        compiler_params=pltpu.CompilerParams(vmem_limit_bytes=vmem_limit),
        cost_estimate=pl.CostEstimate(flops=int(micros * 1.1e9), bytes_accessed=0, transcendentals=0),
    )


token_block = 512


def attn_fwd(ids, x, mask, bias, gain, parts):
    t, d = x.shape
    block = token_block
    return call(
        attn_fwd_kernel, t // block,
        [tok(block, d), pl.BlockSpec((block // 64, 64, 128), lambda i, ids: (i, 0, 0)), full(bias.shape),
         full((1, d))] + [full(parts[0].shape)] * 4,
        [tok(block, d)] + [tok(block, 384)] * 5,
        [sds((t, d), bf)] + [sds((t, 384), bf)] * 5,
        [pltpu.VMEM((512, 1152), bf), pltpu.VMEM((384, 512), bf)],
        4, "attn_fwd")(ids, x, mask, bias, gain, *parts)


def attn_bwd(ids, x, q, k, v, p, att, g, gain, parts, bias_in, with_table):
    t, d = x.shape
    block = token_block
    n = 1664 if with_table else 1536
    packed = (2, 4, 32, n)
    return call(
        attn_bwd_kernel, t // block,
        [tok(block, d)] + [tok(block, 384)] * 5 + [tok(block, d), full((1, d))]
        + [full(parts[0].shape)] * 4 + [full(bias_in.shape)],
        [tok(block, 1152), full(packed), full(packed), full((64, 384))],
        [sds((t, 1152), bf), sds(packed, bf), sds(packed, bf), sds((64, 384), f32)],
        [pltpu.VMEM((384, 512), bf), pltpu.VMEM((t, d), bf),
         pltpu.VMEM((t, 1152), bf), pltpu.VMEM((t, 384), bf), pltpu.VMEM((t, d), bf),
         pltpu.VMEM((64, 384), f32), pltpu.VMEM((512, n), bf)],
        6, "attn_bwd")(ids, x, q, k, v, p, att, g, gain, *parts, bias_in)


def input_grad(ids, x, back, g, gain, parts):
    t, d = x.shape
    block = token_block
    width = back.shape[1]
    return call(
        input_grad_kernel, t // block,
        [tok(block, d), tok(block, width), tok(block, d), full((1, d))] + [full(parts[0].shape)] * 4,
        [tok(block, d)], [sds((t, d), bf)], [pltpu.VMEM((512, width), bf)],
        20, "input_grad")(ids, x, back, g, gain, *parts)[0]


def ffn_fwd(ids, x, gain, parts):
    t, d = x.shape
    block = token_block
    return call(
        ffn_fwd_kernel, t // block,
        [tok(block, d), full((1, d))] + [full(parts[0].shape)] * 4,
        [tok(block, d), tok(block, 1024), tok(block, 1024)],
        [sds((t, d), bf), sds((t, 1024), bf), sds((t, 1024), bf)],
        [pltpu.VMEM((512, 2048), bf), pltpu.VMEM((1024, 512), bf)],
        4, "ffn_fwd")(ids, x, gain, *parts)


def ffn_bwd(ids, x, gate, up, g, gain, parts):
    t, d = x.shape
    block = token_block
    packed = (2, 4, 32, 3072)
    return call(
        ffn_bwd_kernel, t // block,
        [tok(block, d), tok(block, 1024), tok(block, 1024), tok(block, d), full((1, d))]
        + [full(parts[0].shape)] * 4,
        [tok(block, 2048), full(packed), full(packed)],
        [sds((t, 2048), bf), sds(packed, bf), sds(packed, bf)],
        [pltpu.VMEM((1024, 512), bf), pltpu.VMEM((t, d), bf),
         pltpu.VMEM((t, 2048), bf), pltpu.VMEM((t, 1024), bf), pltpu.VMEM((t, d), bf),
         pltpu.VMEM((512, 3072), bf)],
        6, "ffn_bwd")(ids, x, gate, up, g, gain, *parts)


def pack_kernel(ids, q, k, v, o, gate, up, down, gains, a0, f0, a1, f1):
    core = ids[2]
    row = lax.broadcasted_iota(jnp.int32, (32, 128), 0)
    pair = [jnp.concatenate([gains[l, 0:1, :], gains[l, 1:2, :]], axis=1) for l in range(2)]
    a0[:, 1536:] = jnp.where(row == 0, pair[0], jnp.where(row == 1, pair[1], 0.0)).astype(bf)
    rows = pl.ds(pl.multiple_of(core * 32, 32), 32)
    for layer, a_ref, f_ref in ((0, a0, f0), (1, a1, f1)):
        for at, w in enumerate((q, k, v)):
            a_ref[:, at * 384:at * 384 + 384] = w[layer, rows, :]
        for i in range(3):
            for j in range(2):
                columns = pl.ds(pl.multiple_of(core * 256 + j * 128, 128), 128)
                a_ref[j * 16:j * 16 + 16, 1152 + i * 128:1280 + i * 128] = (
                    o[layer, i * 16:i * 16 + 16, columns])
        f_ref[:, :1024] = gate[layer, rows, :]
        f_ref[:, 1024:2048] = up[layer, rows, :]
        for i in range(2):
            f_ref[:, 2048 + i * 512:2560 + i * 512] = (
                down[layer, pl.ds(pl.multiple_of(core * 64 + i * 32, 32), 32), :])


def pack_weights(ids, *weights):
    shapes = ((32, 1664), (32, 3072), (32, 1536), (32, 3072))
    return call(
        pack_kernel, 1, [full(w.shape) for w in weights], [full(shape) for shape in shapes],
        [sds(shape, bf) for shape in shapes], [], 2, "pack_weights")(ids, *weights)


def unpack_kernel(ids, own, peer, qw, kw, vw, gw, uw, gain, q, k, v, o, gate, up, down, gains, table):
    first = ids[2] == 0
    base = 0

    def row_sums(*pairs):
        total = None
        for weight, grad in pairs:
            term = weight.astype(f32) * grad
            total = term if total is None else total + term
        ones = jnp.ones((8, total.shape[1]), f32)
        sums = lax.dot_general(ones, total, (((1,), (1,)), ((), ())), preferred_element_type=f32,
                               precision=lax.Precision.HIGHEST)
        return sums[0:1, :]

    for s in (3, 2, 1, 0):
        layer = s // 2
        for core in range(2):
            def part(start, width, rows=slice(0, 32)):
                columns = slice(base + start, base + start + width)
                one, two = own[rows, columns].astype(f32), peer[rows, columns].astype(f32)
                return jnp.where(first, one, two) if core == 0 else jnp.where(first, two, one)

            rows = slice(core * 32, core * 32 + 32)
            if s % 2 == 0:
                for at, w in enumerate((q, k, v)):
                    w[layer, rows, :] = part(at * 384, 384)
                for i in range(3):
                    for j in range(2):
                        o[layer, i * 16:i * 16 + 16, core * 256 + j * 128:core * 256 + j * 128 + 128] = (
                            part(1152 + i * 128, 128, slice(j * 16, j * 16 + 16)))
            else:
                gate[layer, rows, :] = part(0, 1024)
                up[layer, rows, :] = part(1024, 1024)
                for i in range(2):
                    down[layer, core * 64 + i * 32:core * 64 + i * 32 + 32, :] = part(2048 + i * 512, 512)
            if s == 0 and core == 1:
                table[...] = part(1536, 128)[:, :6]
        if s % 2 == 0:
            sums = row_sums(*((w[layer], grad[layer]) for w, grad in ((qw, q), (kw, k), (vw, v))))
        else:
            sums = row_sums(*((w[layer], grad[layer]) for w, grad in ((gw, gate), (uw, up))))
        gains[layer, s % 2:s % 2 + 1, :] = sums / gain[layer, s % 2:s % 2 + 1, :]
        base += 1536 if s % 2 == 0 else 3072


def unpack_grads(ids, own, peer, shards, gains, shapes):
    q, k, v, o, gate, up, down = shards
    args = (own, peer, q, k, v, gate, up, gains)
    return call(
        unpack_kernel, 1, [full(array.shape) for array in args], [full(shape) for shape in shapes],
        [sds(shape, f32) for shape in shapes], [], 3, "unpack_grads")(ids, *args)


def move(sources, scratch, targets, sems):
    def fetch(ref, at):
        return pltpu.make_async_copy(ref, scratch.at[at], sems.at[0, at])

    for at, options in enumerate(sources):
        for condition, ref in options:
            if condition is None:
                fetch(ref, at).start()
            else:
                @pl.when(condition)
                def _(ref=ref, at=at):
                    fetch(ref, at).start()
    for at, target in enumerate(targets):
        fetch(sources[at][0][1], at).wait()
        pltpu.make_async_copy(scratch.at[at], target, sems.at[1, at]).start()
    for at, target in enumerate(targets):
        pltpu.make_async_copy(scratch.at[at], target, sems.at[1, at]).wait()


def place_kernel(ids, *refs):
    own, relay, far, cross = refs[:4], refs[4], refs[5:9], refs[9:-3]
    out, scratch, sems = refs[-3:]
    cross = cross + (relay.at[1],) * (4 - len(cross))
    section = ids[3]
    pick = lambda group: [(section == at, ref) for at, ref in enumerate(group)]
    move([pick(own), [(None, relay.at[0])], pick(far), pick(cross)], scratch,
         [out.at[section ^ bit] for bit in range(4)], sems)


def moving(kernel, ids, arrays, out_shape, slots, micros, name):
    anywhere = pl.BlockSpec(memory_space=pl.ANY)
    t, d = arrays[0].shape[-2:]
    return pl.pallas_call(
        kernel,
        grid_spec=pltpu.PrefetchScalarGridSpec(
            num_scalar_prefetch=1, grid=(1,), in_specs=[anywhere] * len(arrays), out_specs=anywhere,
            scratch_shapes=[pltpu.VMEM((slots, t, d), bf), pltpu.SemaphoreType.DMA((2, slots))]),
        out_shape=out_shape, name=name,
        compiler_params=pltpu.CompilerParams(vmem_limit_bytes=vmem_limit),
        cost_estimate=pl.CostEstimate(flops=int(micros * 1.1e9), bytes_accessed=0, transcendentals=0),
    )(ids, *arrays)


def place(ids, own, relay, far, cross):
    arrays = (*own, relay, *far, *cross)
    return moving(place_kernel, ids, arrays, sds((4,) + own[0].shape, bf), 4, 3, "place")


def relay_kernel(ids, *refs):
    own, far = refs[:4], refs[4:8]
    out, scratch, sems = refs[8:]
    pick = lambda group: [((ids[3] ^ 1) == at, ref) for at, ref in enumerate(group)]
    move([pick(own), pick(far)], scratch, [out.at[0], out.at[1]], sems)


def relay(ids, own, far):
    t, d = own[0].shape
    both = moving(relay_kernel, ids, (*own, *far), sds((2, t, d), bf), 2, 2, "relay")
    return swapped(both, "section", 1)


def z_shift(values, by):
    half = lax.axis_size("dp") // 2
    pairs = [(z * 2 + y, ((z + by) % half) * 2 + y) for z in range(half) for y in range(2)]
    return lax.ppermute(values, "dp", pairs)


def swapped(values, axis, bit):
    return lax.ppermute(values, axis, [(i, i ^ bit) for i in range(lax.axis_size(axis))])


def after(values, *others):
    return lax.optimization_barrier((values,) + others)[0]


def added(*terms):
    total = terms[0].astype(f32)
    for term in terms[1:]:
        total = total + term.astype(f32)
    return total.astype(bf)


def gather_part(piece, z, previous):
    if previous is not None:
        piece = after(piece, *previous)
    got = [z_shift(piece, by) for by in range(1, 4)]
    column = jnp.stack([lax.select_n((z - at) % 4, piece, *got) for at in range(4)])
    return (column, swapped(column, "dp", 1)), got


def gather_core(column, other, hold):
    if hold is not None:
        column, other = lax.optimization_barrier((column, other, hold))[:2]
    return column, other, swapped(column, "section", 1), swapped(other, "section", 1)


def reduce_first(keep, give):
    got = swapped(give, "section", 1)
    sent = swapped(added(keep[1], got[1]), "dp", 1)
    far = swapped(added(keep[0, 2:], got[0, 2:], sent[2:]), "dp", 4)
    return dict(keep=keep, core=got, y=sent, far=far)


def reduce_near(step):
    terms = (step["keep"][0, 1], step["core"][0, 1], step["y"][1], step["far"][1])
    return swapped(added(*terms), "dp", 2)


def reduce_last(step):
    return added(step["keep"][0, 0], step["core"][0, 0], step["y"][0], step["far"][0], step["near"])


def to_packed(q, k, v, o, gate, up, down):
    o_part = o.reshape(8, 3, 16, 2, 2, 128).transpose(0, 3, 4, 2, 1, 5).reshape(512, 384)
    d_part = down.reshape(16, 2, 32, 512).transpose(0, 2, 1, 3).reshape(512, 1024)
    return jnp.concatenate([q, k, v, o_part], axis=1), jnp.concatenate([gate, up, d_part], axis=1)


def from_packed(attn, ffn):
    q, k, v = (attn[:, at * 384:at * 384 + 384] for at in range(3))
    o = attn[:, 1152:1536].reshape(8, 2, 2, 16, 3, 128).transpose(0, 4, 3, 1, 2, 5).reshape(384, 512)
    down = ffn[:, 2048:].reshape(16, 32, 2, 512).transpose(0, 2, 1, 3).reshape(1024, 512)
    return q, k, v, o, ffn[:, :1024], ffn[:, 1024:2048], down


def parts_of(whole):
    split = whole.reshape(4, 2, 2, 32, whole.shape[1])
    return tuple(split[:, y, core] for core in range(2) for y in range(2))


def whole_of(keep, give):
    split = jnp.stack([keep, give]).transpose(2, 1, 0, 3, 4)
    return split.reshape(512, keep.shape[3])


def gains_of(column, other, y):
    small = [part[:, :2, 1536:1664].reshape(4, 2, 2, 64) for part in (column, other)]
    pair = [jnp.where(y == at, small[0], small[1]) for at in range(2)]
    return jnp.stack(pair, axis=3).transpose(1, 2, 0, 3, 4).reshape(2, 2, 512).astype(f32)


def body(inputs, cotangent, segments, observed, q_weight, k_weight, v_weight, o_weight,
         gate_weight, up_weight, down_weight, gains, position_table):
    section = lax.axis_index("section")
    dp = lax.axis_index("dp")
    micro_count, row_count, seq_count, width = inputs.shape
    layers = q_weight.shape[0]
    heads = position_table.shape[1]
    tokens = row_count * seq_count
    shards = (q_weight, k_weight, v_weight, o_weight, gate_weight, up_weight, down_weight)
    eight = lax.axis_size("dp") == 8
    own_ids = jnp.stack([dp // 2, dp % 2, section % 2, section]).astype(jnp.int32)
    ids = own_ids if eight else jnp.stack([0 * dp, 0 * dp, 0 * dp, section]).astype(jnp.int32)

    weights = [None] * 4
    if eight:
        pieces = pack_weights(own_ids, *shards, gains.astype(f32))
    else:
        whole = [lax.all_gather(w, "dp", axis=1, tiled=True) for w in shards]
        for layer in range(layers):
            weights[2 * layer], weights[2 * layer + 1] = (
                parts_of(w) for w in to_packed(*(w[layer] for w in whole)))
        gains_all = lax.all_gather(gains, "dp", axis=2, tiled=True).astype(f32)

    x = lax.dynamic_index_in_dim(inputs, section, 0, keepdims=False).reshape(tokens, width)
    grad = lax.dynamic_index_in_dim(cotangent, section, 0, keepdims=False).reshape(tokens, width)
    seg = lax.dynamic_index_in_dim(segments, section, 0, keepdims=False)
    obs = lax.dynamic_index_in_dim(observed, section, 0, keepdims=False)
    allowed = (seg[:, :, None] == seg[:, None, :]) & (obs[:, :, None] == 1)
    mask = jnp.where(allowed, 0.0, masked).astype(f32)
    mask = jnp.concatenate([mask, mask], axis=2)
    position = jnp.arange(seq_count, dtype=jnp.int32)
    bucket = bucket_of(position[:, None], position[None, :])
    onehot = (bucket[:, :, None] == jnp.arange(position_table.shape[0])[None, None, :]).astype(f32)
    bias = jnp.einsum("jib,bh->jhi", onehot, position_table.astype(f32), precision=lax.Precision.HIGHEST)
    bias = bias.reshape(seq_count, heads * seq_count)

    chip = section // 2

    def across(value, pairs):
        return lax.ppermute(value, "section", pairs)

    arrived = [()] * 4
    if eight:
        previous = None
        for s in range(4):
            weights[s], previous = gather_part(pieces[s], dp // 2, previous)
            arrived[s] = previous
        gains_all = gains_of(*weights[0], dp % 2)

    states, kept = [x], []
    out_far = [None] * 4
    for s in range(4):
        gain = gains_all[s // 2, s % 2][None]
        feed = after(states[s], *arrived[s + 1]) if s < 3 else states[s]
        if eight:
            weights[s] = gather_core(*weights[s], states[s] if s > 0 else None)
        if s % 2 == 0:
            out, *saved = attn_fwd(ids, feed, mask, bias, gain, weights[s])
        else:
            out, *saved = ffn_fwd(ids, feed, gain, weights[s])
        states.append(out)
        kept.append(saved)
        if s >= 2:
            out_far[s] = out_far[s - 2] = swapped(jnp.where(chip == 0, out, states[s - 1]), "section", 2)
    outs = states[1:]

    grads, grad_far = [None] * 4, [None] * 4
    packed, steps = [None] * 4, [None] * 4
    bias_sum = jnp.zeros((seq_count, heads * seq_count), f32)

    def wait(value, *names):
        others = [steps[s][name] for s, name in names] if eight else []
        return after(value, *others) if others else value

    def back_part(s, grad):
        gain = gains_all[s // 2, s % 2][None]
        if s % 2 == 1:
            back, keep, give = ffn_bwd(ids, states[s], *kept[s], grad, gain, weights[s])
            total = bias_sum
        else:
            back, keep, give, total = attn_bwd(
                ids, states[s], *kept[s], grad, gain, weights[s], bias_sum, eight and s == 0)
        if eight:
            steps[s] = reduce_first(keep, give)
        else:
            packed[s] = whole_of(keep, give)
        return back, total

    def front_part(s, back, grad):
        gain = gains_all[s // 2, s % 2][None]
        grads[s] = input_grad(ids, states[s], back, grad, gain, weights[s])
        grad_far[s] = across(grads[s], [(0, 2), (1, 3)] if s >= 2 else [(2, 0), (3, 1)])
        return grads[s]

    back, bias_sum = back_part(3, grad)
    grad = front_part(3, back, after(grad, out_far[2]))
    back, bias_sum = back_part(2, wait(grad, (3, "core")))
    grad = front_part(2, back, after(wait(grad, (3, "y")), out_far[3]))
    out_relay = relay(ids, outs, out_far[:3] + [after(out_far[3], grad)])
    back, bias_sum = back_part(1, wait(grad, (2, "core"), (3, "far")))
    if eight:
        steps[3]["near"] = reduce_near(steps[3])
    grad = front_part(1, back, after(wait(grad, (2, "y"), (3, "near")), grad_far[3]))
    back, bias_sum = back_part(0, after(wait(grad, (1, "core")), grad_far[2], out_relay))
    if eight:
        steps[2]["far"] = after(steps[2]["far"], steps[0]["keep"])
        for s in (2, 1, 0):
            steps[s]["near"] = reduce_near(steps[s])
    grad = front_part(0, back, wait(grad, (2, "far")))

    shape = (1, micro_count, row_count, seq_count, width)
    section_outputs = place(ids, outs, out_relay, out_far, []).reshape(shape)
    grad_relay = relay(ids, grads, grad_far)
    section_grads = place(ids, grads, grad_relay, grad_far, []).reshape(shape)

    if eight:
        own = []
        for pair in ((3, 2), (1, 0)):
            both = jnp.concatenate([reduce_last(steps[s]) for s in pair], axis=1)
            own.append(added(both, swapped(both, "section", 2)))
        own = jnp.concatenate(own, axis=1)
        shapes = [w.shape for w in shards] + [gains.shape, position_table.shape]
        final = unpack_grads(ids, own, swapped(own, "section", 1), shards, gains.astype(f32), shapes)
        return (section_outputs, section_grads) + tuple(final)

    dense = [from_packed(packed[2 * layer], packed[2 * layer + 1]) for layer in range(layers)]
    final = []
    for at in range(7):
        both = jnp.stack([d[at] for d in dense])
        part = lax.psum_scatter(both, "dp", scatter_dimension=1, tiled=True)
        final.append(lax.psum(part, "section").astype(f32))
    terms = [w.astype(f32) * final[at] for at, w in enumerate(shards)]
    gain_sums = [sum(jnp.sum(terms[at], axis=2) for at in group) for group in ((0, 1, 2), (4, 5))]
    gains_grad = jnp.stack(gain_sums, axis=1) / gains.astype(f32)
    bias_sum = bias_sum.reshape(seq_count, heads, seq_count)
    table = jnp.einsum("jib,jhi->bh", onehot, bias_sum, precision=lax.Precision.HIGHEST)
    return (section_outputs, section_grads) + tuple(final) + (gains_grad, lax.psum(table, ("section", "dp")))


def solution(mesh):
    rows4 = P(None, "dp", None, None)
    rows3 = P(None, "dp", None)
    staged = P("section", None, "dp", None, None)
    return jax.shard_map(
        body,
        mesh=mesh,
        in_specs=(rows4, rows4) + (rows3,) * 9 + (P(None, None, "dp"), P()),
        out_specs=(staged, staged) + (rows3,) * 7 + (P(None, None, "dp"), P()),
        check_vma=False,
    )
```

```python
import jax
import jax.numpy as jnp
from jax import lax
from jax.experimental import pallas as pl
from jax.experimental.pallas import tpu as pltpu
from jax.sharding import PartitionSpec as P

eps_norm = 1e-06
limits = (12, 16, 23, 32, 46, 64, 91)
masked = -1e30
bf = jnp.bfloat16
f32 = jnp.float32
vmem_mib = dict(
    attn_fwd=40, ffn_fwd=40, ffn_both=42, ffn_bwd=30, attn_bwd=22,
    input_grad=12, pack_weights=56, unpack_grads=16, place=9, relay=6)


def dot_nn(a, b):
    return lax.dot_general(a, b, (((1,), (0,)), ((), ())), preferred_element_type=f32)


def dot_nt(a, b):
    return lax.dot_general(a, b, (((1,), (1,)), ((), ())), preferred_element_type=f32)


def dot_tn(a, b):
    return lax.dot_general(a, b, (((0,), (0,)), ((), ())), preferred_element_type=f32)


def row_scale(x):
    return lax.rsqrt(jnp.mean(x * x, axis=-1, keepdims=True) + eps_norm)


def pair_parts(values):
    lane = lax.broadcasted_iota(jnp.int32, values.shape, 1)
    zero = jnp.zeros_like(values)
    return jnp.concatenate(
        [jnp.where(lane < 64, values, zero), jnp.where(lane < 64, zero, values)], axis=0
    )


def pair_pick(values):
    half = values.shape[0] // 2
    lane = lax.broadcasted_iota(jnp.int32, (half, values.shape[1]), 1)
    return jnp.where(lane < 64, values[:half], values[half:])


blocks = 16
block_rows = 32


def order_of(ids, z, other_y, other_core):
    return (z * 2 + (ids[1] ^ other_y)) * 2 + (ids[2] ^ other_core)


def open_attn(ids, parts, wqkv, wo):
    for at, ref in enumerate(parts):
        other_y, other_core = at % 2, at // 2
        for z in range(4):
            place = order_of(ids, z, other_y, other_core)
            if wqkv is not None:
                wqkv[pl.ds(pl.multiple_of(place * 32, 32), 32), :] = ref[z, :, :1152]
            shard = z * 2 + (ids[1] ^ other_y)
            core = ids[2] ^ other_core
            for i in range(3):
                rows = pl.ds(pl.multiple_of(shard * 48 + i * 16, 16), 16)
                for j in range(2):
                    columns = pl.ds(pl.multiple_of(core * 256 + j * 128, 128), 128)
                    wo[rows, columns] = ref[z, j * 16:j * 16 + 16, 1152 + i * 128:1280 + i * 128]


def open_ffn(ids, parts, wgu, wd):
    for at, ref in enumerate(parts):
        other_y, other_core = at % 2, at // 2
        for z in range(4):
            place = order_of(ids, z, other_y, other_core)
            if wgu is not None:
                wgu[pl.ds(pl.multiple_of(place * 32, 32), 32), :] = ref[z, :, :2048]
            for i in range(2):
                wd[pl.ds(pl.multiple_of(place * 64 + i * 32, 32), 32), :] = (
                    ref[z, :, 2048 + i * 512:2560 + i * 512])


def hand_out(ids, packed, refs):
    for at, ref in enumerate(refs):
        for by in range(4):
            place = order_of(ids, ids[0] ^ by, at % 2, at // 2)
            ref[by] = packed[pl.ds(pl.multiple_of(place * 32, 32), 32), :]


def attn_fwd_kernel(ids, x_ref, mask_ref, bias_ref, gain_ref, w0, w1, w2, w3,
                    out_ref, q_ref, k_ref, v_ref, p_ref, att_ref, wqkv, wo):
    @pl.when(pl.program_id(0) == 0)
    def _():
        open_attn(ids, (w0, w1, w2, w3), wqkv, wo)

    x = x_ref[...].astype(f32)
    a = (x * row_scale(x) * gain_ref[...]).astype(bf)
    q = dot_nn(a, wqkv[:, :384]).astype(bf)
    k = dot_nn(a, wqkv[:, 384:768]).astype(bf)
    v = dot_nn(a, wqkv[:, 768:]).astype(bf)
    q_ref[...] = q
    k_ref[...] = k
    v_ref[...] = v
    rows = x.shape[0] // 64
    units = [(r, h) for r in range(rows) for h in range(3)]
    at = lambda arr, r, h: arr[r * 64:r * 64 + 64, h * 128:h * 128 + 128]
    scores = [dot_nt(at(k, r, h), pair_parts(at(q, r, h))) for r, h in units]
    probs = []
    for (r, h), s in zip(units, scores):
        s = s + (bias_ref[:, h * 128:h * 128 + 128] + mask_ref[r])
        e = jnp.exp(s - jnp.max(s, axis=0, keepdims=True))
        p = (e * (1.0 / jnp.sum(e, axis=0, keepdims=True))).astype(bf)
        p_ref[r * 64:r * 64 + 64, h * 128:h * 128 + 128] = p
        probs.append(p)
    full_att = [dot_tn(p, at(v, r, h)) for (r, h), p in zip(units, probs)]
    att = {unit: pair_pick(part).astype(bf) for unit, part in zip(units, full_att)}
    att = jnp.concatenate(
        [jnp.concatenate([att[r, h] for h in range(3)], axis=1) for r in range(rows)], axis=0)
    att_ref[...] = att
    out_ref[...] = (x + dot_nn(att, wo[...])).astype(bf)


def normed(x_ref, gain_ref):
    x = x_ref[...].astype(f32)
    return (x * row_scale(x) * gain_ref[...]).astype(bf)


def input_grad_kernel(ids, x_ref, back_ref, g_ref, gain_ref, w0, w1, w2, w3, gin_ref, w_s):
    width = back_ref.shape[1]

    @pl.when(pl.program_id(0) == 0)
    def _():
        for at, ref in enumerate((w0, w1, w2, w3)):
            for z in range(4):
                place = order_of(ids, z, at % 2, at // 2)
                w_s[pl.ds(pl.multiple_of(place * 32, 32), 32), :] = ref[z, :, :width]

    gx = dot_nt(back_ref[...], w_s[...])
    x = x_ref[...].astype(f32)
    scale = row_scale(x)
    n = x * scale
    e = gx * gain_ref[...]
    dx = scale * (e - n * jnp.mean(e * n, axis=-1, keepdims=True))
    gin_ref[...] = (g_ref[...].astype(f32) + dx).astype(bf)


def bucket_of(key, query):
    offset = key - query
    distance = jnp.abs(offset)
    far = jnp.full(distance.shape, 8, jnp.int32)
    for threshold in limits:
        far = far + (distance >= threshold).astype(jnp.int32)
    near = jnp.where(distance < 8, distance, jnp.minimum(far, 15))
    return near + 16 * (offset > 0).astype(jnp.int32)


def table_terms(bias_grad):
    key = lax.broadcasted_iota(jnp.int32, (64, 128), 0)
    query = lax.broadcasted_iota(jnp.int32, (64, 128), 1) & 63
    bucket = bucket_of(key, query)
    pieces = [bias_grad[:, h * 128:h * 128 + 128] for h in range(3)]
    sums = [[], [], []]
    for b in range(32):
        hit = bucket == b
        for h in range(3):
            sums[h].append(jnp.sum(jnp.where(hit, pieces[h], 0.0), axis=0, keepdims=True))
    lane = lax.broadcasted_iota(jnp.int32, (32, 128), 1)
    table = jnp.zeros((32, 128), f32)
    for h in range(3):
        part = jnp.concatenate(sums[h], axis=0)
        low = jnp.sum(jnp.where(lane < 64, part, 0.0), axis=1, keepdims=True)
        high = jnp.sum(jnp.where(lane < 64, 0.0, part), axis=1, keepdims=True)
        table = jnp.where(lane == 2 * h, low, jnp.where(lane == 2 * h + 1, high, table))
    return table


def attn_bwd_kernel(ids, x_ref, q_ref, k_ref, v_ref, p_ref, att_ref, g_ref, gain_ref, w0, w1, w2, w3,
                    bias_in, back_ref, r0, r1, r2, r3, dbias_ref,
                    wo, a_s, dqkv_s, att_s, g_s, dbias_s, packed):
    step = pl.program_id(0)
    last = pl.num_programs(0) - 1
    block = x_ref.shape[0]
    with_table = r0.shape[2] > 1536

    @pl.when(step == 0)
    def _():
        open_attn(ids, (w0, w1, w2, w3), None, wo)
        dbias_s[...] = bias_in[...]

    here = pl.ds(pl.multiple_of(step * block, block), block)
    g_low = g_ref[...]
    da = dot_nt(g_low, wo[...]).astype(bf)
    att_s[here, :] = att_ref[...]
    g_s[here, :] = g_low
    rows = block // 64
    units = [(r, h) for r in range(rows) for h in range(3)]
    at = lambda arr, r, h: arr[r * 64:r * 64 + 64, h * 128:h * 128 + 128]
    db = [None] * 3
    da_bds = [pair_parts(at(da, r, h)) for r, h in units]
    dps = [dot_nt(at(v_ref, r, h), da_bd) for (r, h), da_bd in zip(units, da_bds)]
    dv_u = {(r, h): dot_nn(at(p_ref, r, h), da_bd).astype(bf) for (r, h), da_bd in zip(units, da_bds)}
    dss = []
    for (r, h), dp in zip(units, dps):
        pf = at(p_ref, r, h).astype(f32)
        ds = pf * (dp - jnp.sum(pf * dp, axis=0, keepdims=True))
        db[h] = ds if db[h] is None else db[h] + ds
        dss.append(ds.astype(bf))
    dk_u = {(r, h): dot_nn(ds, pair_parts(at(q_ref, r, h))).astype(bf) for (r, h), ds in zip(units, dss)}
    full_dq = [dot_tn(ds, at(k_ref, r, h)) for (r, h), ds in zip(units, dss)]
    dq_u = {unit: pair_pick(part).astype(bf) for unit, part in zip(units, full_dq)}
    dqkv = jnp.concatenate(
        [jnp.concatenate([u[r, h] for u in (dq_u, dk_u, dv_u) for h in range(3)], axis=1)
         for r in range(rows)], axis=0)
    dqkv_s[here, :] = dqkv
    for h in range(3):
        dbias_s[:, h * 128:h * 128 + 128] += db[h]
    back_ref[...] = dqkv
    a_s[here, :] = normed(x_ref, gain_ref)

    @pl.when(step == last)
    def _():
        for h in range(3):
            columns = slice(h * 384, h * 384 + 384)
            packed[:, columns] = dot_tn(a_s[...], dqkv_s[:, columns]).astype(bf)
        dwo = dot_tn(att_s[...], g_s[...]).astype(bf)
        for shard in range(8):
            for core in range(2):
                for i in range(3):
                    for j in range(2):
                        packed[(shard * 2 + core) * 32 + j * 16:(shard * 2 + core) * 32 + j * 16 + 16,
                               1152 + i * 128:1280 + i * 128] = (
                            dwo[shard * 48 + i * 16:shard * 48 + i * 16 + 16,
                                core * 256 + j * 128:core * 256 + j * 128 + 128])
        dbias_ref[...] = dbias_s[...]
        if with_table:
            table = table_terms(dbias_s[...]).astype(bf)
            for at in range(16):
                packed[at * 32:at * 32 + 32, 1536:1664] = table
        hand_out(ids, packed, (r0, r1, r2, r3))


def gelu_parts(u):
    c = 0.7978845608028654
    u2 = u * u
    t = jnp.tanh(u * (c + (c * 0.044715) * u2))
    half = 0.5 + 0.5 * t
    act = u * half
    slope = half + (0.5 * u) * (1.0 - t * t) * (c + (3.0 * c * 0.044715) * u2)
    return act, slope


def gelu(u):
    c = 0.7978845608028654
    t = jnp.tanh(u * (c + (c * 0.044715) * (u * u)))
    return u * (0.5 + 0.5 * t)


def ffn_fwd_kernel(ids, x_ref, gain_ref, w0, w1, w2, w3, out_ref, gate_ref, up_ref, wgu, wd):
    @pl.when(pl.program_id(0) == 0)
    def _():
        open_ffn(ids, (w0, w1, w2, w3), wgu, wd)

    x = x_ref[...].astype(f32)
    a = (x * row_scale(x) * gain_ref[...]).astype(bf)
    gate = dot_nn(a, wgu[:, :1024])
    up = dot_nn(a, wgu[:, 1024:])
    gate_ref[...] = gate.astype(bf)
    up_ref[...] = up.astype(bf)
    hidden = (gelu(gate) * up).astype(bf)
    out_ref[...] = (x + dot_nn(hidden, wd[...])).astype(bf)


def ffn_weight_grads(ids, a_s, gub_s, hid_s, g_s, packed, refs):
    for h in range(4):
        columns = slice(h * 512, h * 512 + 512)
        packed[:, columns] = dot_tn(a_s[...], gub_s[:, columns]).astype(bf)
    for h in range(2):
        dwd = dot_tn(hid_s[:, h * 512:h * 512 + 512], g_s[...]).astype(bf)
        for at in range(8):
            for i in range(2):
                packed[(h * 8 + at) * 32:(h * 8 + at) * 32 + 32, 2048 + i * 512:2560 + i * 512] = (
                    dwd[at * 64 + i * 32:at * 64 + i * 32 + 32])
    hand_out(ids, packed, refs)


def ffn_bwd_kernel(ids, x_ref, gate_ref, up_ref, g_ref, gain_ref, w0, w1, w2, w3,
                   back_ref, r0, r1, r2, r3, wd, a_s, gub_s, hid_s, g_s, packed):
    step = pl.program_id(0)
    block = x_ref.shape[0]

    @pl.when(step == 0)
    def _():
        open_ffn(ids, (w0, w1, w2, w3), None, wd)

    here = pl.ds(pl.multiple_of(step * block, block), block)
    g_low = g_ref[...]
    g_s[here, :] = g_low
    hg = dot_nt(g_low, wd[...])
    gate = gate_ref[...].astype(f32)
    up = up_ref[...].astype(f32)
    act, slope = gelu_parts(gate)
    hid_s[here, :] = (act * up).astype(bf)
    gb = (hg * up * slope).astype(bf)
    ub = (hg * act).astype(bf)
    gub_s[here, :1024] = gb
    gub_s[here, 1024:] = ub
    back_ref[:, :1024] = gb
    back_ref[:, 1024:] = ub
    a_s[here, :] = normed(x_ref, gain_ref)

    @pl.when(step == pl.num_programs(0) - 1)
    def _():
        ffn_weight_grads(ids, a_s, gub_s, hid_s, g_s, packed, (r0, r1, r2, r3))


def ffn_both_kernel(ids, x_ref, g_ref, gain_ref, w0, w1, w2, w3,
                    out_ref, back_ref, r0, r1, r2, r3, wgu, wd, a_s, gub_s, hid_s, g_s, packed):
    step = pl.program_id(0)
    block = x_ref.shape[0]

    @pl.when(step == 0)
    def _():
        open_ffn(ids, (w0, w1, w2, w3), wgu, wd)

    here = pl.ds(pl.multiple_of(step * block, block), block)
    x = x_ref[...].astype(f32)
    a = (x * row_scale(x) * gain_ref[...]).astype(bf)
    gate = dot_nn(a, wgu[:, :1024])
    up = dot_nn(a, wgu[:, 1024:])
    g_low = g_ref[...]
    g_s[here, :] = g_low
    hg = dot_nt(g_low, wd[...])
    act, slope = gelu_parts(gate)
    hidden = (act * up).astype(bf)
    hid_s[here, :] = hidden
    out_ref[...] = (x + dot_nn(hidden, wd[...])).astype(bf)
    gb = (hg * up * slope).astype(bf)
    ub = (hg * act).astype(bf)
    gub_s[here, :1024] = gb
    gub_s[here, 1024:] = ub
    back_ref[:, :1024] = gb
    back_ref[:, 1024:] = ub
    a_s[here, :] = a

    @pl.when(step == pl.num_programs(0) - 1)
    def _():
        ffn_weight_grads(ids, a_s, gub_s, hid_s, g_s, packed, (r0, r1, r2, r3))


def tok(block, width):
    return pl.BlockSpec((block, width), lambda i, ids: (i, 0))


def picked(block, width):
    return pl.BlockSpec((None, block, width), lambda i, ids: (ids[3], i, 0))


def tokens_of(array, block):
    return (tok if array.ndim == 2 else picked)(block, array.shape[-1])


def full(shape):
    zero = (0,) * len(shape)
    return pl.BlockSpec(shape, lambda i, ids: zero)


def sds(shape, dtype):
    return jax.ShapeDtypeStruct(shape, dtype)


def call(kernel, grid, in_specs, out_specs, out_shape, scratch, micros, name):
    return pl.pallas_call(
        kernel,
        grid_spec=pltpu.PrefetchScalarGridSpec(
            num_scalar_prefetch=1, grid=(grid,), in_specs=in_specs, out_specs=out_specs,
            scratch_shapes=scratch),
        out_shape=out_shape, name=name,
        compiler_params=pltpu.CompilerParams(vmem_limit_bytes=vmem_mib[name] << 20),
        cost_estimate=pl.CostEstimate(flops=int(micros * 1.1e9), bytes_accessed=0, transcendentals=0),
    )


token_block = 512


def attn_fwd(ids, x, mask, bias, gain, parts):
    t, d = x.shape[-2:]
    block = token_block
    return call(
        attn_fwd_kernel, t // block,
        [tokens_of(x, block), pl.BlockSpec((block // 64, 64, 128), lambda i, ids: (i, 0, 0)),
         full(bias.shape), full((1, d))] + [full(parts[0].shape)] * 4,
        [tok(block, d)] + [tok(block, 384)] * 5,
        [sds((t, d), bf)] + [sds((t, 384), bf)] * 5,
        [pltpu.VMEM((512, 1152), bf), pltpu.VMEM((384, 512), bf)],
        7, "attn_fwd")(ids, x, mask, bias, gain, *parts)


def attn_bwd(ids, x, q, k, v, p, att, g, gain, parts, bias_in, with_table):
    t, d = x.shape[-2:]
    block = token_block
    n = 1664 if with_table else 1536
    packed = (4, 32, n)
    return call(
        attn_bwd_kernel, t // block,
        [tokens_of(x, block)] + [tok(block, 384)] * 5 + [tok(block, d), full((1, d))]
        + [full(parts[0].shape)] * 4 + [full(bias_in.shape)],
        [tok(block, 1152)] + [full(packed)] * 4 + [full((64, 384))],
        [sds((t, 1152), bf)] + [sds(packed, bf)] * 4 + [sds((64, 384), f32)],
        [pltpu.VMEM((384, 512), bf), pltpu.VMEM((t, d), bf),
         pltpu.VMEM((t, 1152), bf), pltpu.VMEM((t, 384), bf), pltpu.VMEM((t, d), bf),
         pltpu.VMEM((64, 384), f32), pltpu.VMEM((512, n), bf)],
        9, "attn_bwd")(ids, x, q, k, v, p, att, g, gain, *parts, bias_in)


def input_grad(ids, x, back, g, gain, parts):
    t, d = x.shape[-2:]
    block = token_block
    width = back.shape[1]
    rows, columns = parts[0].shape[1:]
    part = pl.BlockSpec((4, rows, width if width % 128 == 0 and columns != width else columns),
                        lambda i, ids: (0, 0, 0))
    return call(
        input_grad_kernel, t // block,
        [tokens_of(x, block), tok(block, width), tokens_of(g, block), full((1, d))] + [part] * 4,
        [tok(block, d)], [sds((t, d), bf)], [pltpu.VMEM((512, width), bf)],
        20, "input_grad")(ids, x, back, g, gain, *parts)[0]


def ffn_fwd(ids, x, gain, parts):
    t, d = x.shape
    block = token_block
    return call(
        ffn_fwd_kernel, t // block,
        [tok(block, d), full((1, d))] + [full(parts[0].shape)] * 4,
        [tok(block, d), tok(block, 1024), tok(block, 1024)],
        [sds((t, d), bf), sds((t, 1024), bf), sds((t, 1024), bf)],
        [pltpu.VMEM((512, 2048), bf), pltpu.VMEM((1024, 512), bf)],
        7, "ffn_fwd")(ids, x, gain, *parts)


def ffn_scratch(t, d):
    return [pltpu.VMEM((1024, 512), bf), pltpu.VMEM((t, d), bf),
            pltpu.VMEM((t, 2048), bf), pltpu.VMEM((t, 1024), bf), pltpu.VMEM((t, d), bf),
            pltpu.VMEM((512, 3072), bf)]


def ffn_bwd(ids, x, gate, up, g, gain, parts):
    t, d = x.shape
    block = token_block
    packed = (4, 32, 3072)
    return call(
        ffn_bwd_kernel, t // block,
        [tok(block, d), tok(block, 1024), tok(block, 1024), tok(block, d), full((1, d))]
        + [full(parts[0].shape)] * 4,
        [tok(block, 2048)] + [full(packed)] * 4,
        [sds((t, 2048), bf)] + [sds(packed, bf)] * 4,
        ffn_scratch(t, d), 12, "ffn_bwd")(ids, x, gate, up, g, gain, *parts)


def ffn_both(ids, x, g, gain, parts):
    t, d = x.shape
    block = token_block
    packed = (4, 32, 3072)
    return call(
        ffn_both_kernel, t // block,
        [tok(block, d), tokens_of(g, block), full((1, d))] + [full(parts[0].shape)] * 4,
        [tok(block, d), tok(block, 2048)] + [full(packed)] * 4,
        [sds((t, d), bf), sds((t, 2048), bf)] + [sds(packed, bf)] * 4,
        [pltpu.VMEM((512, 2048), bf)] + ffn_scratch(t, d), 15, "ffn_both")(ids, x, g, gain, *parts)


def pack_kernel(ids, q, k, v, o, gate, up, down, gains, a0, f0, a1, f1):
    core = ids[2]
    row = lax.broadcasted_iota(jnp.int32, (32, 128), 0)
    pair = [jnp.concatenate([gains[l, 0:1, :], gains[l, 1:2, :]], axis=1) for l in range(2)]
    a0[:, 1536:] = jnp.where(row == 0, pair[0], jnp.where(row == 1, pair[1], 0.0)).astype(bf)
    rows = pl.ds(pl.multiple_of(core * 32, 32), 32)
    for layer, a_ref, f_ref in ((0, a0, f0), (1, a1, f1)):
        for at, w in enumerate((q, k, v)):
            a_ref[:, at * 384:at * 384 + 384] = w[layer, rows, :]
        for i in range(3):
            for j in range(2):
                columns = pl.ds(pl.multiple_of(core * 256 + j * 128, 128), 128)
                a_ref[j * 16:j * 16 + 16, 1152 + i * 128:1280 + i * 128] = (
                    o[layer, i * 16:i * 16 + 16, columns])
        f_ref[:, :1024] = gate[layer, rows, :]
        f_ref[:, 1024:2048] = up[layer, rows, :]
        for i in range(2):
            f_ref[:, 2048 + i * 512:2560 + i * 512] = (
                down[layer, pl.ds(pl.multiple_of(core * 64 + i * 32, 32), 32), :])


def pack_weights(ids, *weights):
    shapes = ((32, 1664), (32, 3072), (32, 1536), (32, 3072))
    return call(
        pack_kernel, 1, [full(w.shape) for w in weights], [full(shape) for shape in shapes],
        [sds(shape, bf) for shape in shapes], [], 2, "pack_weights")(ids, *weights)


def unpack_kernel(ids, own, peer, qw, kw, vw, gw, uw, gain, q, k, v, o, gate, up, down, gains, table):
    first = ids[2] == 0
    base = 0

    def row_sums(*pairs):
        total = None
        for weight, grad in pairs:
            term = weight.astype(f32) * grad
            total = term if total is None else total + term
        ones = jnp.ones((8, total.shape[1]), f32)
        sums = lax.dot_general(ones, total, (((1,), (1,)), ((), ())), preferred_element_type=f32,
                               precision=lax.Precision.HIGHEST)
        return sums[0:1, :]

    for s in (3, 2, 1, 0):
        layer = s // 2
        for core in range(2):
            def part(start, width, rows=slice(0, 32)):
                columns = slice(base + start, base + start + width)
                one, two = own[rows, columns].astype(f32), peer[rows, columns].astype(f32)
                return jnp.where(first, one, two) if core == 0 else jnp.where(first, two, one)

            rows = slice(core * 32, core * 32 + 32)
            if s % 2 == 0:
                for at, w in enumerate((q, k, v)):
                    w[layer, rows, :] = part(at * 384, 384)
                for i in range(3):
                    for j in range(2):
                        o[layer, i * 16:i * 16 + 16, core * 256 + j * 128:core * 256 + j * 128 + 128] = (
                            part(1152 + i * 128, 128, slice(j * 16, j * 16 + 16)))
            else:
                gate[layer, rows, :] = part(0, 1024)
                up[layer, rows, :] = part(1024, 1024)
                for i in range(2):
                    down[layer, core * 64 + i * 32:core * 64 + i * 32 + 32, :] = part(2048 + i * 512, 512)
            if s == 0 and core == 1:
                table[...] = part(1536, 128).T[:6, :]
        if s % 2 == 0:
            sums = row_sums(*((w[layer], grad[layer]) for w, grad in ((qw, q), (kw, k), (vw, v))))
        else:
            sums = row_sums(*((w[layer], grad[layer]) for w, grad in ((gw, gate), (uw, up))))
        gains[layer, s % 2:s % 2 + 1, :] = sums / gain[layer, s % 2:s % 2 + 1, :]
        base += 1536 if s % 2 == 0 else 3072


def unpack_grads(ids, own, peer, shards, gains, shapes):
    q, k, v, o, gate, up, down = shards
    args = (own, peer, q, k, v, gate, up, gains)
    return call(
        unpack_kernel, 1, [full(array.shape) for array in args], [full(shape) for shape in shapes],
        [sds(shape, f32) for shape in shapes], [], 3, "unpack_grads")(ids, *args)


def move(sources, scratch, targets, sems):
    def fetch(ref, at):
        return pltpu.make_async_copy(ref, scratch.at[at], sems.at[0, at])

    for at, options in enumerate(sources):
        for condition, ref in options:
            if condition is None:
                fetch(ref, at).start()
            else:
                @pl.when(condition)
                def _(ref=ref, at=at):
                    fetch(ref, at).start()
    for at, target in enumerate(targets):
        fetch(sources[at][0][1], at).wait()
        pltpu.make_async_copy(scratch.at[at], target, sems.at[1, at]).start()
    for at, target in enumerate(targets):
        pltpu.make_async_copy(scratch.at[at], target, sems.at[1, at]).wait()


def place_kernel(ids, *refs):
    own, relay, far, cross = refs[:4], refs[4], refs[5:9], refs[9:-3]
    out, scratch, sems = refs[-3:]
    cross = cross + (relay.at[1],) * (4 - len(cross))
    section = ids[3]
    pick = lambda group: [(section == at, ref) for at, ref in enumerate(group)]
    move([pick(own), [(None, relay.at[0])], pick(far), pick(cross)], scratch,
         [out.at[section ^ bit] for bit in range(4)], sems)


def moving(kernel, ids, arrays, out_shape, slots, micros, name):
    anywhere = pl.BlockSpec(memory_space=pl.ANY)
    t, d = arrays[0].shape[-2:]
    return pl.pallas_call(
        kernel,
        grid_spec=pltpu.PrefetchScalarGridSpec(
            num_scalar_prefetch=1, grid=(1,), in_specs=[anywhere] * len(arrays), out_specs=anywhere,
            scratch_shapes=[pltpu.VMEM((slots, t, d), bf), pltpu.SemaphoreType.DMA((2, slots))]),
        out_shape=out_shape, name=name,
        compiler_params=pltpu.CompilerParams(vmem_limit_bytes=vmem_mib[name] << 20),
        cost_estimate=pl.CostEstimate(flops=int(micros * 1.1e9), bytes_accessed=0, transcendentals=0),
    )(ids, *arrays)


def place(ids, own, relay, far, cross):
    arrays = (*own, relay, *far, *cross)
    return moving(place_kernel, ids, arrays, sds((4,) + own[0].shape, bf), 4, 3, "place")


def relay_kernel(ids, *refs):
    own, far = refs[:4], refs[4:8]
    out, scratch, sems = refs[8:]
    pick = lambda group: [((ids[3] ^ 1) == at, ref) for at, ref in enumerate(group)]
    move([pick(own), pick(far)], scratch, [out.at[0], out.at[1]], sems)


def relay(ids, own, far):
    t, d = own[0].shape
    both = moving(relay_kernel, ids, (*own, *far), sds((2, t, d), bf), 2, 2, "relay")
    return swapped(both, "section", 1)


def z_shift(values, by):
    half = lax.axis_size("dp") // 2
    pairs = [(z * 2 + y, ((z + by) % half) * 2 + y) for z in range(half) for y in range(2)]
    return lax.ppermute(values, "dp", pairs)


def swapped(values, axis, bit):
    return lax.ppermute(values, axis, [(i, i ^ bit) for i in range(lax.axis_size(axis))])


def after(values, *others):
    return lax.optimization_barrier((values,) + others)[0]


def added(*terms):
    total = terms[0].astype(f32)
    for term in terms[1:]:
        total = total + term.astype(f32)
    return total.astype(bf)


def gather_part(piece, z, previous):
    if previous is not None:
        piece = after(piece, *previous)
    got = [z_shift(piece, by) for by in range(1, 4)]
    column = jnp.stack([lax.select_n((z - at) % 4, piece, *got) for at in range(4)])
    return (column, swapped(column, "dp", 1)), got


def gather_core(column, other, hold):
    if hold is not None:
        column, other = lax.optimization_barrier((column, other, hold))[:2]
    return column, other, swapped(column, "section", 1), swapped(other, "section", 1)


def reduce_first(own, other, give_own, give_other):
    first = swapped(give_other, "section", 1)
    sent = swapped(added(other, first), "dp", 1)
    got = swapped(give_own, "section", 1)
    far = swapped(added(own[2:], got[2:], sent[2:]), "dp", 4)
    return dict(keep=own, first=first, core=got, y=sent, far=far)


def reduce_near(step):
    terms = (step["keep"][1], step["core"][1], step["y"][1], step["far"][1])
    return swapped(added(*terms), "dp", 2)


def reduce_last(step):
    return added(step["keep"][0], step["core"][0], step["y"][0], step["far"][0], step["near"])


def to_packed(q, k, v, o, gate, up, down):
    o_part = o.reshape(8, 3, 16, 2, 2, 128).transpose(0, 3, 4, 2, 1, 5).reshape(512, 384)
    d_part = down.reshape(16, 2, 32, 512).transpose(0, 2, 1, 3).reshape(512, 1024)
    return jnp.concatenate([q, k, v, o_part], axis=1), jnp.concatenate([gate, up, d_part], axis=1)


def from_packed(attn, ffn):
    q, k, v = (attn[:, at * 384:at * 384 + 384] for at in range(3))
    o = attn[:, 1152:1536].reshape(8, 2, 2, 16, 3, 128).transpose(0, 4, 3, 1, 2, 5).reshape(384, 512)
    down = ffn[:, 2048:].reshape(16, 32, 2, 512).transpose(0, 2, 1, 3).reshape(1024, 512)
    return q, k, v, o, ffn[:, :1024], ffn[:, 1024:2048], down


def parts_of(whole):
    split = whole.reshape(4, 2, 2, 32, whole.shape[1])
    return tuple(split[:, y, core] for core in range(2) for y in range(2))


def whole_of(parts):
    split = jnp.stack(parts).reshape(2, 2, 4, 32, -1).transpose(2, 1, 0, 3, 4)
    return split.reshape(512, -1)


def gains_of(column, other, y):
    small = [part[:, :2, 1536:1664].reshape(4, 2, 2, 64) for part in (column, other)]
    pair = [jnp.where(y == at, small[0], small[1]) for at in range(2)]
    return jnp.stack(pair, axis=3).transpose(1, 2, 0, 3, 4).reshape(2, 2, 512).astype(f32)


def body(inputs, cotangent, segments, observed, q_weight, k_weight, v_weight, o_weight,
         gate_weight, up_weight, down_weight, gains, position_table):
    section = lax.axis_index("section")
    dp = lax.axis_index("dp")
    micro_count, row_count, seq_count, width = inputs.shape
    layers = q_weight.shape[0]
    heads = position_table.shape[1]
    tokens = row_count * seq_count
    shards = (q_weight, k_weight, v_weight, o_weight, gate_weight, up_weight, down_weight)
    eight = lax.axis_size("dp") == 8
    own_ids = jnp.stack([dp // 2, dp % 2, section % 2, section]).astype(jnp.int32)
    ids = own_ids if eight else jnp.stack([0 * dp, 0 * dp, 0 * dp, section]).astype(jnp.int32)

    weights = [None] * 4
    if eight:
        pieces = pack_weights(own_ids, *shards, gains.astype(f32))
    else:
        whole = [lax.all_gather(w, "dp", axis=1, tiled=True) for w in shards]
        for layer in range(layers):
            weights[2 * layer], weights[2 * layer + 1] = (
                parts_of(w) for w in to_packed(*(w[layer] for w in whole)))
        gains_all = lax.all_gather(gains, "dp", axis=2, tiled=True).astype(f32)

    x = inputs.reshape(micro_count, tokens, width)
    grad = cotangent.reshape(micro_count, tokens, width)
    seg = lax.dynamic_index_in_dim(segments, section, 0, keepdims=False)
    obs = lax.dynamic_index_in_dim(observed, section, 0, keepdims=False)
    allowed = (seg[:, :, None] == seg[:, None, :]) & (obs[:, :, None] == 1)
    mask = jnp.where(allowed, 0.0, masked).astype(f32)
    mask = jnp.concatenate([mask, mask], axis=2)
    position = jnp.arange(seq_count, dtype=jnp.int32)
    bucket = bucket_of(position[:, None], position[None, :])
    onehot = (bucket[:, :, None] == jnp.arange(position_table.shape[0])[None, None, :]).astype(f32)
    bias = jnp.einsum("jib,bh->jhi", onehot, position_table.astype(f32), precision=lax.Precision.HIGHEST)
    bias = bias.reshape(seq_count, heads * seq_count)

    chip = section // 2

    def across(value, pairs):
        return lax.ppermute(value, "section", pairs)

    arrived = [()] * 4
    if eight:
        previous = None
        for s in range(4):
            weights[s], previous = gather_part(pieces[s], dp // 2, previous)
            arrived[s] = previous
            if s == 1:
                previous = previous + [weights[0][1]]
            if s == 1:
                previous = previous + [weights[0][1]]
            if s == 1:
                previous = previous + [weights[0][1]]
        gains_all = gains_of(*weights[0], dp % 2)

    chip = section // 2

    def both_ways(first, second):
        return swapped(jnp.where(chip == 0, first, second), "section", 2)

    def wait(value, *names):
        others = [steps[s][name] for s, name in names] if eight else []
        return after(value, *others) if others else value

    states, kept = [x], []
    packed, steps = [None] * 4, [None] * 4
    outs, grads, out_far, grad_far = [None] * 4, [None] * 4, [None] * 4, [None] * 4
    for s in range(4):
        gain = gains_all[s // 2, s % 2][None]
        feed = after(states[s], *arrived[s + 1]) if s < 3 else states[s]
        if eight:
            weights[s] = gather_core(*weights[s], states[s] if s > 0 else None)
        if s == 3:
            outs[3], last_back, *last_parts = ffn_both(ids, feed, grad, gain, weights[3])
            break
        if s % 2 == 0:
            out, *saved = attn_fwd(ids, feed, mask, bias, gain, weights[s])
        else:
            out, *saved = ffn_fwd(ids, feed, gain, weights[s])
        states.append(out)
        kept.append(saved)
        outs[s] = out
    out_far[0] = out_far[2] = both_ways(outs[2], outs[0])

    def back_part(s, grad):
        if s == 3:
            parts = last_parts
            back, total = last_back, bias_sum
        elif s == 1:
            back, *parts = ffn_bwd(ids, states[1], *kept[1], grad, gains_all[0, 1][None], weights[1])
            total = bias_sum
        else:
            back, *parts, total = attn_bwd(
                ids, states[s], *kept[s], grad, gains_all[s // 2, 0][None], weights[s], bias_sum,
                eight and s == 0)
        if eight:
            steps[s] = reduce_first(*parts)
        else:
            packed[s] = whole_of(parts)
        return back, total

    def front_part(s, back, grad):
        grads[s] = input_grad(ids, states[s], back, grad, gains_all[s // 2, s % 2][None], weights[s])
        return grads[s]

    bias_sum = jnp.zeros((seq_count, heads * seq_count), f32)
    back, bias_sum = back_part(3, grad)
    grad = front_part(3, back, grad)
    out_far[1] = grad_far[3] = both_ways(grad, outs[1])
    back, bias_sum = back_part(2, after(wait(grad, (3, "first")), out_far[0]))
    grad = front_part(2, back, grad)
    back, bias_sum = back_part(1, wait(grad, (2, "first"), (3, "y")))
    if eight:
        steps[3]["near"] = reduce_near(steps[3])
    grad = front_part(1, back, after(wait(grad, (2, "y")), out_far[1]))
    out_far[3] = grad_far[1] = both_ways(outs[3], grad)
    back, bias_sum = back_part(0, wait(grad, (1, "first"), (3, "near")))
    grad = front_part(0, back, wait(grad, (2, "far"), (1, "y")))
    grad_far[0] = grad_far[2] = both_ways(grads[2], grad)
    if eight:
        steps[2]["far"] = after(steps[2]["far"], grad)
        for s in (2, 1, 0):
            if s == 1:
                steps[1]["far"] = after(steps[1]["far"], grad_far[1])
            steps[s]["near"] = reduce_near(steps[s])
    out_relay = relay(ids, outs, out_far[:3] + [after(out_far[3], grads[0])])

    shape = (1, micro_count, row_count, seq_count, width)
    section_outputs = place(ids, outs, out_relay, out_far, []).reshape(shape)
    grad_relay = relay(ids, grads, grad_far)
    section_grads = place(ids, grads, grad_relay, grad_far, []).reshape(shape)

    if eight:
        own = []
        for pair in ((3, 2), (1, 0)):
            both = jnp.concatenate([reduce_last(steps[s]) for s in pair], axis=1)
            own.append(added(both, swapped(both, "section", 2)))
        own = after(jnp.concatenate(own, axis=1), section_outputs, section_grads)
        shapes = [w.shape for w in shards] + [gains.shape, position_table.shape[::-1]]
        *final, table = unpack_grads(
            ids, own, swapped(own, "section", 1), shards, gains.astype(f32), shapes)
        return (section_outputs, section_grads) + tuple(final) + (table.T,)

    dense = [from_packed(packed[2 * layer], packed[2 * layer + 1]) for layer in range(layers)]
    final = []
    for at in range(7):
        both = jnp.stack([d[at] for d in dense])
        part = lax.psum_scatter(both, "dp", scatter_dimension=1, tiled=True)
        final.append(lax.psum(part, "section").astype(f32))
    terms = [w.astype(f32) * final[at] for at, w in enumerate(shards)]
    gain_sums = [sum(jnp.sum(terms[at], axis=2) for at in group) for group in ((0, 1, 2), (4, 5))]
    gains_grad = jnp.stack(gain_sums, axis=1) / gains.astype(f32)
    bias_sum = bias_sum.reshape(seq_count, heads, seq_count)
    table = jnp.einsum("jib,jhi->bh", onehot, bias_sum, precision=lax.Precision.HIGHEST)
    return (section_outputs, section_grads) + tuple(final) + (gains_grad, lax.psum(table, ("section", "dp")))


def solution(mesh):
    rows4 = P(None, "dp", None, None)
    rows3 = P(None, "dp", None)
    staged = P("section", None, "dp", None, None)
    return jax.shard_map(
        body,
        mesh=mesh,
        in_specs=(rows4, rows4) + (rows3,) * 9 + (P(None, None, "dp"), P()),
        out_specs=(staged, staged) + (rows3,) * 7 + (P(None, None, "dp"), P()),
        check_vma=False,
    )
```

```python
import jax
import jax.numpy as jnp
from jax import lax
from jax.experimental import pallas as pl
from jax.experimental.pallas import tpu as pltpu
from jax.sharding import PartitionSpec as P

eps_norm = 1e-06
limits = (12, 16, 23, 32, 46, 64, 91)
masked = -1e30
bf = jnp.bfloat16
f32 = jnp.float32
vmem_mib = dict(
    attn_fwd=56, ffn_fwd=40, ffn_both=42, ffn_bwd=30, attn_bwd=22,
    input_grad=12, pack_weights=56, finish=20, place=9, relay=6)


def dot_nn(a, b):
    return lax.dot_general(a, b, (((1,), (0,)), ((), ())), preferred_element_type=f32)


def dot_nt(a, b):
    return lax.dot_general(a, b, (((1,), (1,)), ((), ())), preferred_element_type=f32)


def dot_tn(a, b):
    return lax.dot_general(a, b, (((0,), (0,)), ((), ())), preferred_element_type=f32)


def row_scale(x):
    return lax.rsqrt(jnp.mean(x * x, axis=-1, keepdims=True) + eps_norm)


def pair_parts(values):
    lane = lax.broadcasted_iota(jnp.int32, values.shape, 1)
    zero = jnp.zeros_like(values)
    return jnp.concatenate(
        [jnp.where(lane < 64, values, zero), jnp.where(lane < 64, zero, values)], axis=0
    )


def pair_pick(values):
    half = values.shape[0] // 2
    lane = lax.broadcasted_iota(jnp.int32, (half, values.shape[1]), 1)
    return jnp.where(lane < 64, values[:half], values[half:])


blocks = 16
block_rows = 32


def order_of(ids, z, other_y, other_core):
    return (z * 2 + (ids[1] ^ other_y)) * 2 + (ids[2] ^ other_core)


def open_attn(ids, parts, wqkv, wo):
    for at, ref in enumerate(parts):
        other_y, other_core = at % 2, at // 2
        for z in range(4):
            place = order_of(ids, z, other_y, other_core)
            if wqkv is not None:
                wqkv[pl.ds(pl.multiple_of(place * 32, 32), 32), :] = ref[z, :, :1152]
            shard = z * 2 + (ids[1] ^ other_y)
            core = ids[2] ^ other_core
            for i in range(3):
                rows = pl.ds(pl.multiple_of(shard * 48 + i * 16, 16), 16)
                for j in range(2):
                    columns = pl.ds(pl.multiple_of(core * 256 + j * 128, 128), 128)
                    wo[rows, columns] = ref[z, j * 16:j * 16 + 16, 1152 + i * 128:1280 + i * 128]


def open_ffn(ids, parts, wgu, wd):
    for at, ref in enumerate(parts):
        other_y, other_core = at % 2, at // 2
        for z in range(4):
            place = order_of(ids, z, other_y, other_core)
            if wgu is not None:
                wgu[pl.ds(pl.multiple_of(place * 32, 32), 32), :] = ref[z, :, :2048]
            for i in range(2):
                wd[pl.ds(pl.multiple_of(place * 64 + i * 32, 32), 32), :] = (
                    ref[z, :, 2048 + i * 512:2560 + i * 512])


def hand_out(ids, packed, refs):
    for at, ref in enumerate(refs):
        for by in range(4):
            place = order_of(ids, ids[0] ^ by, at % 2, at // 2)
            ref[by] = packed[pl.ds(pl.multiple_of(place * 32, 32), 32), :]


def attn_fwd_kernel(ids, x_ref, mask_ref, bias_ref, gain_ref, w0, w1, w2, w3,
                    out_ref, q_ref, k_ref, v_ref, p_ref, att_ref, wqkv, wo):
    @pl.when(pl.program_id(0) == 0)
    def _():
        open_attn(ids, (w0, w1, w2, w3), wqkv, wo)

    x = x_ref[...].astype(f32)
    a = (x * row_scale(x) * gain_ref[...]).astype(bf)
    q = dot_nn(a, wqkv[:, :384]).astype(bf)
    k = dot_nn(a, wqkv[:, 384:768]).astype(bf)
    v = dot_nn(a, wqkv[:, 768:]).astype(bf)
    q_ref[...] = q
    k_ref[...] = k
    v_ref[...] = v
    rows = x.shape[0] // 64
    units = [(r, h) for r in range(rows) for h in range(3)]
    at = lambda arr, r, h: arr[r * 64:r * 64 + 64, h * 128:h * 128 + 128]
    scores = [dot_nt(at(k, r, h), pair_parts(at(q, r, h))) for r, h in units]
    probs = []
    for (r, h), s in zip(units, scores):
        s = s + (bias_ref[:, h * 128:h * 128 + 128] + mask_ref[r])
        e = jnp.exp(s - jnp.max(s, axis=0, keepdims=True))
        p = (e * (1.0 / jnp.sum(e, axis=0, keepdims=True))).astype(bf)
        p_ref[r * 64:r * 64 + 64, h * 128:h * 128 + 128] = p
        probs.append(p)
    full_att = [dot_tn(p, at(v, r, h)) for (r, h), p in zip(units, probs)]
    att = {unit: pair_pick(part).astype(bf) for unit, part in zip(units, full_att)}
    att = jnp.concatenate(
        [jnp.concatenate([att[r, h] for h in range(3)], axis=1) for r in range(rows)], axis=0)
    att_ref[...] = att
    out_ref[...] = (x + dot_nn(att, wo[...])).astype(bf)


def normed(x_ref, gain_ref):
    x = x_ref[...].astype(f32)
    return (x * row_scale(x) * gain_ref[...]).astype(bf)


def norm_back(x_ref, gain_ref, gx, g_low):
    x = x_ref[...].astype(f32)
    scale = row_scale(x)
    n = x * scale
    e = gx * gain_ref[...]
    dx = scale * (e - n * jnp.mean(e * n, axis=-1, keepdims=True))
    return (g_low.astype(f32) + dx).astype(bf), (n * gain_ref[...]).astype(bf)


def input_grad_kernel(ids, x_ref, back_ref, g_ref, gain_ref, w0, w1, w2, w3, gin_ref, w_s):
    width = back_ref.shape[1]

    @pl.when(pl.program_id(0) == 0)
    def _():
        for at, ref in enumerate((w0, w1, w2, w3)):
            for z in range(4):
                place = order_of(ids, z, at % 2, at // 2)
                w_s[pl.ds(pl.multiple_of(place * 32, 32), 32), :] = ref[z, :, :width]

    gin_ref[...] = norm_back(x_ref, gain_ref, dot_nt(back_ref[...], w_s[...]), g_ref[...])[0]


def bucket_of(key, query):
    offset = key - query
    distance = jnp.abs(offset)
    far = jnp.full(distance.shape, 8, jnp.int32)
    for threshold in limits:
        far = far + (distance >= threshold).astype(jnp.int32)
    near = jnp.where(distance < 8, distance, jnp.minimum(far, 15))
    return near + 16 * (offset > 0).astype(jnp.int32)


def table_terms(bias_grad):
    key = lax.broadcasted_iota(jnp.int32, (64, 128), 0)
    query = lax.broadcasted_iota(jnp.int32, (64, 128), 1) & 63
    bucket = bucket_of(key, query)
    pieces = [bias_grad[:, h * 128:h * 128 + 128] for h in range(3)]
    sums = [[], [], []]
    for b in range(32):
        hit = bucket == b
        for h in range(3):
            sums[h].append(jnp.sum(jnp.where(hit, pieces[h], 0.0), axis=0, keepdims=True))
    lane = lax.broadcasted_iota(jnp.int32, (32, 128), 1)
    table = jnp.zeros((32, 128), f32)
    for h in range(3):
        part = jnp.concatenate(sums[h], axis=0)
        low = jnp.sum(jnp.where(lane < 64, part, 0.0), axis=1, keepdims=True)
        high = jnp.sum(jnp.where(lane < 64, 0.0, part), axis=1, keepdims=True)
        table = jnp.where(lane == 2 * h, low, jnp.where(lane == 2 * h + 1, high, table))
    return table


def attn_bwd_kernel(ids, x_ref, q_ref, k_ref, v_ref, p_ref, att_ref, g_ref, gain_ref, w0, w1, w2, w3,
                    bias_in, back_ref, r0, r1, r2, r3, dbias_ref,
                    wo, a_s, dqkv_s, att_s, g_s, dbias_s, packed):
    step = pl.program_id(0)
    last = pl.num_programs(0) - 1
    block = x_ref.shape[0]
    with_table = r0.shape[2] > 1536

    @pl.when(step == 0)
    def _():
        open_attn(ids, (w0, w1, w2, w3), None, wo)
        dbias_s[...] = bias_in[...]

    here = pl.ds(pl.multiple_of(step * block, block), block)
    g_low = g_ref[...]
    da = dot_nt(g_low, wo[...]).astype(bf)
    att_s[here, :] = att_ref[...]
    g_s[here, :] = g_low
    rows = block // 64
    units = [(r, h) for r in range(rows) for h in range(3)]
    at = lambda arr, r, h: arr[r * 64:r * 64 + 64, h * 128:h * 128 + 128]
    db = [None] * 3
    da_bds = [pair_parts(at(da, r, h)) for r, h in units]
    dps = [dot_nt(at(v_ref, r, h), da_bd) for (r, h), da_bd in zip(units, da_bds)]
    dv_u = {(r, h): dot_nn(at(p_ref, r, h), da_bd).astype(bf) for (r, h), da_bd in zip(units, da_bds)}
    dss = []
    for (r, h), dp in zip(units, dps):
        pf = at(p_ref, r, h).astype(f32)
        ds = pf * (dp - jnp.sum(pf * dp, axis=0, keepdims=True))
        db[h] = ds if db[h] is None else db[h] + ds
        dss.append(ds.astype(bf))
    dk_u = {(r, h): dot_nn(ds, pair_parts(at(q_ref, r, h))).astype(bf) for (r, h), ds in zip(units, dss)}
    full_dq = [dot_tn(ds, at(k_ref, r, h)) for (r, h), ds in zip(units, dss)]
    dq_u = {unit: pair_pick(part).astype(bf) for unit, part in zip(units, full_dq)}
    dqkv = jnp.concatenate(
        [jnp.concatenate([u[r, h] for u in (dq_u, dk_u, dv_u) for h in range(3)], axis=1)
         for r in range(rows)], axis=0)
    dqkv_s[here, :] = dqkv
    for h in range(3):
        dbias_s[:, h * 128:h * 128 + 128] += db[h]
    back_ref[...] = dqkv
    a_s[here, :] = normed(x_ref, gain_ref)

    @pl.when(step == last)
    def _():
        for h in range(3):
            columns = slice(h * 384, h * 384 + 384)
            packed[:, columns] = dot_tn(a_s[...], dqkv_s[:, columns]).astype(bf)
        dwo = dot_tn(att_s[...], g_s[...]).astype(bf)
        for shard in range(8):
            for core in range(2):
                for i in range(3):
                    for j in range(2):
                        packed[(shard * 2 + core) * 32 + j * 16:(shard * 2 + core) * 32 + j * 16 + 16,
                               1152 + i * 128:1280 + i * 128] = (
                            dwo[shard * 48 + i * 16:shard * 48 + i * 16 + 16,
                                core * 256 + j * 128:core * 256 + j * 128 + 128])
        dbias_ref[...] = dbias_s[...]
        if with_table:
            table = table_terms(dbias_s[...]).astype(bf)
            for at in range(16):
                packed[at * 32:at * 32 + 32, 1536:1664] = table
        hand_out(ids, packed, (r0, r1, r2, r3))


def gelu_parts(u):
    c = 0.7978845608028654
    u2 = u * u
    t = jnp.tanh(u * (c + (c * 0.044715) * u2))
    half = 0.5 + 0.5 * t
    act = u * half
    slope = half + (0.5 * u) * (1.0 - t * t) * (c + (3.0 * c * 0.044715) * u2)
    return act, slope


def gelu(u):
    c = 0.7978845608028654
    t = jnp.tanh(u * (c + (c * 0.044715) * (u * u)))
    return u * (0.5 + 0.5 * t)


def ffn_fwd_kernel(ids, x_ref, gain_ref, w0, w1, w2, w3, out_ref, gate_ref, up_ref, wgu, wd):
    @pl.when(pl.program_id(0) == 0)
    def _():
        open_ffn(ids, (w0, w1, w2, w3), wgu, wd)

    x = x_ref[...].astype(f32)
    a = (x * row_scale(x) * gain_ref[...]).astype(bf)
    gate = dot_nn(a, wgu[:, :1024])
    up = dot_nn(a, wgu[:, 1024:])
    gate_ref[...] = gate.astype(bf)
    up_ref[...] = up.astype(bf)
    hidden = (gelu(gate) * up).astype(bf)
    out_ref[...] = (x + dot_nn(hidden, wd[...])).astype(bf)


def ffn_weight_grads(ids, a_s, gub_s, hid_s, g_s, packed, refs):
    for h in range(4):
        columns = slice(h * 512, h * 512 + 512)
        packed[:, columns] = dot_tn(a_s[...], gub_s[:, columns]).astype(bf)
    for h in range(2):
        dwd = dot_tn(hid_s[:, h * 512:h * 512 + 512], g_s[...]).astype(bf)
        for at in range(8):
            for i in range(2):
                packed[(h * 8 + at) * 32:(h * 8 + at) * 32 + 32, 2048 + i * 512:2560 + i * 512] = (
                    dwd[at * 64 + i * 32:at * 64 + i * 32 + 32])
    hand_out(ids, packed, refs)


def ffn_bwd_kernel(ids, x_ref, gate_ref, up_ref, g_ref, gain_ref, w0, w1, w2, w3,
                   gin_ref, r0, r1, r2, r3, wgu, wd, a_s, gub_s, hid_s, g_s, packed):
    step = pl.program_id(0)
    block = x_ref.shape[0]

    @pl.when(step == 0)
    def _():
        open_ffn(ids, (w0, w1, w2, w3), wgu, wd)

    here = pl.ds(pl.multiple_of(step * block, block), block)
    g_low = g_ref[...]
    g_s[here, :] = g_low
    hg = dot_nt(g_low, wd[...])
    gate = gate_ref[...].astype(f32)
    up = up_ref[...].astype(f32)
    act, slope = gelu_parts(gate)
    hid_s[here, :] = (act * up).astype(bf)
    gb = (hg * up * slope).astype(bf)
    ub = (hg * act).astype(bf)
    gub_s[here, :1024] = gb
    gub_s[here, 1024:] = ub
    gx = dot_nt(gb, wgu[:, :1024]) + dot_nt(ub, wgu[:, 1024:])
    gin_ref[...], a_s[here, :] = norm_back(x_ref, gain_ref, gx, g_low)

    @pl.when(step == pl.num_programs(0) - 1)
    def _():
        ffn_weight_grads(ids, a_s, gub_s, hid_s, g_s, packed, (r0, r1, r2, r3))


def ffn_both_kernel(ids, x_ref, g_ref, gain_ref, w0, w1, w2, w3,
                    out_ref, back_ref, r0, r1, r2, r3, wgu, wd, a_s, gub_s, hid_s, g_s, packed):
    step = pl.program_id(0)
    block = x_ref.shape[0]

    @pl.when(step == 0)
    def _():
        open_ffn(ids, (w0, w1, w2, w3), wgu, wd)

    here = pl.ds(pl.multiple_of(step * block, block), block)
    x = x_ref[...].astype(f32)
    a = (x * row_scale(x) * gain_ref[...]).astype(bf)
    gate = dot_nn(a, wgu[:, :1024])
    up = dot_nn(a, wgu[:, 1024:])
    g_low = g_ref[...]
    g_s[here, :] = g_low
    hg = dot_nt(g_low, wd[...])
    act, slope = gelu_parts(gate)
    hidden = (act * up).astype(bf)
    hid_s[here, :] = hidden
    out_ref[...] = (x + dot_nn(hidden, wd[...])).astype(bf)
    gb = (hg * up * slope).astype(bf)
    ub = (hg * act).astype(bf)
    gub_s[here, :1024] = gb
    gub_s[here, 1024:] = ub
    back_ref[:, :1024] = gb
    back_ref[:, 1024:] = ub
    a_s[here, :] = a

    @pl.when(step == pl.num_programs(0) - 1)
    def _():
        ffn_weight_grads(ids, a_s, gub_s, hid_s, g_s, packed, (r0, r1, r2, r3))


def tok(block, width):
    return pl.BlockSpec((block, width), lambda i, ids: (i, 0))


def picked(block, width):
    return pl.BlockSpec((None, block, width), lambda i, ids: (ids[3], i, 0))


def tokens_of(array, block):
    return (tok if array.ndim == 2 else picked)(block, array.shape[-1])


def full(shape):
    zero = (0,) * len(shape)
    return pl.BlockSpec(shape, lambda i, ids: zero)


def sds(shape, dtype):
    return jax.ShapeDtypeStruct(shape, dtype)


def call(kernel, grid, in_specs, out_specs, out_shape, scratch, micros, name):
    return pl.pallas_call(
        kernel,
        grid_spec=pltpu.PrefetchScalarGridSpec(
            num_scalar_prefetch=1, grid=(grid,), in_specs=in_specs, out_specs=out_specs,
            scratch_shapes=scratch),
        out_shape=out_shape, name=name,
        compiler_params=pltpu.CompilerParams(vmem_limit_bytes=vmem_mib[name] << 20),
        cost_estimate=pl.CostEstimate(flops=int(micros * 1.1e9), bytes_accessed=0, transcendentals=0),
    )


token_block = 512


def attn_fwd(ids, x, mask, bias, gain, parts):
    t, d = x.shape[-2:]
    block = token_block
    return call(
        attn_fwd_kernel, t // block,
        [tokens_of(x, block), pl.BlockSpec((block // 64, 64, 128), lambda i, ids: (i, 0, 0)),
         full(bias.shape), full((1, d))] + [full(parts[0].shape)] * 4,
        [tok(block, d)] + [tok(block, 384)] * 5,
        [sds((t, d), bf)] + [sds((t, 384), bf)] * 5,
        [pltpu.VMEM((512, 1152), bf), pltpu.VMEM((384, 512), bf)],
        15, "attn_fwd")(ids, x, mask, bias, gain, *parts)


def attn_bwd(ids, x, q, k, v, p, att, g, gain, parts, bias_in, with_table):
    t, d = x.shape[-2:]
    block = token_block
    n = 1664 if with_table else 1536
    packed = (4, 32, n)
    return call(
        attn_bwd_kernel, t // block,
        [tokens_of(x, block)] + [tok(block, 384)] * 5 + [tok(block, d), full((1, d))]
        + [full(parts[0].shape)] * 4 + [full(bias_in.shape)],
        [tok(block, 1152)] + [full(packed)] * 4 + [full((64, 384))],
        [sds((t, 1152), bf)] + [sds(packed, bf)] * 4 + [sds((64, 384), f32)],
        [pltpu.VMEM((384, 512), bf), pltpu.VMEM((t, d), bf),
         pltpu.VMEM((t, 1152), bf), pltpu.VMEM((t, 384), bf), pltpu.VMEM((t, d), bf),
         pltpu.VMEM((64, 384), f32), pltpu.VMEM((512, n), bf)],
        9, "attn_bwd")(ids, x, q, k, v, p, att, g, gain, *parts, bias_in)


def input_grad(ids, x, back, g, gain, parts, micros):
    t, d = x.shape[-2:]
    block = token_block
    width = back.shape[1]
    rows, columns = parts[0].shape[1:]
    part = pl.BlockSpec((4, rows, width if width % 128 == 0 and columns != width else columns),
                        lambda i, ids: (0, 0, 0))
    return call(
        input_grad_kernel, t // block,
        [tokens_of(x, block), tok(block, width), tokens_of(g, block), full((1, d))] + [part] * 4,
        [tok(block, d)], [sds((t, d), bf)], [pltpu.VMEM((512, width), bf)],
        micros, "input_grad")(ids, x, back, g, gain, *parts)[0]


def ffn_fwd(ids, x, gain, parts):
    t, d = x.shape
    block = token_block
    return call(
        ffn_fwd_kernel, t // block,
        [tok(block, d), full((1, d))] + [full(parts[0].shape)] * 4,
        [tok(block, d), tok(block, 1024), tok(block, 1024)],
        [sds((t, d), bf), sds((t, 1024), bf), sds((t, 1024), bf)],
        [pltpu.VMEM((512, 2048), bf), pltpu.VMEM((1024, 512), bf)],
        0.3, "ffn_fwd")(ids, x, gain, *parts)


def ffn_scratch(t, d):
    return [pltpu.VMEM((1024, 512), bf), pltpu.VMEM((t, d), bf),
            pltpu.VMEM((t, 2048), bf), pltpu.VMEM((t, 1024), bf), pltpu.VMEM((t, d), bf),
            pltpu.VMEM((512, 3072), bf)]


def ffn_bwd(ids, x, gate, up, g, gain, parts):
    t, d = x.shape
    block = token_block
    packed = (4, 32, 3072)
    return call(
        ffn_bwd_kernel, t // block,
        [tok(block, d), tok(block, 1024), tok(block, 1024), tok(block, d), full((1, d))]
        + [full(parts[0].shape)] * 4,
        [tok(block, d)] + [full(packed)] * 4,
        [sds((t, d), bf)] + [sds(packed, bf)] * 4,
        [pltpu.VMEM((512, 2048), bf)] + ffn_scratch(t, d), 12, "ffn_bwd")(ids, x, gate, up, g, gain, *parts)


def ffn_both(ids, x, g, gain, parts):
    t, d = x.shape
    block = token_block
    packed = (4, 32, 3072)
    return call(
        ffn_both_kernel, t // block,
        [tok(block, d), tokens_of(g, block), full((1, d))] + [full(parts[0].shape)] * 4,
        [tok(block, d), tok(block, 2048)] + [full(packed)] * 4,
        [sds((t, d), bf), sds((t, 2048), bf)] + [sds(packed, bf)] * 4,
        [pltpu.VMEM((512, 2048), bf)] + ffn_scratch(t, d), 15, "ffn_both")(ids, x, g, gain, *parts)


def pack_attn_kernel(ids, q, k, v, o, *refs):
    core = ids[2]
    rows = pl.ds(pl.multiple_of(core * 32, 32), 32)
    out = refs[-1]
    layer = 1
    if len(refs) == 2:
        layer, gains = 0, refs[0]
        pair = [jnp.concatenate([gains[l, 0:1, :], gains[l, 1:2, :]], axis=1).astype(f32) for l in range(2)]
        row = lax.broadcasted_iota(jnp.int32, (32, 128), 0)
        out[:, 1536:] = jnp.where(row == 0, pair[0], jnp.where(row == 1, pair[1], 0.0)).astype(bf)
    for at, w in enumerate((q, k, v)):
        out[:, at * 384:at * 384 + 384] = w[layer, rows, :]
    for i in range(3):
        for j in range(2):
            columns = pl.ds(pl.multiple_of(core * 256 + j * 128, 128), 128)
            out[j * 16:j * 16 + 16, 1152 + i * 128:1280 + i * 128] = o[layer, i * 16:i * 16 + 16, columns]


def pack_ffn_kernel(ids, gate, up, down, *outs):
    core = ids[2]
    rows = pl.ds(pl.multiple_of(core * 32, 32), 32)
    for layer, out in enumerate(outs):
        out[:, :1024] = gate[layer, rows, :]
        out[:, 1024:2048] = up[layer, rows, :]
        for i in range(2):
            out[:, 2048 + i * 512:2560 + i * 512] = (
                down[layer, pl.ds(pl.multiple_of(core * 64 + i * 32, 32), 32), :])


def pack_weights(ids, shards, gains):
    attn, ffn = shards[:4], shards[4:]
    specs = [full(w.shape) for w in attn]
    first = call(pack_attn_kernel, 1, specs + [full(gains.shape)], [full((32, 1664))],
                 [sds((32, 1664), bf)], [], 2, "pack_weights")(ids, *attn, gains)[0]
    third = call(pack_attn_kernel, 1, specs, [full((32, 1536))],
                 [sds((32, 1536), bf)], [], 2, "pack_weights")(ids, *attn)[0]
    second, fourth = call(pack_ffn_kernel, 1, [full(w.shape) for w in ffn], [full((32, 3072))] * 2,
                          [sds((32, 3072), bf)] * 2, [], 2, "pack_weights")(ids, *ffn)
    return first, second, third, fourth


def finish_kernel(ids, own, peer, qw, kw, vw, gw, uw, gain, *refs):
    with_moves = len(refs) > 9
    if with_moves:
        moved, refs, moving_refs = refs[:9], refs[9:18], refs[18:]
        arrive, pass_on, leave = place_moves(ids, moved, *moving_refs)
        arrive()
    q, k, v, o, gate, up, down, gains, table = refs
    first = ids[2] == 0
    base = 0

    def row_sums(*pairs):
        total = None
        for weight, grad in pairs:
            term = weight.astype(f32) * grad
            total = term if total is None else total + term
        ones = jnp.ones((8, total.shape[1]), f32)
        sums = lax.dot_general(ones, total, (((1,), (1,)), ((), ())), preferred_element_type=f32,
                               precision=lax.Precision.HIGHEST)
        return sums[0:1, :]

    for s in (3, 2, 1, 0):
        layer = s // 2
        for core in range(2):
            def part(start, width, rows=slice(0, 32)):
                columns = slice(base + start, base + start + width)
                one, two = own[rows, columns].astype(f32), peer[rows, columns].astype(f32)
                return jnp.where(first, one, two) if core == 0 else jnp.where(first, two, one)

            rows = slice(core * 32, core * 32 + 32)
            if s % 2 == 0:
                for at, w in enumerate((q, k, v)):
                    w[layer, rows, :] = part(at * 384, 384)
                for i in range(3):
                    for j in range(2):
                        o[layer, i * 16:i * 16 + 16, core * 256 + j * 128:core * 256 + j * 128 + 128] = (
                            part(1152 + i * 128, 128, slice(j * 16, j * 16 + 16)))
            else:
                gate[layer, rows, :] = part(0, 1024)
                up[layer, rows, :] = part(1024, 1024)
                for i in range(2):
                    down[layer, core * 64 + i * 32:core * 64 + i * 32 + 32, :] = part(2048 + i * 512, 512)
            if s == 0 and core == 1:
                table[...] = part(1536, 128).T[:6, :]
        if s % 2 == 0:
            sums = row_sums(*((w[layer], grad[layer]) for w, grad in ((qw, q), (kw, k), (vw, v))))
        else:
            sums = row_sums(*((w[layer], grad[layer]) for w, grad in ((gw, gate), (uw, up))))
        gains[layer, s % 2:s % 2 + 1, :] = sums / gain[layer, s % 2:s % 2 + 1, :].astype(f32)
        base += 1536 if s % 2 == 0 else 3072
        if s == 3 and with_moves:
            pass_on()
    if with_moves:
        leave()


def finish(ids, own, peer, shards, gains, shapes, moved=()):
    q, k, v, o, gate, up, down = shards
    args = (own, peer, q, k, v, gate, up, gains)
    anywhere = pl.BlockSpec(memory_space=pl.ANY)
    specs, sizes = [full(array.shape) for array in args], [sds(shape, f32) for shape in shapes]
    out_specs, scratch = [full(shape) for shape in shapes], []
    if moved:
        t, d = moved[0].shape
        specs += [anywhere] * len(moved)
        out_specs.append(anywhere)
        sizes.append(sds((4, t, d), bf))
        scratch = [pltpu.VMEM((4, t, d), bf), pltpu.SemaphoreType.DMA((2, 4))]
    return call(finish_kernel, 1, specs, out_specs, sizes, scratch, 3, "finish")(ids, *args, *moved)


def move(sources, scratch, targets, sems):
    def fetch(ref, at):
        return pltpu.make_async_copy(ref, scratch.at[at], sems.at[0, at])

    def store(at):
        return pltpu.make_async_copy(scratch.at[at], targets[at], sems.at[1, at])

    def arrive():
        for at, options in enumerate(sources):
            for condition, ref in options:
                if condition is None:
                    fetch(ref, at).start()
                else:
                    @pl.when(condition)
                    def _(ref=ref, at=at):
                        fetch(ref, at).start()

    def pass_on():
        for at in range(len(targets)):
            fetch(sources[at][0][1], at).wait()
            store(at).start()

    def leave():
        for at in range(len(targets)):
            store(at).wait()

    return arrive, pass_on, leave


def place_moves(ids, refs, out, scratch, sems):
    own, relay, far = refs[:4], refs[4], refs[5:]
    section = ids[3]
    pick = lambda group: [(section == at, ref) for at, ref in enumerate(group)]
    return move([pick(own), [(None, relay.at[0])], pick(far), [(None, relay.at[1])]], scratch,
                [out.at[section ^ bit] for bit in range(4)], sems)


def place_kernel(ids, *refs):
    for part in place_moves(ids, refs[:9], *refs[9:]):
        part()


def moving(kernel, ids, arrays, out_shape, slots, micros, name):
    anywhere = pl.BlockSpec(memory_space=pl.ANY)
    t, d = arrays[0].shape[-2:]
    return pl.pallas_call(
        kernel,
        grid_spec=pltpu.PrefetchScalarGridSpec(
            num_scalar_prefetch=1, grid=(1,), in_specs=[anywhere] * len(arrays), out_specs=anywhere,
            scratch_shapes=[pltpu.VMEM((slots, t, d), bf), pltpu.SemaphoreType.DMA((2, slots))]),
        out_shape=out_shape, name=name,
        compiler_params=pltpu.CompilerParams(vmem_limit_bytes=vmem_mib[name] << 20),
        cost_estimate=pl.CostEstimate(flops=int(micros * 1.1e9), bytes_accessed=0, transcendentals=0),
    )(ids, *arrays)


def place(ids, own, relay, far):
    return moving(place_kernel, ids, (*own, relay, *far), sds((4,) + own[0].shape, bf), 4, 3, "place")


def relay_kernel(ids, *refs):
    own, far = refs[:4], refs[4:8]
    out, scratch, sems = refs[8:]
    pick = lambda group: [((ids[3] ^ 1) == at, ref) for at, ref in enumerate(group)]
    for part in move([pick(own), pick(far)], scratch, [out.at[0], out.at[1]], sems):
        part()


def relay(ids, own, far):
    t, d = own[0].shape
    both = moving(relay_kernel, ids, (*own, *far), sds((2, t, d), bf), 2, 2, "relay")
    return swapped(both, "section", 1)


def z_shift(values, by):
    half = lax.axis_size("dp") // 2
    pairs = [(z * 2 + y, ((z + by) % half) * 2 + y) for z in range(half) for y in range(2)]
    return lax.ppermute(values, "dp", pairs)


def swapped(values, axis, bit):
    return lax.ppermute(values, axis, [(i, i ^ bit) for i in range(lax.axis_size(axis))])


def after(values, *others):
    return lax.optimization_barrier((values,) + others)[0]


def added(*terms):
    total = terms[0].astype(f32)
    for term in terms[1:]:
        total = total + term.astype(f32)
    return total.astype(bf)


def gather_part(piece, z, previous):
    if previous is not None:
        piece = after(piece, *previous)
    got = [z_shift(piece, by) for by in range(1, 4)]
    column = jnp.stack([lax.select_n((z - at) % 4, piece, *got) for at in range(4)])
    return (column, swapped(column, "dp", 1)), got


def gather_core(column, other, *holds):
    if holds:
        column, other = lax.optimization_barrier((column, other) + holds)[:2]
    return column, other, swapped(column, "section", 1), swapped(other, "section", 1)


def reduce_first(own, other, give_own, give_other, straight, hold=None):
    first = swapped(give_other, "section", 1)
    sent = swapped(added(other, first), "dp", 1)
    got = swapped(give_own, "section", 1)
    step = dict(keep=own, first=first, core=got, y=sent)
    if straight:
        step["terms"] = [added(own[by], got[by], sent[by]) for by in range(4)]
    else:
        step["far"] = swapped(added(own[2:], got[2:], sent[2:] if hold is None else after(sent[2:], hold)), "dp", 4)
    return step


def xor_shift(values, z_bits):
    return swapped(values, "dp", 2 * z_bits)


def reduce_near(step):
    terms = (step["keep"][1], step["core"][1], step["y"][1], step["far"][1])
    return swapped(added(*terms), "dp", 2)


def reduce_last(step):
    if "terms" in step:
        return added(step["terms"][0], *step["near"])
    return added(step["keep"][0], step["core"][0], step["y"][0], step["far"][0], step["near"])


def to_packed(q, k, v, o, gate, up, down):
    o_part = o.reshape(8, 3, 16, 2, 2, 128).transpose(0, 3, 4, 2, 1, 5).reshape(512, 384)
    d_part = down.reshape(16, 2, 32, 512).transpose(0, 2, 1, 3).reshape(512, 1024)
    return jnp.concatenate([q, k, v, o_part], axis=1), jnp.concatenate([gate, up, d_part], axis=1)


def from_packed(attn, ffn):
    q, k, v = (attn[:, at * 384:at * 384 + 384] for at in range(3))
    o = attn[:, 1152:1536].reshape(8, 2, 2, 16, 3, 128).transpose(0, 4, 3, 1, 2, 5).reshape(384, 512)
    down = ffn[:, 2048:].reshape(16, 32, 2, 512).transpose(0, 2, 1, 3).reshape(1024, 512)
    return q, k, v, o, ffn[:, :1024], ffn[:, 1024:2048], down


def parts_of(whole):
    split = whole.reshape(4, 2, 2, 32, whole.shape[1])
    return tuple(split[:, y, core] for core in range(2) for y in range(2))


def whole_of(parts):
    split = jnp.stack(parts).reshape(2, 2, 4, 32, -1).transpose(2, 1, 0, 3, 4)
    return split.reshape(512, -1)


def gains_of(column, other, y):
    small = [part[:, :2, 1536:1664].reshape(4, 2, 2, 64) for part in (column, other)]
    pair = [jnp.where(y == at, small[0], small[1]) for at in range(2)]
    return jnp.stack(pair, axis=3).transpose(1, 2, 0, 3, 4).reshape(2, 2, 512).astype(f32)


def body(inputs, cotangent, segments, observed, q_weight, k_weight, v_weight, o_weight,
         gate_weight, up_weight, down_weight, gains, position_table):
    section = lax.axis_index("section")
    dp = lax.axis_index("dp")
    micro_count, row_count, seq_count, width = inputs.shape
    layers = q_weight.shape[0]
    heads = position_table.shape[1]
    tokens = row_count * seq_count
    shards = (q_weight, k_weight, v_weight, o_weight, gate_weight, up_weight, down_weight)
    eight = lax.axis_size("dp") == 8
    own_ids = jnp.stack([dp // 2, dp % 2, section % 2, section]).astype(jnp.int32)
    ids = own_ids if eight else jnp.stack([0 * dp, 0 * dp, 0 * dp, section]).astype(jnp.int32)

    weights = [None] * 4
    if eight:
        pieces = pack_weights(own_ids, shards, gains)
    else:
        whole = [lax.all_gather(w, "dp", axis=1, tiled=True) for w in shards]
        for layer in range(layers):
            weights[2 * layer], weights[2 * layer + 1] = (
                parts_of(w) for w in to_packed(*(w[layer] for w in whole)))
        gains_all = lax.all_gather(gains, "dp", axis=2, tiled=True).astype(f32)

    x = inputs.reshape(micro_count, tokens, width)
    grad = cotangent.reshape(micro_count, tokens, width)
    seg = lax.dynamic_index_in_dim(segments, section, 0, keepdims=False)
    obs = lax.dynamic_index_in_dim(observed, section, 0, keepdims=False)
    allowed = (seg[:, :, None] == seg[:, None, :]) & (obs[:, :, None] == 1)
    mask = jnp.where(allowed, 0.0, masked).astype(f32)
    mask = jnp.concatenate([mask, mask], axis=2)
    position = jnp.arange(seq_count, dtype=jnp.int32)
    bucket = bucket_of(position[:, None], position[None, :])
    onehot = (bucket[:, :, None] == jnp.arange(position_table.shape[0])[None, None, :]).astype(f32)
    bias = jnp.einsum("jib,bh->jhi", onehot, position_table.astype(f32), precision=lax.Precision.HIGHEST)
    bias = bias.reshape(seq_count, heads * seq_count)

    chip = section // 2

    def across(value, pairs):
        return lax.ppermute(value, "section", pairs)

    arrived = [()] * 4
    if eight:
        previous = None
        for s in range(4):
            weights[s], previous = gather_part(pieces[s], dp // 2, previous)
            arrived[s] = previous
            if s == 1:
                previous = previous + [weights[0][1]]
            if s == 1:
                previous = previous + [weights[0][1]]
            if s == 1:
                previous = previous + [weights[0][1]]
        gains_all = gains_of(*weights[0], dp % 2)

    chip = section // 2

    def both_ways(first, second):
        return swapped(jnp.where(chip == 0, first, second), "section", 2)

    def wait(value, *names):
        others = [steps[s][name] for s, name in names] if eight else []
        return after(value, *others) if others else value

    chip = section // 2

    def both_ways(first, second):
        return swapped(jnp.where(chip == 0, first, second), "section", 2)

    moved = {}

    def wait(value, *names):
        others = [moved[name] for name in names if name in moved]
        return after(value, *others) if others else value

    def gain_of(s):
        return gains_all[s // 2, s % 2][None]

    packed, steps = [None] * 4, [None] * 4

    def passed(s, parts):
        if eight:
            hold = [moved[name] for name in () if s == 0 and name in moved]
            steps[s] = reduce_first(*parts, s in (), *hold)
            moved.update({f"{name}{s}": steps[s][name] for name in ("first", "core", "y", "far") if name in steps[s]})
        else:
            packed[s] = whole_of(parts)

    states, kept = [x], []
    outs, grads, out_far, grad_far = [None] * 4, [None] * 4, [None] * 4, [None] * 4
    for s in range(4):
        feed = states[s]
        if eight:
            if s < 3:
                feed = after(feed, *arrived[s + 1])
            holds = [states[s]] if s in (1, 3) else []
            holds += [weights[at][1] for to, at in ((1, 2),) if to == s]
            weights[s] = gather_core(*weights[s], *holds)
        if s == 3:
            outs[3], last_back, *parts = ffn_both(ids, feed, grad, gain_of(3), weights[3])
            break
        if s % 2 == 0:
            out, *saved = attn_fwd(ids, feed, mask, bias, gain_of(s), weights[s])
        else:
            out, *saved = ffn_fwd(ids, feed, gain_of(s), weights[s])
        states.append(out)
        kept.append(saved)
        outs[s] = out
    out_far[0] = out_far[2] = moved["x1"] = both_ways(outs[2], outs[0])
    passed(3, parts)

    bias_sum = jnp.zeros((seq_count, heads * seq_count), f32)
    grads[3] = grad = input_grad(ids, states[3], last_back, grad, gain_of(3), weights[3], 20)
    out_far[1] = grad_far[3] = moved["x2"] = both_ways(grad, outs[1])
    back, *parts, bias_sum = attn_bwd(
        ids, states[2], *kept[2], wait(grad, "first3", "x1"), gain_of(2), weights[2], bias_sum, False)
    passed(2, parts)
    grads[2] = grad = input_grad(
        ids, states[2], back, grad, gain_of(2), weights[2], 20)
    grads[1], *parts = ffn_bwd(
        ids, states[1], *kept[1], wait(grad, "first2", "y3"), gain_of(1), weights[1])
    passed(1, parts)
    grad = grads[1]
    out_far[3] = grad_far[1] = moved["x3"] = both_ways(outs[3], grad)
    back, *parts, bias_sum = attn_bwd(
        ids, states[0], *kept[0], wait(grad, "first1", "y2", "x2"), gain_of(0), weights[0], bias_sum, eight)
    passed(0, parts)
    grads[0] = input_grad(
        ids, states[0], back, wait(grad, "far3", "y1", "y2"), gain_of(0), weights[0], 20)
    moved["g0"] = grads[0]
    grad_far[0] = grad_far[2] = moved["x4"] = both_ways(grads[2], wait(grads[0], "x3"))

    shape = (1, micro_count, row_count, seq_count, width)
    out_relay = relay(ids, outs, out_far[:3] + [wait(out_far[3], "g0")])
    section_outputs = moved["placed"] = place(ids, outs, out_relay, out_far)
    if eight:
        for s, names in ((3, ("g0", )), (2, ("g0", )), (1, ("x3", )), (0, ())):
            if s in ():
                terms = steps[s]["terms"]
                steps[s]["near"] = [xor_shift(wait(terms[by], *names), by) for by in (1, 2, 3)]
                continue
            steps[s]["far"] = wait(steps[s]["far"], *names)
            steps[s]["near"] = moved[f"near{s}"] = reduce_near(steps[s])
    grad_relay = relay(ids, grads, grad_far)
    grad_pieces = (*grads, grad_relay, *grad_far)
    section_outputs = section_outputs.reshape(shape)

    if eight:
        own = []
        for group in ((3, 2), (1, 0)):
            both = jnp.concatenate([reduce_last(steps[s]) for s in group], axis=1)
            own.append(added(both, swapped(both, "section", 2)))
        own = jnp.concatenate(own, axis=1)
        shapes = [w.shape for w in shards] + [gains.shape, position_table.shape[::-1]]
        peer = swapped(own, "section", 1)
        *final, table, section_grads = finish(ids, own, peer, shards, gains, shapes, grad_pieces)
        return (section_outputs, section_grads.reshape(shape)) + tuple(final) + (table.T,)

    section_grads = place(ids, grads, grad_relay, grad_far).reshape(shape)
    dense = [from_packed(packed[2 * layer], packed[2 * layer + 1]) for layer in range(layers)]
    final = []
    for at in range(7):
        both = jnp.stack([d[at] for d in dense])
        part = lax.psum_scatter(both, "dp", scatter_dimension=1, tiled=True)
        final.append(lax.psum(part, "section").astype(f32))
    terms = [w.astype(f32) * final[at] for at, w in enumerate(shards)]
    gain_sums = [sum(jnp.sum(terms[at], axis=2) for at in group) for group in ((0, 1, 2), (4, 5))]
    gains_grad = jnp.stack(gain_sums, axis=1) / gains.astype(f32)
    bias_sum = bias_sum.reshape(seq_count, heads, seq_count)
    table = jnp.einsum("jib,jhi->bh", onehot, bias_sum, precision=lax.Precision.HIGHEST)
    return (section_outputs, section_grads) + tuple(final) + (gains_grad, lax.psum(table, ("section", "dp")))


def solution(mesh):
    rows4 = P(None, "dp", None, None)
    rows3 = P(None, "dp", None)
    staged = P("section", None, "dp", None, None)
    return jax.shard_map(
        body,
        mesh=mesh,
        in_specs=(rows4, rows4) + (rows3,) * 9 + (P(None, None, "dp"), P()),
        out_specs=(staged, staged) + (rows3,) * 7 + (P(None, None, "dp"), P()),
        check_vma=False,
    )
```

```python
from functools import partial
import jax
import jax.numpy as jnp
from jax import lax
from jax.experimental import pallas as pl
from jax.experimental.pallas import tpu as pltpu
from jax.sharding import PartitionSpec as P

eps_norm = 1e-06
limits = (12, 16, 23, 32, 46, 64, 91)
masked = -1e30
bf = jnp.bfloat16
f32 = jnp.float32
vmem_mib = dict(
    attn_fwd=56, ffn_fwd=40, ffn_both=38, ffn_bwd=36, attn_front=34,
    attn_whole=28, attn_bwd=22, input_grad=12, pack_weights=56, finish=20, place=9, relay=6)


def dot_nn(a, b):
    return lax.dot_general(a, b, (((1,), (0,)), ((), ())), preferred_element_type=f32)


def dot_nt(a, b):
    return lax.dot_general(a, b, (((1,), (1,)), ((), ())), preferred_element_type=f32)


def dot_tn(a, b):
    return lax.dot_general(a, b, (((0,), (0,)), ((), ())), preferred_element_type=f32)


def row_scale(x):
    return lax.rsqrt(jnp.mean(x * x, axis=-1, keepdims=True) + eps_norm)


def pair_parts(values):
    lane = lax.broadcasted_iota(jnp.int32, values.shape, 1)
    zero = jnp.zeros_like(values)
    return jnp.concatenate(
        [jnp.where(lane < 64, values, zero), jnp.where(lane < 64, zero, values)], axis=0
    )


def pair_pick(values):
    half = values.shape[0] // 2
    lane = lax.broadcasted_iota(jnp.int32, (half, values.shape[1]), 1)
    return jnp.where(lane < 64, values[:half], values[half:])


blocks = 16
block_rows = 32


def order_of(ids, z, other_y, other_core):
    return (z * 2 + (ids[1] ^ other_y)) * 2 + (ids[2] ^ other_core)


def open_attn(ids, parts, wqkv, wo):
    for at, ref in enumerate(parts):
        other_y, other_core = at % 2, at // 2
        for z in range(4):
            place = order_of(ids, z, other_y, other_core)
            if wqkv is not None:
                wqkv[pl.ds(pl.multiple_of(place * 32, 32), 32), :] = ref[z, :, :1152]
            shard = z * 2 + (ids[1] ^ other_y)
            core = ids[2] ^ other_core
            for i in range(3):
                rows = pl.ds(pl.multiple_of(shard * 48 + i * 16, 16), 16)
                for j in range(2):
                    columns = pl.ds(pl.multiple_of(core * 256 + j * 128, 128), 128)
                    wo[rows, columns] = ref[z, j * 16:j * 16 + 16, 1152 + i * 128:1280 + i * 128]


def open_ffn(ids, parts, wgu, wd):
    for at, ref in enumerate(parts):
        other_y, other_core = at % 2, at // 2
        for z in range(4):
            place = order_of(ids, z, other_y, other_core)
            if wgu is not None:
                wgu[pl.ds(pl.multiple_of(place * 32, 32), 32), :] = ref[z, :, :2048]
            for i in range(2):
                wd[pl.ds(pl.multiple_of(place * 64 + i * 32, 32), 32), :] = (
                    ref[z, :, 2048 + i * 512:2560 + i * 512])


def open_columns(ids, parts, matrix):
    for at, ref in enumerate(parts):
        for z in range(4):
            place = order_of(ids, z, at % 2, at // 2)
            matrix[pl.ds(pl.multiple_of(place * 32, 32), 32), :] = ref[z, :, :matrix.shape[1]]


z_order = (0, 2, 1, 3)


def hand_out(ids, packed, refs):
    for at, ref in enumerate(refs):
        for by in range(4):
            place = order_of(ids, ids[0] ^ z_order[by], at % 2, at // 2)
            ref[by] = packed[pl.ds(pl.multiple_of(place * 32, 32), 32), :]


def attn_fwd_kernel(ids, x_ref, mask_ref, bias_ref, gain_ref, w0, w1, w2, w3,
                    out_ref, q_ref, k_ref, v_ref, p_ref, att_ref, wqkv, wo):
    @pl.when(pl.program_id(0) == 0)
    def _():
        open_attn(ids, (w0, w1, w2, w3), wqkv, wo)

    x = x_ref[...].astype(f32)
    a = (x * row_scale(x) * gain_ref[...]).astype(bf)
    q = dot_nn(a, wqkv[:, :384]).astype(bf)
    k = dot_nn(a, wqkv[:, 384:768]).astype(bf)
    v = dot_nn(a, wqkv[:, 768:]).astype(bf)
    q_ref[...] = q
    k_ref[...] = k
    v_ref[...] = v
    rows = x.shape[0] // 64
    units = [(r, h) for r in range(rows) for h in range(3)]
    at = lambda arr, r, h: arr[r * 64:r * 64 + 64, h * 128:h * 128 + 128]
    scores = [dot_nt(at(k, r, h), pair_parts(at(q, r, h))) for r, h in units]
    probs = []
    for (r, h), s in zip(units, scores):
        s = s + (bias_ref[:, h * 128:h * 128 + 128] + mask_ref[r])
        e = jnp.exp(s - jnp.max(s, axis=0, keepdims=True))
        p = (e * (1.0 / jnp.sum(e, axis=0, keepdims=True))).astype(bf)
        p_ref[r * 64:r * 64 + 64, h * 128:h * 128 + 128] = p
        probs.append(p)
    full_att = [dot_tn(p, at(v, r, h)) for (r, h), p in zip(units, probs)]
    att = {unit: pair_pick(part).astype(bf) for unit, part in zip(units, full_att)}
    att = jnp.concatenate(
        [jnp.concatenate([att[r, h] for h in range(3)], axis=1) for r in range(rows)], axis=0)
    att_ref[...] = att
    out_ref[...] = (x + dot_nn(att, wo[...])).astype(bf)


def normed(x_ref, gain_ref):
    x = x_ref[...].astype(f32)
    return (x * row_scale(x) * gain_ref[...]).astype(bf)


def norm_back(x_ref, gain_ref, gx, g_low):
    x = x_ref[...].astype(f32)
    scale = row_scale(x)
    n = x * scale
    e = gx * gain_ref[...]
    dx = scale * (e - n * jnp.mean(e * n, axis=-1, keepdims=True))
    return (g_low.astype(f32) + dx).astype(bf), (n * gain_ref[...]).astype(bf)


def input_grad_kernel(ids, x_ref, back_ref, g_ref, gain_ref, w0, w1, w2, w3, gin_ref, w_s):
    @pl.when(pl.program_id(0) == 0)
    def _():
        open_columns(ids, (w0, w1, w2, w3), w_s)

    gin_ref[...] = norm_back(x_ref, gain_ref, dot_nt(back_ref[...], w_s[...]), g_ref[...])[0]


def bucket_of(key, query):
    offset = key - query
    distance = jnp.abs(offset)
    far = jnp.full(distance.shape, 8, jnp.int32)
    for threshold in limits:
        far = far + (distance >= threshold).astype(jnp.int32)
    near = jnp.where(distance < 8, distance, jnp.minimum(far, 15))
    return near + 16 * (offset > 0).astype(jnp.int32)


def table_terms(bias_grad):
    key = lax.broadcasted_iota(jnp.int32, (64, 128), 0)
    query = lax.broadcasted_iota(jnp.int32, (64, 128), 1) & 63
    bucket = bucket_of(key, query)
    pieces = [bias_grad[:, h * 128:h * 128 + 128] for h in range(3)]
    sums = [[], [], []]
    for b in range(32):
        hit = bucket == b
        for h in range(3):
            sums[h].append(jnp.sum(jnp.where(hit, pieces[h], 0.0), axis=0, keepdims=True))
    lane = lax.broadcasted_iota(jnp.int32, (32, 128), 1)
    table = jnp.zeros((32, 128), f32)
    for h in range(3):
        part = jnp.concatenate(sums[h], axis=0)
        low = jnp.sum(jnp.where(lane < 64, part, 0.0), axis=1, keepdims=True)
        high = jnp.sum(jnp.where(lane < 64, 0.0, part), axis=1, keepdims=True)
        table = jnp.where(lane == 2 * h, low, jnp.where(lane == 2 * h + 1, high, table))
    return table


def attn_bwd_kernel(front, whole, ids, x_ref, q_ref, k_ref, v_ref, p_ref, att_ref, g_ref, gain_ref,
                    w0, w1, w2, w3, bias_in, *refs):
    refs = list(refs)
    if front:
        next_x, next_back, next_gain, n0, n1, n2, n3, *refs = refs
        grad_ref, *refs = refs
        next_w = refs.pop()
    if whole:
        wqkv = refs.pop()
    back_ref, r0, r1, r2, r3, dbias_ref, wo, a_s, dqkv_s, att_s, g_s, dbias_s, packed = refs
    step = pl.program_id(0)
    last = pl.num_programs(0) - 1
    block = x_ref.shape[0]
    with_table = r0.shape[2] > 1536

    @pl.when(step == 0)
    def _():
        open_attn(ids, (w0, w1, w2, w3), wqkv if whole else None, wo)
        if front:
            open_columns(ids, (n0, n1, n2, n3), next_w)
        dbias_s[...] = bias_in[...]

    here = pl.ds(pl.multiple_of(step * block, block), block)
    g_low = g_ref[...]
    if front:
        g_low = norm_back(next_x, next_gain, dot_nt(next_back[...], next_w[...]), g_low)[0]
        grad_ref[...] = g_low
    da = dot_nt(g_low, wo[...]).astype(bf)
    att_s[here, :] = att_ref[...]
    g_s[here, :] = g_low
    rows = block // 64
    units = [(r, h) for r in range(rows) for h in range(3)]
    at = lambda arr, r, h: arr[r * 64:r * 64 + 64, h * 128:h * 128 + 128]
    db = [None] * 3
    da_bds = [pair_parts(at(da, r, h)) for r, h in units]
    dps = [dot_nt(at(v_ref, r, h), da_bd) for (r, h), da_bd in zip(units, da_bds)]
    dv_u = {(r, h): dot_nn(at(p_ref, r, h), da_bd).astype(bf) for (r, h), da_bd in zip(units, da_bds)}
    dss = []
    for (r, h), dp in zip(units, dps):
        pf = at(p_ref, r, h).astype(f32)
        ds = pf * (dp - jnp.sum(pf * dp, axis=0, keepdims=True))
        db[h] = ds if db[h] is None else db[h] + ds
        dss.append(ds.astype(bf))
    dk_u = {(r, h): dot_nn(ds, pair_parts(at(q_ref, r, h))).astype(bf) for (r, h), ds in zip(units, dss)}
    full_dq = [dot_tn(ds, at(k_ref, r, h)) for (r, h), ds in zip(units, dss)]
    dq_u = {unit: pair_pick(part).astype(bf) for unit, part in zip(units, full_dq)}
    dqkv = jnp.concatenate(
        [jnp.concatenate([u[r, h] for u in (dq_u, dk_u, dv_u) for h in range(3)], axis=1)
         for r in range(rows)], axis=0)
    dqkv_s[here, :] = dqkv
    for h in range(3):
        dbias_s[:, h * 128:h * 128 + 128] += db[h]
    if whole:
        back_ref[...], a_s[here, :] = norm_back(x_ref, gain_ref, dot_nt(dqkv, wqkv[...]), g_low)
    else:
        back_ref[...] = dqkv
        a_s[here, :] = normed(x_ref, gain_ref)

    @pl.when(step == last)
    def _():
        for h in range(3):
            columns = slice(h * 384, h * 384 + 384)
            packed[:, columns] = dot_tn(a_s[...], dqkv_s[:, columns]).astype(bf)
        dwo = dot_tn(att_s[...], g_s[...]).astype(bf)
        for shard in range(8):
            for core in range(2):
                for i in range(3):
                    for j in range(2):
                        packed[(shard * 2 + core) * 32 + j * 16:(shard * 2 + core) * 32 + j * 16 + 16,
                               1152 + i * 128:1280 + i * 128] = (
                            dwo[shard * 48 + i * 16:shard * 48 + i * 16 + 16,
                                core * 256 + j * 128:core * 256 + j * 128 + 128])
        dbias_ref[...] = dbias_s[...]
        if with_table:
            table = table_terms(dbias_s[...]).astype(bf)
            for at in range(16):
                packed[at * 32:at * 32 + 32, 1536:1664] = table
        hand_out(ids, packed, (r0, r1, r2, r3))


def gelu_parts(u):
    c = 0.7978845608028654
    u2 = u * u
    t = jnp.tanh(u * (c + (c * 0.044715) * u2))
    half = 0.5 + 0.5 * t
    act = u * half
    slope = half + (0.5 * u) * (1.0 - t * t) * (c + (3.0 * c * 0.044715) * u2)
    return act, slope


def gelu(u):
    c = 0.7978845608028654
    t = jnp.tanh(u * (c + (c * 0.044715) * (u * u)))
    return u * (0.5 + 0.5 * t)


def ffn_fwd_kernel(ids, x_ref, gain_ref, w0, w1, w2, w3, out_ref, gate_ref, up_ref, wgu, wd):
    @pl.when(pl.program_id(0) == 0)
    def _():
        open_ffn(ids, (w0, w1, w2, w3), wgu, wd)

    x = x_ref[...].astype(f32)
    a = (x * row_scale(x) * gain_ref[...]).astype(bf)
    gate = dot_nn(a, wgu[:, :1024])
    up = dot_nn(a, wgu[:, 1024:])
    gate_ref[...] = gate.astype(bf)
    up_ref[...] = up.astype(bf)
    hidden = (gelu(gate) * up).astype(bf)
    out_ref[...] = (x + dot_nn(hidden, wd[...])).astype(bf)


def ffn_weight_grads(ids, a_s, gub_s, hid_s, g_s, packed, refs):
    for h in range(4):
        columns = slice(h * 512, h * 512 + 512)
        packed[:, columns] = dot_tn(a_s[...], gub_s[:, columns]).astype(bf)
    for h in range(2):
        dwd = dot_tn(hid_s[:, h * 512:h * 512 + 512], g_s[...]).astype(bf)
        for at in range(8):
            for i in range(2):
                packed[(h * 8 + at) * 32:(h * 8 + at) * 32 + 32, 2048 + i * 512:2560 + i * 512] = (
                    dwd[at * 64 + i * 32:at * 64 + i * 32 + 32])
    hand_out(ids, packed, refs)


def ffn_bwd_kernel(ids, x_ref, gate_ref, up_ref, g_ref, gain_ref, w0, w1, w2, w3,
                   gin_ref, r0, r1, r2, r3, wgu, wd, a_s, gub_s, hid_s, g_s, packed):
    step = pl.program_id(0)
    block = x_ref.shape[0]

    @pl.when(step == 0)
    def _():
        open_ffn(ids, (w0, w1, w2, w3), wgu, wd)

    here = pl.ds(pl.multiple_of(step * block, block), block)
    g_low = g_ref[...]
    g_s[here, :] = g_low
    hg = dot_nt(g_low, wd[...])
    gate = gate_ref[...].astype(f32)
    up = up_ref[...].astype(f32)
    act, slope = gelu_parts(gate)
    hid_s[here, :] = (act * up).astype(bf)
    gb = (hg * up * slope).astype(bf)
    ub = (hg * act).astype(bf)
    gub_s[here, :1024] = gb
    gub_s[here, 1024:] = ub
    gx = dot_nt(gb, wgu[:, :1024]) + dot_nt(ub, wgu[:, 1024:])
    gin_ref[...], a_s[here, :] = norm_back(x_ref, gain_ref, gx, g_low)

    @pl.when(step == pl.num_programs(0) - 1)
    def _():
        ffn_weight_grads(ids, a_s, gub_s, hid_s, g_s, packed, (r0, r1, r2, r3))


def ffn_both_kernel(ids, x_ref, g_ref, gain_ref, w0, w1, w2, w3,
                    out_ref, back_ref, r0, r1, r2, r3, wgu, wd, a_s, gub_s, hid_s, g_s, packed):
    step = pl.program_id(0)
    block = x_ref.shape[0]

    @pl.when(step == 0)
    def _():
        open_ffn(ids, (w0, w1, w2, w3), wgu, wd)

    here = pl.ds(pl.multiple_of(step * block, block), block)
    x = x_ref[...].astype(f32)
    a = (x * row_scale(x) * gain_ref[...]).astype(bf)
    gate = dot_nn(a, wgu[:, :1024])
    up = dot_nn(a, wgu[:, 1024:])
    g_low = g_ref[...]
    g_s[here, :] = g_low
    hg = dot_nt(g_low, wd[...])
    act, slope = gelu_parts(gate)
    hidden = (act * up).astype(bf)
    hid_s[here, :] = hidden
    out_ref[...] = (x + dot_nn(hidden, wd[...])).astype(bf)
    gb = (hg * up * slope).astype(bf)
    ub = (hg * act).astype(bf)
    gub_s[here, :1024] = gb
    gub_s[here, 1024:] = ub
    back_ref[:, :1024] = gb
    back_ref[:, 1024:] = ub
    a_s[here, :] = a

    @pl.when(step == pl.num_programs(0) - 1)
    def _():
        ffn_weight_grads(ids, a_s, gub_s, hid_s, g_s, packed, (r0, r1, r2, r3))


def tok(block, width):
    return pl.BlockSpec((block, width), lambda i, ids: (i, 0))


def picked(block, width):
    return pl.BlockSpec((None, block, width), lambda i, ids: (ids[3], i, 0))


def tokens_of(array, block):
    return (tok if array.ndim == 2 else picked)(block, array.shape[-1])


def full(shape):
    zero = (0,) * len(shape)
    return pl.BlockSpec(shape, lambda i, ids: zero)


def sds(shape, dtype):
    return jax.ShapeDtypeStruct(shape, dtype)


def call(kernel, grid, in_specs, out_specs, out_shape, scratch, micros, name):
    return pl.pallas_call(
        kernel,
        grid_spec=pltpu.PrefetchScalarGridSpec(
            num_scalar_prefetch=1, grid=(grid,), in_specs=in_specs, out_specs=out_specs,
            scratch_shapes=scratch),
        out_shape=out_shape, name=name,
        compiler_params=pltpu.CompilerParams(vmem_limit_bytes=vmem_mib[name] << 20),
        cost_estimate=pl.CostEstimate(flops=int(micros * 1.1e9), bytes_accessed=0, transcendentals=0),
    )


token_block = 512


def attn_fwd(ids, x, mask, bias, gain, parts):
    t, d = x.shape[-2:]
    block = token_block
    return call(
        attn_fwd_kernel, t // block,
        [tokens_of(x, block), pl.BlockSpec((block // 64, 64, 128), lambda i, ids: (i, 0, 0)),
         full(bias.shape), full((1, d))] + [full(parts[0].shape)] * 4,
        [tok(block, d)] + [tok(block, 384)] * 5,
        [sds((t, d), bf)] + [sds((t, 384), bf)] * 5,
        [pltpu.VMEM((512, 1152), bf), pltpu.VMEM((384, 512), bf)],
        15, "attn_fwd")(ids, x, mask, bias, gain, *parts)


def attn_bwd(ids, x, q, k, v, p, att, g, gain, parts, bias_in, whole, ahead=None, table=False):
    t, d = x.shape[-2:]
    block = token_block
    packed = (4, 32, 1664 if whole or table else 1536)
    width = d if whole else 1152
    args = [x, q, k, v, p, att, g, gain, *parts, bias_in]
    specs = ([tokens_of(x, block)] + [tok(block, 384)] * 5 + [tokens_of(g, block), full((1, d))]
             + [full(parts[0].shape)] * 4 + [full(bias_in.shape)])
    out_specs = [tok(block, width)] + [full(packed)] * 4 + [full((64, 384))]
    sizes = [sds((t, width), bf)] + [sds(packed, bf)] * 4 + [sds((64, 384), f32)]
    scratch = [pltpu.VMEM((384, 512), bf), pltpu.VMEM((t, d), bf), pltpu.VMEM((t, 1152), bf),
               pltpu.VMEM((t, 384), bf), pltpu.VMEM((t, d), bf), pltpu.VMEM((64, 384), f32),
               pltpu.VMEM((512, packed[2]), bf)]
    if whole:
        scratch.append(pltpu.VMEM((512, 1152), bf))
    if ahead is not None:
        next_x, next_back, next_gain, next_parts = ahead
        args += [next_x, next_back, next_gain, *next_parts]
        specs += [tok(block, d), tok(block, 2048), full((1, d))] + [columns_of(next_parts[0], 2048)] * 4
        out_specs.insert(0, tok(block, d))
        sizes.insert(0, sds((t, d), bf))
        scratch.append(pltpu.VMEM((512, 2048), bf))
    kernel = partial(attn_bwd_kernel, ahead is not None, whole)
    return call(kernel, t // block, specs, out_specs, sizes, scratch,
                15 if ahead is not None else 12 if whole else 9, "attn_front" if ahead is not None else "attn_whole" if whole else "attn_bwd")(ids, *args)


def columns_of(part, width):
    return pl.BlockSpec((4, part.shape[1], width), lambda i, ids: (0, 0, 0))


def input_grad(ids, x, back, g, gain, parts, micros):
    t, d = x.shape[-2:]
    block = token_block
    width = back.shape[1]
    part = columns_of(parts[0], width)
    return call(
        input_grad_kernel, t // block,
        [tokens_of(x, block), tok(block, width), tokens_of(g, block), full((1, d))] + [part] * 4,
        [tok(block, d)], [sds((t, d), bf)], [pltpu.VMEM((512, width), bf)],
        micros, "input_grad")(ids, x, back, g, gain, *parts)[0]


def ffn_fwd(ids, x, gain, parts):
    t, d = x.shape
    block = token_block
    return call(
        ffn_fwd_kernel, t // block,
        [tok(block, d), full((1, d))] + [full(parts[0].shape)] * 4,
        [tok(block, d), tok(block, 1024), tok(block, 1024)],
        [sds((t, d), bf), sds((t, 1024), bf), sds((t, 1024), bf)],
        [pltpu.VMEM((512, 2048), bf), pltpu.VMEM((1024, 512), bf)],
        0.3, "ffn_fwd")(ids, x, gain, *parts)


def ffn_scratch(t, d):
    return [pltpu.VMEM((1024, 512), bf), pltpu.VMEM((t, d), bf),
            pltpu.VMEM((t, 2048), bf), pltpu.VMEM((t, 1024), bf), pltpu.VMEM((t, d), bf),
            pltpu.VMEM((512, 3072), bf)]


def ffn_bwd(ids, x, gate, up, g, gain, parts):
    t, d = x.shape
    block = token_block
    packed = (4, 32, 3072)
    return call(
        ffn_bwd_kernel, t // block,
        [tok(block, d), tok(block, 1024), tok(block, 1024), tok(block, d), full((1, d))]
        + [full(parts[0].shape)] * 4,
        [tok(block, d)] + [full(packed)] * 4,
        [sds((t, d), bf)] + [sds(packed, bf)] * 4,
        [pltpu.VMEM((512, 2048), bf)] + ffn_scratch(t, d), 12, "ffn_bwd")(ids, x, gate, up, g, gain, *parts)


def ffn_both(ids, x, g, gain, parts):
    t, d = x.shape
    block = token_block
    packed = (4, 32, 3072)
    return call(
        ffn_both_kernel, t // block,
        [tok(block, d), tokens_of(g, block), full((1, d))] + [full(parts[0].shape)] * 4,
        [tok(block, d), tok(block, 2048)] + [full(packed)] * 4,
        [sds((t, d), bf), sds((t, 2048), bf)] + [sds(packed, bf)] * 4,
        [pltpu.VMEM((512, 2048), bf)] + ffn_scratch(t, d), 15, "ffn_both")(ids, x, g, gain, *parts)


def pack_attn_kernel(ids, q, k, v, o, *refs):
    core = ids[2]
    rows = pl.ds(pl.multiple_of(core * 32, 32), 32)
    out = refs[-1]
    layer = 1
    if len(refs) == 2:
        layer, gains = 0, refs[0]
        pair = [jnp.concatenate([gains[l, 0:1, :], gains[l, 1:2, :]], axis=1).astype(f32) for l in range(2)]
        row = lax.broadcasted_iota(jnp.int32, (32, 128), 0)
        out[:, 1536:] = jnp.where(row == 0, pair[0], jnp.where(row == 1, pair[1], 0.0)).astype(bf)
    for at, w in enumerate((q, k, v)):
        out[:, at * 384:at * 384 + 384] = w[layer, rows, :]
    for i in range(3):
        for j in range(2):
            columns = pl.ds(pl.multiple_of(core * 256 + j * 128, 128), 128)
            out[j * 16:j * 16 + 16, 1152 + i * 128:1280 + i * 128] = o[layer, i * 16:i * 16 + 16, columns]


def pack_ffn_kernel(ids, gate, up, down, *outs):
    core = ids[2]
    rows = pl.ds(pl.multiple_of(core * 32, 32), 32)
    for layer, out in enumerate(outs):
        out[:, :1024] = gate[layer, rows, :]
        out[:, 1024:2048] = up[layer, rows, :]
        for i in range(2):
            out[:, 2048 + i * 512:2560 + i * 512] = (
                down[layer, pl.ds(pl.multiple_of(core * 64 + i * 32, 32), 32), :])


def pack_weights(ids, shards, gains):
    attn, ffn = shards[:4], shards[4:]
    specs = [full(w.shape) for w in attn]
    first = call(pack_attn_kernel, 1, specs + [full(gains.shape)], [full((32, 1664))],
                 [sds((32, 1664), bf)], [], 2, "pack_weights")(ids, *attn, gains)[0]
    third = call(pack_attn_kernel, 1, specs, [full((32, 1536))],
                 [sds((32, 1536), bf)], [], 2, "pack_weights")(ids, *attn)[0]
    second, fourth = call(pack_ffn_kernel, 1, [full(w.shape) for w in ffn], [full((32, 3072))] * 2,
                          [sds((32, 3072), bf)] * 2, [], 2, "pack_weights")(ids, *ffn)
    return first, second, third, fourth


def finish_kernel(ids, own, peer, qw, kw, vw, gw, uw, gain, *refs):
    with_moves = len(refs) > 9
    if with_moves:
        moved, refs, moving_refs = refs[:9], refs[9:18], refs[18:]
        arrive, pass_on, leave = place_moves(ids, moved, *moving_refs)
        arrive()
    q, k, v, o, gate, up, down, gains, table = refs
    first = ids[2] == 0
    base = 0

    def row_sums(*pairs):
        total = None
        for weight, grad in pairs:
            term = weight.astype(f32) * grad
            total = term if total is None else total + term
        ones = jnp.ones((8, total.shape[1]), f32)
        sums = lax.dot_general(ones, total, (((1,), (1,)), ((), ())), preferred_element_type=f32,
                               precision=lax.Precision.HIGHEST)
        return sums[0:1, :]

    for s in (3, 2, 1, 0):
        layer = s // 2
        for core in range(2):
            def part(start, width, rows=slice(0, 32)):
                columns = slice(base + start, base + start + width)
                one, two = own[rows, columns].astype(f32), peer[rows, columns].astype(f32)
                return jnp.where(first, one, two) if core == 0 else jnp.where(first, two, one)

            rows = slice(core * 32, core * 32 + 32)
            if s % 2 == 0:
                for at, w in enumerate((q, k, v)):
                    w[layer, rows, :] = part(at * 384, 384)
                for i in range(3):
                    for j in range(2):
                        o[layer, i * 16:i * 16 + 16, core * 256 + j * 128:core * 256 + j * 128 + 128] = (
                            part(1152 + i * 128, 128, slice(j * 16, j * 16 + 16)))
            else:
                gate[layer, rows, :] = part(0, 1024)
                up[layer, rows, :] = part(1024, 1024)
                for i in range(2):
                    down[layer, core * 64 + i * 32:core * 64 + i * 32 + 32, :] = part(2048 + i * 512, 512)
            if s == 0 and core == 1:
                table[...] = part(1536, 128).T[:6, :]
        if s % 2 == 0:
            sums = row_sums(*((w[layer], grad[layer]) for w, grad in ((qw, q), (kw, k), (vw, v))))
        else:
            sums = row_sums(*((w[layer], grad[layer]) for w, grad in ((gw, gate), (uw, up))))
        gains[layer, s % 2:s % 2 + 1, :] = sums / gain[layer, s % 2:s % 2 + 1, :].astype(f32)
        base += 1536 if s % 2 == 0 else 3072
        if s == 3 and with_moves:
            pass_on()
    if with_moves:
        leave()


def finish(ids, own, peer, shards, gains, shapes, moved=()):
    q, k, v, o, gate, up, down = shards
    args = (own, peer, q, k, v, gate, up, gains)
    anywhere = pl.BlockSpec(memory_space=pl.ANY)
    specs, sizes = [full(array.shape) for array in args], [sds(shape, f32) for shape in shapes]
    out_specs, scratch = [full(shape) for shape in shapes], []
    if moved:
        t, d = moved[0].shape
        specs += [anywhere] * len(moved)
        out_specs.append(anywhere)
        sizes.append(sds((4, t, d), bf))
        scratch = [pltpu.VMEM((4, t, d), bf), pltpu.SemaphoreType.DMA((2, 4))]
    return call(finish_kernel, 1, specs, out_specs, sizes, scratch, 3, "finish")(ids, *args, *moved)


def move(sources, scratch, targets, sems):
    def fetch(ref, at):
        return pltpu.make_async_copy(ref, scratch.at[at], sems.at[0, at])

    def store(at):
        return pltpu.make_async_copy(scratch.at[at], targets[at], sems.at[1, at])

    def arrive():
        for at, options in enumerate(sources):
            for condition, ref in options:
                if condition is None:
                    fetch(ref, at).start()
                else:
                    @pl.when(condition)
                    def _(ref=ref, at=at):
                        fetch(ref, at).start()

    def pass_on():
        for at in range(len(targets)):
            fetch(sources[at][0][1], at).wait()
            store(at).start()

    def leave():
        for at in range(len(targets)):
            store(at).wait()

    return arrive, pass_on, leave


def place_moves(ids, refs, out, scratch, sems):
    own, relay, far = refs[:4], refs[4], refs[5:]
    section = ids[3]
    pick = lambda group: [(section == at, ref) for at, ref in enumerate(group)]
    return move([pick(own), [(None, relay.at[0])], pick(far), [(None, relay.at[1])]], scratch,
                [out.at[section ^ bit] for bit in range(4)], sems)


def place_kernel(ids, *refs):
    for part in place_moves(ids, refs[:9], *refs[9:]):
        part()


def moving(kernel, ids, arrays, out_shape, slots, micros, name):
    anywhere = pl.BlockSpec(memory_space=pl.ANY)
    t, d = arrays[0].shape[-2:]
    return pl.pallas_call(
        kernel,
        grid_spec=pltpu.PrefetchScalarGridSpec(
            num_scalar_prefetch=1, grid=(1,), in_specs=[anywhere] * len(arrays), out_specs=anywhere,
            scratch_shapes=[pltpu.VMEM((slots, t, d), bf), pltpu.SemaphoreType.DMA((2, slots))]),
        out_shape=out_shape, name=name,
        compiler_params=pltpu.CompilerParams(vmem_limit_bytes=vmem_mib[name] << 20),
        cost_estimate=pl.CostEstimate(flops=int(micros * 1.1e9), bytes_accessed=0, transcendentals=0),
    )(ids, *arrays)


def place(ids, own, relay, far):
    return moving(place_kernel, ids, (*own, relay, *far), sds((4,) + own[0].shape, bf), 4, 3, "place")


def relay_kernel(ids, *refs):
    own, far = refs[:4], refs[4:8]
    out, scratch, sems = refs[8:]
    pick = lambda group: [((ids[3] ^ 1) == at, ref) for at, ref in enumerate(group)]
    for part in move([pick(own), pick(far)], scratch, [out.at[0], out.at[1]], sems):
        part()


def relay(ids, own, far):
    t, d = own[0].shape
    both = moving(relay_kernel, ids, (*own, *far), sds((2, t, d), bf), 2, 2, "relay")
    return swapped(both, "section", 1)


def z_shift(values, by):
    half = lax.axis_size("dp") // 2
    pairs = [(z * 2 + y, ((z + by) % half) * 2 + y) for z in range(half) for y in range(2)]
    return lax.ppermute(values, "dp", pairs)


def swapped(values, axis, bit):
    return lax.ppermute(values, axis, [(i, i ^ bit) for i in range(lax.axis_size(axis))])


def after(values, *others):
    return lax.optimization_barrier((values,) + others)[0]


def added(*terms):
    total = terms[0].astype(f32)
    for term in terms[1:]:
        total = total + term.astype(f32)
    return total.astype(bf)


def gather_part(piece, z, previous):
    if previous is not None:
        piece = after(piece, *previous)
    got = [z_shift(piece, by) for by in range(1, 4)]
    column = jnp.stack([lax.select_n((z - at) % 4, piece, *got) for at in range(4)])
    return (column, swapped(column, "dp", 1)), got


def gather_core(column, other, *holds):
    if holds:
        column, other = lax.optimization_barrier((column, other) + holds)[:2]
    return column, other, swapped(column, "section", 1), swapped(other, "section", 1)


def reduce_first(own, other, give_own, give_other, straight, hold=None):
    first = swapped(give_other, "section", 1)
    sent = swapped(added(other, first), "dp", 1)
    got = swapped(give_own, "section", 1)
    step = dict(keep=own, first=first, core=got, y=sent)
    if straight:
        step["terms"] = [added(own[by], got[by], sent[by]) for by in range(4)]
    else:
        step["far"] = swapped(added(own[2:], got[2:], sent[2:] if hold is None else after(sent[2:], hold)), "dp", 2)
    return step


def xor_shift(values, z_bits):
    return swapped(values, "dp", 2 * z_bits)


def reduce_near(step):
    terms = (step["keep"][1], step["core"][1], step["y"][1], step["far"][1])
    return swapped(added(*terms), "dp", 4)


def reduce_last(step):
    if "terms" in step:
        return added(step["terms"][0], *step["near"])
    return added(step["keep"][0], step["core"][0], step["y"][0], step["far"][0], step["near"])


def to_packed(q, k, v, o, gate, up, down):
    o_part = o.reshape(8, 3, 16, 2, 2, 128).transpose(0, 3, 4, 2, 1, 5).reshape(512, 384)
    d_part = down.reshape(16, 2, 32, 512).transpose(0, 2, 1, 3).reshape(512, 1024)
    return jnp.concatenate([q, k, v, o_part], axis=1), jnp.concatenate([gate, up, d_part], axis=1)


def from_packed(attn, ffn):
    q, k, v = (attn[:, at * 384:at * 384 + 384] for at in range(3))
    o = attn[:, 1152:1536].reshape(8, 2, 2, 16, 3, 128).transpose(0, 4, 3, 1, 2, 5).reshape(384, 512)
    down = ffn[:, 2048:].reshape(16, 32, 2, 512).transpose(0, 2, 1, 3).reshape(1024, 512)
    return q, k, v, o, ffn[:, :1024], ffn[:, 1024:2048], down


def parts_of(whole):
    split = whole.reshape(4, 2, 2, 32, whole.shape[1])
    return tuple(split[:, y, core] for core in range(2) for y in range(2))


def whole_of(parts):
    parts = [part[..., :1536] if part.shape[2] == 1664 else part for part in parts]
    parts = [jnp.stack([part[by] for by in z_order]) for part in parts]
    split = jnp.stack(parts).reshape(2, 2, 4, 32, -1).transpose(2, 1, 0, 3, 4)
    return split.reshape(512, -1)


def gains_of(column, other, y):
    small = [part[:, :2, 1536:1664].reshape(4, 2, 2, 64) for part in (column, other)]
    pair = [jnp.where(y == at, small[0], small[1]) for at in range(2)]
    return jnp.stack(pair, axis=3).transpose(1, 2, 0, 3, 4).reshape(2, 2, 512).astype(f32)


def body(inputs, cotangent, segments, observed, q_weight, k_weight, v_weight, o_weight,
         gate_weight, up_weight, down_weight, gains, position_table):
    section = lax.axis_index("section")
    dp = lax.axis_index("dp")
    micro_count, row_count, seq_count, width = inputs.shape
    layers = q_weight.shape[0]
    heads = position_table.shape[1]
    tokens = row_count * seq_count
    shards = (q_weight, k_weight, v_weight, o_weight, gate_weight, up_weight, down_weight)
    eight = lax.axis_size("dp") == 8
    own_ids = jnp.stack([dp // 2, dp % 2, section % 2, section]).astype(jnp.int32)
    ids = own_ids if eight else jnp.stack([0 * dp, 0 * dp, 0 * dp, section]).astype(jnp.int32)

    weights = [None] * 4
    if eight:
        pieces = pack_weights(own_ids, shards, gains)
    else:
        whole = [lax.all_gather(w, "dp", axis=1, tiled=True) for w in shards]
        for layer in range(layers):
            weights[2 * layer], weights[2 * layer + 1] = (
                parts_of(w) for w in to_packed(*(w[layer] for w in whole)))
        gains_all = lax.all_gather(gains, "dp", axis=2, tiled=True).astype(f32)

    x = inputs.reshape(micro_count, tokens, width)
    grad = cotangent.reshape(micro_count, tokens, width)
    seg = lax.dynamic_index_in_dim(segments, section, 0, keepdims=False)
    obs = lax.dynamic_index_in_dim(observed, section, 0, keepdims=False)
    allowed = (seg[:, :, None] == seg[:, None, :]) & (obs[:, :, None] == 1)
    mask = jnp.where(allowed, 0.0, masked).astype(f32)
    mask = jnp.concatenate([mask, mask], axis=2)
    position = jnp.arange(seq_count, dtype=jnp.int32)
    bucket = bucket_of(position[:, None], position[None, :])
    onehot = (bucket[:, :, None] == jnp.arange(position_table.shape[0])[None, None, :]).astype(f32)
    bias = jnp.einsum("jib,bh->jhi", onehot, position_table.astype(f32), precision=lax.Precision.HIGHEST)
    bias = bias.reshape(seq_count, heads * seq_count)

    chip = section // 2

    def across(value, pairs):
        return lax.ppermute(value, "section", pairs)

    arrived = [()] * 4
    if eight:
        previous = None
        for s in range(4):
            weights[s], previous = gather_part(pieces[s], dp // 2, previous)
            arrived[s] = previous
            if s == 1:
                previous = previous + [weights[0][1]]
            if s == 1:
                previous = previous + [weights[0][1]]
            if s == 1:
                previous = previous + [weights[0][1]]
        gains_all = gains_of(*weights[0], dp % 2)

    chip = section // 2

    def both_ways(first, second):
        return swapped(jnp.where(chip == 0, first, second), "section", 2)

    def wait(value, *names):
        others = [steps[s][name] for s, name in names] if eight else []
        return after(value, *others) if others else value

    chip = section // 2

    def both_ways(first, second):
        return swapped(jnp.where(chip == 0, first, second), "section", 2)

    moved = {}

    def wait(value, *names):
        others = [moved[name] for name in names if name in moved]
        return after(value, *others) if others else value

    def gain_of(s):
        return gains_all[s // 2, s % 2][None]

    packed, steps = [None] * 4, [None] * 4

    def passed(s, parts):
        if eight:
            for at, names in ((1, ("far3", )), (0, ("near3", ))):
                if s == at:
                    parts[3] = wait(parts[3], *names)
            hold = [moved[name] for name in () if s == 0 and name in moved]
            steps[s] = reduce_first(*parts, s in (), *hold)
            moved.update({f"{name}{s}": steps[s][name] for name in ("first", "core", "y", "far") if name in steps[s]})
        else:
            packed[s] = whole_of(parts)

    states, kept = [x], []
    outs, grads, out_far, grad_far = [None] * 4, [None] * 4, [None] * 4, [None] * 4
    for s in range(4):
        feed = states[s]
        if eight:
            if s < 3:
                feed = after(feed, *arrived[s + 1])
            holds = [states[s]] if s in (1, 3) else []
            holds += [weights[at][1] for to, at in ((1, 2),) if to == s]
            weights[s] = gather_core(*weights[s], *holds)
        if s == 3:
            outs[3], last_back, *parts = ffn_both(ids, feed, grad, gain_of(3), weights[3])
            break
        if s % 2 == 0:
            out, *saved = attn_fwd(ids, feed, mask, bias, gain_of(s), weights[s])
        else:
            out, *saved = ffn_fwd(ids, feed, gain_of(s), weights[s])
        states.append(out)
        kept.append(saved)
        outs[s] = out
    out_far[0] = out_far[2] = moved["x1"] = both_ways(outs[2], outs[0])
    passed(3, parts)

    bias_sum = jnp.zeros((seq_count, heads * seq_count), f32)
    grads[3] = grad = input_grad(ids, states[3], last_back, grad, gain_of(3), weights[3], 20)
    out_far[1] = grad_far[3] = moved["x2"] = both_ways(grad, outs[1])
    back, *parts, bias_sum = attn_bwd(
        ids, states[2], *kept[2], wait(grad, "first3", "x1"), gain_of(2), weights[2], bias_sum, False)
    passed(2, parts)
    grads[2] = grad = input_grad(
        ids, states[2], back, grad, gain_of(2), weights[2], 20)
    grads[1], *parts = ffn_bwd(
        ids, states[1], *kept[1], wait(grad, "first2", "y3"), gain_of(1), weights[1])
    passed(1, parts)
    grad = grads[1]
    if eight and 3 in (3,):
        steps[3]["near"] = moved["near3"] = reduce_near(steps[3])
    out_far[3] = grad_far[1] = moved["x3"] = both_ways(outs[3], grad)
    grads[0], *parts, bias_sum = attn_bwd(
        ids, states[0], *kept[0], wait(grad, "first1", "y2", "x2"), gain_of(0), weights[0], bias_sum, True)
    passed(0, parts)
    moved["g0"] = grads[0]
    grad_far[0] = grad_far[2] = moved["x4"] = both_ways(grads[2], wait(grads[0], "x3", "y1"))

    shape = (1, micro_count, row_count, seq_count, width)
    out_relay = relay(ids, outs, out_far[:3] + [wait(out_far[3], "y0")])
    section_outputs = moved["placed"] = place(ids, outs, out_relay, out_far)
    if eight:
        for s, names in ((3, ("y1", )), (2, ("y0", )), (1, ()), (0, ())):
            if "near" in steps[s]:
                continue
            if s in ():
                terms = steps[s]["terms"]
                steps[s]["near"] = [
                    xor_shift(wait(terms[by], *names), z_order[by]) for by in (1, 2, 3)]
                moved[f"near{s}"] = steps[s]["near"][-1]
                continue
            steps[s]["far"] = wait(steps[s]["far"], *names)
            steps[s]["near"] = moved[f"near{s}"] = reduce_near(steps[s])
    grad_relay = moved["relayed"] = relay(ids, grads, grad_far)
    grad_pieces = (*grads, grad_relay, *grad_far)
    section_outputs = section_outputs.reshape(shape)

    if eight:
        own = []
        for group in ((3, 2), (1, 0)):
            both = jnp.concatenate([reduce_last(steps[s]) for s in group], axis=1)
            own.append(added(both, swapped(both, "section", 2)))
        own = jnp.concatenate(own, axis=1)
        shapes = [w.shape for w in shards] + [gains.shape, position_table.shape[::-1]]
        peer = swapped(own, "section", 1)
        *final, table, section_grads = finish(ids, own, peer, shards, gains, shapes, grad_pieces)
        return (section_outputs, section_grads.reshape(shape)) + tuple(final) + (table.T,)

    section_grads = place(ids, grads, grad_relay, grad_far).reshape(shape)
    dense = [from_packed(packed[2 * layer], packed[2 * layer + 1]) for layer in range(layers)]
    final = []
    for at in range(7):
        both = jnp.stack([d[at] for d in dense])
        part = lax.psum_scatter(both, "dp", scatter_dimension=1, tiled=True)
        final.append(lax.psum(part, "section").astype(f32))
    terms = [w.astype(f32) * final[at] for at, w in enumerate(shards)]
    gain_sums = [sum(jnp.sum(terms[at], axis=2) for at in group) for group in ((0, 1, 2), (4, 5))]
    gains_grad = jnp.stack(gain_sums, axis=1) / gains.astype(f32)
    bias_sum = bias_sum.reshape(seq_count, heads, seq_count)
    table = jnp.einsum("jib,jhi->bh", onehot, bias_sum, precision=lax.Precision.HIGHEST)
    return (section_outputs, section_grads) + tuple(final) + (gains_grad, lax.psum(table, ("section", "dp")))


def solution(mesh):
    rows4 = P(None, "dp", None, None)
    rows3 = P(None, "dp", None)
    staged = P("section", None, "dp", None, None)
    return jax.shard_map(
        body,
        mesh=mesh,
        in_specs=(rows4, rows4) + (rows3,) * 9 + (P(None, None, "dp"), P()),
        out_specs=(staged, staged) + (rows3,) * 7 + (P(None, None, "dp"), P()),
        check_vma=False,
    )
```

```python
from functools import partial
import jax
import jax.numpy as jnp
from jax import lax
from jax.experimental import pallas as pl
from jax.experimental.pallas import tpu as pltpu
from jax.sharding import PartitionSpec as P

eps_norm = 1e-06
limits = (12, 16, 23, 32, 46, 64, 91)
masked = -1e30
bf = jnp.bfloat16
f32 = jnp.float32
vmem_mib = dict(
    attn_fwd=56, ffn_fwd=40, ffn_both=38, ffn_bwd=33, attn_front=34,
    attn_whole=28, attn_bwd=22, input_grad=12, pack_weights=56, finish=20, place=9, relay=6)


def dot_nn(a, b):
    return lax.dot_general(a, b, (((1,), (0,)), ((), ())), preferred_element_type=f32)


def dot_nt(a, b):
    return lax.dot_general(a, b, (((1,), (1,)), ((), ())), preferred_element_type=f32)


def dot_tn(a, b):
    return lax.dot_general(a, b, (((0,), (0,)), ((), ())), preferred_element_type=f32)


def row_scale(x):
    return lax.rsqrt(jnp.mean(x * x, axis=-1, keepdims=True) + eps_norm)


def pair_parts(values):
    lane = lax.broadcasted_iota(jnp.int32, values.shape, 1)
    zero = jnp.zeros_like(values)
    return jnp.concatenate(
        [jnp.where(lane < 64, values, zero), jnp.where(lane < 64, zero, values)], axis=0
    )


def pair_pick(values):
    half = values.shape[0] // 2
    lane = lax.broadcasted_iota(jnp.int32, (half, values.shape[1]), 1)
    return jnp.where(lane < 64, values[:half], values[half:])


blocks = 16
block_rows = 32


def order_of(ids, z, other_y, other_core):
    return (z * 2 + (ids[1] ^ other_y)) * 2 + (ids[2] ^ other_core)


def open_attn(ids, parts, wqkv, wo):
    for at, ref in enumerate(parts):
        other_y, other_core = at % 2, at // 2
        for z in range(4):
            place = order_of(ids, z, other_y, other_core)
            if wqkv is not None:
                wqkv[pl.ds(pl.multiple_of(place * 32, 32), 32), :] = ref[z, :, :1152]
            shard = z * 2 + (ids[1] ^ other_y)
            core = ids[2] ^ other_core
            for i in range(3):
                rows = pl.ds(pl.multiple_of(shard * 48 + i * 16, 16), 16)
                for j in range(2):
                    columns = pl.ds(pl.multiple_of(core * 256 + j * 128, 128), 128)
                    wo[rows, columns] = ref[z, j * 16:j * 16 + 16, 1152 + i * 128:1280 + i * 128]


def open_ffn(ids, parts, wgu, wd):
    for at, ref in enumerate(parts):
        other_y, other_core = at % 2, at // 2
        for z in range(4):
            place = order_of(ids, z, other_y, other_core)
            if wgu is not None:
                wgu[pl.ds(pl.multiple_of(place * 32, 32), 32), :] = ref[z, :, :2048]
            for i in range(2):
                wd[pl.ds(pl.multiple_of(place * 64 + i * 32, 32), 32), :] = (
                    ref[z, :, 2048 + i * 512:2560 + i * 512])


def open_columns(ids, parts, matrix):
    for at, ref in enumerate(parts):
        for z in range(4):
            place = order_of(ids, z, at % 2, at // 2)
            matrix[pl.ds(pl.multiple_of(place * 32, 32), 32), :] = ref[z, :, :matrix.shape[1]]


z_order = (0, 2, 1, 3)


def hand_out(ids, packed, refs):
    for at, ref in enumerate(refs):
        for by in range(4):
            place = order_of(ids, ids[0] ^ z_order[by], at % 2, at // 2)
            ref[by] = packed[pl.ds(pl.multiple_of(place * 32, 32), 32), :]


def attn_fwd_kernel(ids, x_ref, mask_ref, bias_ref, gain_ref, w0, w1, w2, w3,
                    out_ref, q_ref, k_ref, v_ref, p_ref, att_ref, wqkv, wo):
    @pl.when(pl.program_id(0) == 0)
    def _():
        open_attn(ids, (w0, w1, w2, w3), wqkv, wo)

    x = x_ref[...].astype(f32)
    a = (x * row_scale(x) * gain_ref[...]).astype(bf)
    q = dot_nn(a, wqkv[:, :384]).astype(bf)
    k = dot_nn(a, wqkv[:, 384:768]).astype(bf)
    v = dot_nn(a, wqkv[:, 768:]).astype(bf)
    q_ref[...] = q
    k_ref[...] = k
    v_ref[...] = v
    rows = x.shape[0] // 64
    units = [(r, h) for r in range(rows) for h in range(3)]
    at = lambda arr, r, h: arr[r * 64:r * 64 + 64, h * 128:h * 128 + 128]
    scores = [dot_nt(at(k, r, h), pair_parts(at(q, r, h))) for r, h in units]
    probs = []
    for (r, h), s in zip(units, scores):
        s = s + (bias_ref[:, h * 128:h * 128 + 128] + mask_ref[r])
        e = jnp.exp(s - jnp.max(s, axis=0, keepdims=True))
        p = (e * (1.0 / jnp.sum(e, axis=0, keepdims=True))).astype(bf)
        p_ref[r * 64:r * 64 + 64, h * 128:h * 128 + 128] = p
        probs.append(p)
    full_att = [dot_tn(p, at(v, r, h)) for (r, h), p in zip(units, probs)]
    att = {unit: pair_pick(part).astype(bf) for unit, part in zip(units, full_att)}
    att = jnp.concatenate(
        [jnp.concatenate([att[r, h] for h in range(3)], axis=1) for r in range(rows)], axis=0)
    att_ref[...] = att
    out_ref[...] = (x + dot_nn(att, wo[...])).astype(bf)


def normed(x_ref, gain_ref):
    x = x_ref[...].astype(f32)
    return (x * row_scale(x) * gain_ref[...]).astype(bf)


def norm_back(x_ref, gain_ref, gx, g_low):
    x = x_ref[...].astype(f32)
    scale = row_scale(x)
    n = x * scale
    e = gx * gain_ref[...]
    dx = scale * (e - n * jnp.mean(e * n, axis=-1, keepdims=True))
    return (g_low.astype(f32) + dx).astype(bf), (n * gain_ref[...]).astype(bf)


def input_grad_kernel(ids, x_ref, back_ref, g_ref, gain_ref, w0, w1, w2, w3, gin_ref, w_s):
    @pl.when(pl.program_id(0) == 0)
    def _():
        open_columns(ids, (w0, w1, w2, w3), w_s)

    gin_ref[...] = norm_back(x_ref, gain_ref, dot_nt(back_ref[...], w_s[...]), g_ref[...])[0]


def bucket_of(key, query):
    offset = key - query
    distance = jnp.abs(offset)
    far = jnp.full(distance.shape, 8, jnp.int32)
    for threshold in limits:
        far = far + (distance >= threshold).astype(jnp.int32)
    near = jnp.where(distance < 8, distance, jnp.minimum(far, 15))
    return near + 16 * (offset > 0).astype(jnp.int32)


def table_terms(bias_grad):
    key = lax.broadcasted_iota(jnp.int32, (64, 128), 0)
    query = lax.broadcasted_iota(jnp.int32, (64, 128), 1) & 63
    bucket = bucket_of(key, query)
    pieces = [bias_grad[:, h * 128:h * 128 + 128] for h in range(3)]
    sums = [[], [], []]
    for b in range(32):
        hit = bucket == b
        for h in range(3):
            sums[h].append(jnp.sum(jnp.where(hit, pieces[h], 0.0), axis=0, keepdims=True))
    lane = lax.broadcasted_iota(jnp.int32, (32, 128), 1)
    table = jnp.zeros((32, 128), f32)
    for h in range(3):
        part = jnp.concatenate(sums[h], axis=0)
        low = jnp.sum(jnp.where(lane < 64, part, 0.0), axis=1, keepdims=True)
        high = jnp.sum(jnp.where(lane < 64, 0.0, part), axis=1, keepdims=True)
        table = jnp.where(lane == 2 * h, low, jnp.where(lane == 2 * h + 1, high, table))
    return table


def attn_bwd_kernel(front, whole, ids, x_ref, q_ref, k_ref, v_ref, p_ref, att_ref, g_ref, gain_ref,
                    w0, w1, w2, w3, bias_in, *refs):
    refs = list(refs)
    if front:
        next_x, next_back, next_gain, n0, n1, n2, n3, *refs = refs
        grad_ref, *refs = refs
        next_w = refs.pop()
    if whole:
        wqkv = refs.pop()
    back_ref, r0, r1, r2, r3, dbias_ref, wo, a_s, dqkv_s, att_s, g_s, dbias_s, packed = refs
    step = pl.program_id(0)
    last = pl.num_programs(0) - 1
    block = x_ref.shape[0]
    with_table = r0.shape[2] > 1536

    @pl.when(step == 0)
    def _():
        open_attn(ids, (w0, w1, w2, w3), wqkv if whole else None, wo)
        if front:
            open_columns(ids, (n0, n1, n2, n3), next_w)
        dbias_s[...] = bias_in[...]

    here = pl.ds(pl.multiple_of(step * block, block), block)
    g_low = g_ref[...]
    if front:
        g_low = norm_back(next_x, next_gain, dot_nt(next_back[...], next_w[...]), g_low)[0]
        grad_ref[...] = g_low
    da = dot_nt(g_low, wo[...]).astype(bf)
    att_s[here, :] = att_ref[...]
    g_s[here, :] = g_low
    rows = block // 64
    units = [(r, h) for r in range(rows) for h in range(3)]
    at = lambda arr, r, h: arr[r * 64:r * 64 + 64, h * 128:h * 128 + 128]
    db = [None] * 3
    da_bds = [pair_parts(at(da, r, h)) for r, h in units]
    dps = [dot_nt(at(v_ref, r, h), da_bd) for (r, h), da_bd in zip(units, da_bds)]
    dv_u = {(r, h): dot_nn(at(p_ref, r, h), da_bd).astype(bf) for (r, h), da_bd in zip(units, da_bds)}
    dss = []
    for (r, h), dp in zip(units, dps):
        pf = at(p_ref, r, h).astype(f32)
        ds = pf * (dp - jnp.sum(pf * dp, axis=0, keepdims=True))
        db[h] = ds if db[h] is None else db[h] + ds
        dss.append(ds.astype(bf))
    dk_u = {(r, h): dot_nn(ds, pair_parts(at(q_ref, r, h))).astype(bf) for (r, h), ds in zip(units, dss)}
    full_dq = [dot_tn(ds, at(k_ref, r, h)) for (r, h), ds in zip(units, dss)]
    dq_u = {unit: pair_pick(part).astype(bf) for unit, part in zip(units, full_dq)}
    dqkv = jnp.concatenate(
        [jnp.concatenate([u[r, h] for u in (dq_u, dk_u, dv_u) for h in range(3)], axis=1)
         for r in range(rows)], axis=0)
    dqkv_s[here, :] = dqkv
    for h in range(3):
        dbias_s[:, h * 128:h * 128 + 128] += db[h]
    if whole:
        back_ref[...], a_s[here, :] = norm_back(x_ref, gain_ref, dot_nt(dqkv, wqkv[...]), g_low)
    else:
        back_ref[...] = dqkv
        a_s[here, :] = normed(x_ref, gain_ref)

    @pl.when(step == last)
    def _():
        for h in range(3):
            columns = slice(h * 384, h * 384 + 384)
            packed[:, columns] = dot_tn(a_s[...], dqkv_s[:, columns]).astype(bf)
        dwo = dot_tn(att_s[...], g_s[...]).astype(bf)
        for shard in range(8):
            for core in range(2):
                for i in range(3):
                    for j in range(2):
                        packed[(shard * 2 + core) * 32 + j * 16:(shard * 2 + core) * 32 + j * 16 + 16,
                               1152 + i * 128:1280 + i * 128] = (
                            dwo[shard * 48 + i * 16:shard * 48 + i * 16 + 16,
                                core * 256 + j * 128:core * 256 + j * 128 + 128])
        dbias_ref[...] = dbias_s[...]
        if with_table:
            table = table_terms(dbias_s[...]).astype(bf)
            for at in range(16):
                packed[at * 32:at * 32 + 32, 1536:1664] = table
        hand_out(ids, packed, (r0, r1, r2, r3))


def gelu_parts(u):
    c = 0.7978845608028654
    u2 = u * u
    t = jnp.tanh(u * (c + (c * 0.044715) * u2))
    half = 0.5 + 0.5 * t
    act = u * half
    slope = half + (0.5 * u) * (1.0 - t * t) * (c + (3.0 * c * 0.044715) * u2)
    return act, slope


def gelu(u):
    c = 0.7978845608028654
    t = jnp.tanh(u * (c + (c * 0.044715) * (u * u)))
    return u * (0.5 + 0.5 * t)


def ffn_fwd_kernel(ids, x_ref, gain_ref, w0, w1, w2, w3, out_ref, gate_ref, up_ref, wgu, wd):
    @pl.when(pl.program_id(0) == 0)
    def _():
        open_ffn(ids, (w0, w1, w2, w3), wgu, wd)

    x = x_ref[...].astype(f32)
    a = (x * row_scale(x) * gain_ref[...]).astype(bf)
    gate = dot_nn(a, wgu[:, :1024])
    up = dot_nn(a, wgu[:, 1024:])
    gate_ref[...] = gate.astype(bf)
    up_ref[...] = up.astype(bf)
    hidden = (gelu(gate) * up).astype(bf)
    out_ref[...] = (x + dot_nn(hidden, wd[...])).astype(bf)


def ffn_weight_grads(ids, a_s, gub_s, hid_s, g_s, packed, refs):
    for h in range(4):
        columns = slice(h * 512, h * 512 + 512)
        packed[:, columns] = dot_tn(a_s[...], gub_s[:, columns]).astype(bf)
    for h in range(2):
        dwd = dot_tn(hid_s[:, h * 512:h * 512 + 512], g_s[...]).astype(bf)
        for at in range(8):
            for i in range(2):
                packed[(h * 8 + at) * 32:(h * 8 + at) * 32 + 32, 2048 + i * 512:2560 + i * 512] = (
                    dwd[at * 64 + i * 32:at * 64 + i * 32 + 32])
    hand_out(ids, packed, refs)


def ffn_bwd_kernel(ids, x_ref, gate_ref, up_ref, g_ref, gain_ref, w0, w1, w2, w3,
                   gin_ref, r0, r1, r2, r3, wgu, wd, a_s, gub_s, hid_s, g_s, packed):
    step = pl.program_id(0)
    block = x_ref.shape[0]

    @pl.when(step == 0)
    def _():
        open_ffn(ids, (w0, w1, w2, w3), wgu, wd)

    here = pl.ds(pl.multiple_of(step * block, block), block)
    g_low = g_ref[...]
    g_s[here, :] = g_low
    hg = dot_nt(g_low, wd[...])
    gate = gate_ref[...].astype(f32)
    up = up_ref[...].astype(f32)
    act, slope = gelu_parts(gate)
    hid_s[here, :] = (act * up).astype(bf)
    gb = (hg * up * slope).astype(bf)
    ub = (hg * act).astype(bf)
    gub_s[here, :1024] = gb
    gub_s[here, 1024:] = ub
    gx = dot_nt(gb, wgu[:, :1024]) + dot_nt(ub, wgu[:, 1024:])
    gin_ref[...], a_s[here, :] = norm_back(x_ref, gain_ref, gx, g_low)

    @pl.when(step == pl.num_programs(0) - 1)
    def _():
        ffn_weight_grads(ids, a_s, gub_s, hid_s, g_s, packed, (r0, r1, r2, r3))


def ffn_both_kernel(ids, x_ref, g_ref, gain_ref, w0, w1, w2, w3,
                    out_ref, back_ref, r0, r1, r2, r3, wgu, wd, a_s, gub_s, hid_s, g_s, packed):
    step = pl.program_id(0)
    block = x_ref.shape[0]

    @pl.when(step == 0)
    def _():
        open_ffn(ids, (w0, w1, w2, w3), wgu, wd)

    here = pl.ds(pl.multiple_of(step * block, block), block)
    x = x_ref[...].astype(f32)
    a = (x * row_scale(x) * gain_ref[...]).astype(bf)
    gate = dot_nn(a, wgu[:, :1024])
    up = dot_nn(a, wgu[:, 1024:])
    g_low = g_ref[...]
    g_s[here, :] = g_low
    hg = dot_nt(g_low, wd[...])
    act, slope = gelu_parts(gate)
    hidden = (act * up).astype(bf)
    hid_s[here, :] = hidden
    out_ref[...] = (x + dot_nn(hidden, wd[...])).astype(bf)
    gb = (hg * up * slope).astype(bf)
    ub = (hg * act).astype(bf)
    gub_s[here, :1024] = gb
    gub_s[here, 1024:] = ub
    back_ref[:, :1024] = gb
    back_ref[:, 1024:] = ub
    a_s[here, :] = a

    @pl.when(step == pl.num_programs(0) - 1)
    def _():
        ffn_weight_grads(ids, a_s, gub_s, hid_s, g_s, packed, (r0, r1, r2, r3))


def tok(block, width):
    return pl.BlockSpec((block, width), lambda i, ids: (i, 0))


def picked(block, width):
    return pl.BlockSpec((None, block, width), lambda i, ids: (ids[3], i, 0))


def tokens_of(array, block):
    return (tok if array.ndim == 2 else picked)(block, array.shape[-1])


def full(shape):
    zero = (0,) * len(shape)
    return pl.BlockSpec(shape, lambda i, ids: zero)


def sds(shape, dtype):
    return jax.ShapeDtypeStruct(shape, dtype)


def call(kernel, grid, in_specs, out_specs, out_shape, scratch, micros, name):
    return pl.pallas_call(
        kernel,
        grid_spec=pltpu.PrefetchScalarGridSpec(
            num_scalar_prefetch=1, grid=(grid,), in_specs=in_specs, out_specs=out_specs,
            scratch_shapes=scratch),
        out_shape=out_shape, name=name,
        compiler_params=pltpu.CompilerParams(vmem_limit_bytes=vmem_mib[name] << 20),
        cost_estimate=pl.CostEstimate(flops=int(micros * 1.1e9), bytes_accessed=0, transcendentals=0),
    )


token_block = 512


def attn_fwd(ids, x, mask, bias, gain, parts):
    t, d = x.shape[-2:]
    block = token_block
    return call(
        attn_fwd_kernel, t // block,
        [tokens_of(x, block), pl.BlockSpec((block // 64, 64, 128), lambda i, ids: (i, 0, 0)),
         full(bias.shape), full((1, d))] + [full(parts[0].shape)] * 4,
        [tok(block, d)] + [tok(block, 384)] * 5,
        [sds((t, d), bf)] + [sds((t, 384), bf)] * 5,
        [pltpu.VMEM((512, 1152), bf), pltpu.VMEM((384, 512), bf)],
        15, "attn_fwd")(ids, x, mask, bias, gain, *parts)


def attn_bwd(ids, x, q, k, v, p, att, g, gain, parts, bias_in, whole, ahead=None, table=False):
    t, d = x.shape[-2:]
    block = token_block
    packed = (4, 32, 1664 if whole or table else 1536)
    width = d if whole else 1152
    args = [x, q, k, v, p, att, g, gain, *parts, bias_in]
    specs = ([tokens_of(x, block)] + [tok(block, 384)] * 5 + [tokens_of(g, block), full((1, d))]
             + [full(parts[0].shape)] * 4 + [full(bias_in.shape)])
    out_specs = [tok(block, width)] + [full(packed)] * 4 + [full((64, 384))]
    sizes = [sds((t, width), bf)] + [sds(packed, bf)] * 4 + [sds((64, 384), f32)]
    scratch = [pltpu.VMEM((384, 512), bf), pltpu.VMEM((t, d), bf), pltpu.VMEM((t, 1152), bf),
               pltpu.VMEM((t, 384), bf), pltpu.VMEM((t, d), bf), pltpu.VMEM((64, 384), f32),
               pltpu.VMEM((512, packed[2]), bf)]
    if whole:
        scratch.append(pltpu.VMEM((512, 1152), bf))
    if ahead is not None:
        next_x, next_back, next_gain, next_parts = ahead
        args += [next_x, next_back, next_gain, *next_parts]
        specs += [tok(block, d), tok(block, 2048), full((1, d))] + [columns_of(next_parts[0], 2048)] * 4
        out_specs.insert(0, tok(block, d))
        sizes.insert(0, sds((t, d), bf))
        scratch.append(pltpu.VMEM((512, 2048), bf))
    kernel = partial(attn_bwd_kernel, ahead is not None, whole)
    return call(kernel, t // block, specs, out_specs, sizes, scratch,
                15 if ahead is not None else 20 if whole else 9, "attn_front" if ahead is not None else "attn_whole" if whole else "attn_bwd")(ids, *args)


def columns_of(part, width):
    return pl.BlockSpec((4, part.shape[1], width), lambda i, ids: (0, 0, 0))


def input_grad(ids, x, back, g, gain, parts, micros):
    t, d = x.shape[-2:]
    block = token_block
    width = back.shape[1]
    part = columns_of(parts[0], width)
    return call(
        input_grad_kernel, t // block,
        [tokens_of(x, block), tok(block, width), tokens_of(g, block), full((1, d))] + [part] * 4,
        [tok(block, d)], [sds((t, d), bf)], [pltpu.VMEM((512, width), bf)],
        micros, "input_grad")(ids, x, back, g, gain, *parts)[0]


def ffn_fwd(ids, x, gain, parts):
    t, d = x.shape
    block = token_block
    return call(
        ffn_fwd_kernel, t // block,
        [tok(block, d), full((1, d))] + [full(parts[0].shape)] * 4,
        [tok(block, d), tok(block, 1024), tok(block, 1024)],
        [sds((t, d), bf), sds((t, 1024), bf), sds((t, 1024), bf)],
        [pltpu.VMEM((512, 2048), bf), pltpu.VMEM((1024, 512), bf)],
        0.3, "ffn_fwd")(ids, x, gain, *parts)


def ffn_scratch(t, d):
    return [pltpu.VMEM((1024, 512), bf), pltpu.VMEM((t, d), bf),
            pltpu.VMEM((t, 2048), bf), pltpu.VMEM((t, 1024), bf), pltpu.VMEM((t, d), bf),
            pltpu.VMEM((512, 3072), bf)]


def ffn_bwd(ids, x, gate, up, g, gain, parts):
    t, d = x.shape
    block = token_block
    packed = (4, 32, 3072)
    return call(
        ffn_bwd_kernel, t // block,
        [tok(block, d), tok(block, 1024), tok(block, 1024), tok(block, d), full((1, d))]
        + [full(parts[0].shape)] * 4,
        [tok(block, d)] + [full(packed)] * 4,
        [sds((t, d), bf)] + [sds(packed, bf)] * 4,
        [pltpu.VMEM((512, 2048), bf)] + ffn_scratch(t, d), 12, "ffn_bwd")(ids, x, gate, up, g, gain, *parts)


def ffn_both(ids, x, g, gain, parts):
    t, d = x.shape
    block = token_block
    packed = (4, 32, 3072)
    return call(
        ffn_both_kernel, t // block,
        [tok(block, d), tokens_of(g, block), full((1, d))] + [full(parts[0].shape)] * 4,
        [tok(block, d), tok(block, 2048)] + [full(packed)] * 4,
        [sds((t, d), bf), sds((t, 2048), bf)] + [sds(packed, bf)] * 4,
        [pltpu.VMEM((512, 2048), bf)] + ffn_scratch(t, d), 15, "ffn_both")(ids, x, g, gain, *parts)


def pack_attn_kernel(ids, q, k, v, o, *refs):
    core = ids[2]
    rows = pl.ds(pl.multiple_of(core * 32, 32), 32)
    out = refs[-1]
    layer = 1
    if len(refs) == 2:
        layer, gains = 0, refs[0]
        pair = [jnp.concatenate([gains[l, 0:1, :], gains[l, 1:2, :]], axis=1).astype(f32) for l in range(2)]
        row = lax.broadcasted_iota(jnp.int32, (32, 128), 0)
        out[:, 1536:] = jnp.where(row == 0, pair[0], jnp.where(row == 1, pair[1], 0.0)).astype(bf)
    for at, w in enumerate((q, k, v)):
        out[:, at * 384:at * 384 + 384] = w[layer, rows, :]
    for i in range(3):
        for j in range(2):
            columns = pl.ds(pl.multiple_of(core * 256 + j * 128, 128), 128)
            out[j * 16:j * 16 + 16, 1152 + i * 128:1280 + i * 128] = o[layer, i * 16:i * 16 + 16, columns]


def pack_ffn_kernel(ids, gate, up, down, *outs):
    core = ids[2]
    rows = pl.ds(pl.multiple_of(core * 32, 32), 32)
    for layer, out in enumerate(outs):
        out[:, :1024] = gate[layer, rows, :]
        out[:, 1024:2048] = up[layer, rows, :]
        for i in range(2):
            out[:, 2048 + i * 512:2560 + i * 512] = (
                down[layer, pl.ds(pl.multiple_of(core * 64 + i * 32, 32), 32), :])


def pack_weights(ids, shards, gains):
    attn, ffn = shards[:4], shards[4:]
    specs = [full(w.shape) for w in attn]
    first = call(pack_attn_kernel, 1, specs + [full(gains.shape)], [full((32, 1664))],
                 [sds((32, 1664), bf)], [], 2, "pack_weights")(ids, *attn, gains)[0]
    third = call(pack_attn_kernel, 1, specs, [full((32, 1536))],
                 [sds((32, 1536), bf)], [], 2, "pack_weights")(ids, *attn)[0]
    second, fourth = call(pack_ffn_kernel, 1, [full(w.shape) for w in ffn], [full((32, 3072))] * 2,
                          [sds((32, 3072), bf)] * 2, [], 2, "pack_weights")(ids, *ffn)
    return first, second, third, fourth


def finish_kernel(ids, own, peer, qw, kw, vw, gw, uw, gain, *refs):
    with_moves = len(refs) > 9
    if with_moves:
        moved, refs, moving_refs = refs[:9], refs[9:18], refs[18:]
        arrive, pass_on, leave = place_moves(ids, moved, *moving_refs)
        arrive()
    q, k, v, o, gate, up, down, gains, table = refs
    first = ids[2] == 0
    base = 0

    def row_sums(*pairs):
        total = None
        for weight, grad in pairs:
            term = weight.astype(f32) * grad
            total = term if total is None else total + term
        ones = jnp.ones((8, total.shape[1]), f32)
        sums = lax.dot_general(ones, total, (((1,), (1,)), ((), ())), preferred_element_type=f32,
                               precision=lax.Precision.HIGHEST)
        return sums[0:1, :]

    for s in (3, 2, 1, 0):
        layer = s // 2
        for core in range(2):
            def part(start, width, rows=slice(0, 32)):
                columns = slice(base + start, base + start + width)
                one, two = own[rows, columns].astype(f32), peer[rows, columns].astype(f32)
                return jnp.where(first, one, two) if core == 0 else jnp.where(first, two, one)

            rows = slice(core * 32, core * 32 + 32)
            if s % 2 == 0:
                for at, w in enumerate((q, k, v)):
                    w[layer, rows, :] = part(at * 384, 384)
                for i in range(3):
                    for j in range(2):
                        o[layer, i * 16:i * 16 + 16, core * 256 + j * 128:core * 256 + j * 128 + 128] = (
                            part(1152 + i * 128, 128, slice(j * 16, j * 16 + 16)))
            else:
                gate[layer, rows, :] = part(0, 1024)
                up[layer, rows, :] = part(1024, 1024)
                for i in range(2):
                    down[layer, core * 64 + i * 32:core * 64 + i * 32 + 32, :] = part(2048 + i * 512, 512)
            if s == 0 and core == 1:
                table[...] = part(1536, 128).T[:6, :]
        if s % 2 == 0:
            sums = row_sums(*((w[layer], grad[layer]) for w, grad in ((qw, q), (kw, k), (vw, v))))
        else:
            sums = row_sums(*((w[layer], grad[layer]) for w, grad in ((gw, gate), (uw, up))))
        gains[layer, s % 2:s % 2 + 1, :] = sums / gain[layer, s % 2:s % 2 + 1, :].astype(f32)
        base += 1536 if s % 2 == 0 else 3072
        if s == 3 and with_moves:
            pass_on()
    if with_moves:
        leave()


def finish(ids, own, peer, shards, gains, shapes, moved=()):
    q, k, v, o, gate, up, down = shards
    args = (own, peer, q, k, v, gate, up, gains)
    anywhere = pl.BlockSpec(memory_space=pl.ANY)
    specs, sizes = [full(array.shape) for array in args], [sds(shape, f32) for shape in shapes]
    out_specs, scratch = [full(shape) for shape in shapes], []
    if moved:
        t, d = moved[0].shape
        specs += [anywhere] * len(moved)
        out_specs.append(anywhere)
        sizes.append(sds((4, t, d), bf))
        scratch = [pltpu.VMEM((4, t, d), bf), pltpu.SemaphoreType.DMA((2, 4))]
    return call(finish_kernel, 1, specs, out_specs, sizes, scratch, 3, "finish")(ids, *args, *moved)


def move(sources, scratch, targets, sems):
    def fetch(ref, at):
        return pltpu.make_async_copy(ref, scratch.at[at], sems.at[0, at])

    def store(at):
        return pltpu.make_async_copy(scratch.at[at], targets[at], sems.at[1, at])

    def arrive():
        for at, options in enumerate(sources):
            for condition, ref in options:
                if condition is None:
                    fetch(ref, at).start()
                else:
                    @pl.when(condition)
                    def _(ref=ref, at=at):
                        fetch(ref, at).start()

    def pass_on():
        for at in range(len(targets)):
            fetch(sources[at][0][1], at).wait()
            store(at).start()

    def leave():
        for at in range(len(targets)):
            store(at).wait()

    return arrive, pass_on, leave


def place_moves(ids, refs, out, scratch, sems):
    own, relay, far = refs[:4], refs[4], refs[5:]
    section = ids[3]
    pick = lambda group: [(section == at, ref) for at, ref in enumerate(group)]
    return move([pick(own), [(None, relay.at[0])], pick(far), [(None, relay.at[1])]], scratch,
                [out.at[section ^ bit] for bit in range(4)], sems)


def place_kernel(ids, *refs):
    for part in place_moves(ids, refs[:9], *refs[9:]):
        part()


def moving(kernel, ids, arrays, out_shape, slots, micros, name):
    anywhere = pl.BlockSpec(memory_space=pl.ANY)
    t, d = arrays[0].shape[-2:]
    return pl.pallas_call(
        kernel,
        grid_spec=pltpu.PrefetchScalarGridSpec(
            num_scalar_prefetch=1, grid=(1,), in_specs=[anywhere] * len(arrays), out_specs=anywhere,
            scratch_shapes=[pltpu.VMEM((slots, t, d), bf), pltpu.SemaphoreType.DMA((2, slots))]),
        out_shape=out_shape, name=name,
        compiler_params=pltpu.CompilerParams(vmem_limit_bytes=vmem_mib[name] << 20),
        cost_estimate=pl.CostEstimate(flops=int(micros * 1.1e9), bytes_accessed=0, transcendentals=0),
    )(ids, *arrays)


def place(ids, own, relay, far):
    return moving(place_kernel, ids, (*own, relay, *far), sds((4,) + own[0].shape, bf), 4, 3, "place")


def relay_kernel(ids, *refs):
    own, far = refs[:4], refs[4:8]
    out, scratch, sems = refs[8:]
    pick = lambda group: [((ids[3] ^ 1) == at, ref) for at, ref in enumerate(group)]
    for part in move([pick(own), pick(far)], scratch, [out.at[0], out.at[1]], sems):
        part()


def relay(ids, own, far):
    t, d = own[0].shape
    both = moving(relay_kernel, ids, (*own, *far), sds((2, t, d), bf), 2, 2, "relay")
    return swapped(both, "section", 1)


def z_shift(values, by):
    half = lax.axis_size("dp") // 2
    pairs = [(z * 2 + y, ((z + by) % half) * 2 + y) for z in range(half) for y in range(2)]
    return lax.ppermute(values, "dp", pairs)


def swapped(values, axis, bit):
    return lax.ppermute(values, axis, [(i, i ^ bit) for i in range(lax.axis_size(axis))])


def after(values, *others):
    return lax.optimization_barrier((values,) + others)[0]


def added(*terms):
    total = terms[0].astype(f32)
    for term in terms[1:]:
        total = total + term.astype(f32)
    return total.astype(bf)


def gather_part(piece, z, previous):
    if previous is not None:
        piece = after(piece, *previous)
    got = [z_shift(piece, by) for by in range(1, 4)]
    column = jnp.stack([lax.select_n((z - at) % 4, piece, *got) for at in range(4)])
    return (column, swapped(column, "dp", 1)), got


def gather_core(column, other, *holds):
    if holds:
        column, other = lax.optimization_barrier((column, other) + holds)[:2]
    return column, other, swapped(column, "section", 1), swapped(other, "section", 1)


def reduce_first(own, other, give_own, give_other, straight, hold=None):
    first = swapped(give_other, "section", 1)
    sent = swapped(added(other, first), "dp", 1)
    got = swapped(give_own, "section", 1)
    step = dict(keep=own, first=first, core=got, y=sent)
    if straight:
        step["terms"] = [added(own[by], got[by], sent[by]) for by in range(4)]
    else:
        step["far"] = swapped(added(own[2:], got[2:], sent[2:] if hold is None else after(sent[2:], hold)), "dp", 2)
    return step


def xor_shift(values, z_bits):
    return swapped(values, "dp", 2 * z_bits)


def reduce_near(step):
    terms = (step["keep"][1], step["core"][1], step["y"][1], step["far"][1])
    return swapped(added(*terms), "dp", 4)


def reduce_last(step):
    if "terms" in step:
        return added(step["terms"][0], *step["near"])
    return added(step["keep"][0], step["core"][0], step["y"][0], step["far"][0], step["near"])


def to_packed(q, k, v, o, gate, up, down):
    o_part = o.reshape(8, 3, 16, 2, 2, 128).transpose(0, 3, 4, 2, 1, 5).reshape(512, 384)
    d_part = down.reshape(16, 2, 32, 512).transpose(0, 2, 1, 3).reshape(512, 1024)
    return jnp.concatenate([q, k, v, o_part], axis=1), jnp.concatenate([gate, up, d_part], axis=1)


def from_packed(attn, ffn):
    q, k, v = (attn[:, at * 384:at * 384 + 384] for at in range(3))
    o = attn[:, 1152:1536].reshape(8, 2, 2, 16, 3, 128).transpose(0, 4, 3, 1, 2, 5).reshape(384, 512)
    down = ffn[:, 2048:].reshape(16, 32, 2, 512).transpose(0, 2, 1, 3).reshape(1024, 512)
    return q, k, v, o, ffn[:, :1024], ffn[:, 1024:2048], down


def parts_of(whole):
    split = whole.reshape(4, 2, 2, 32, whole.shape[1])
    return tuple(split[:, y, core] for core in range(2) for y in range(2))


def whole_of(parts):
    parts = [part[..., :1536] if part.shape[2] == 1664 else part for part in parts]
    parts = [jnp.stack([part[by] for by in z_order]) for part in parts]
    split = jnp.stack(parts).reshape(2, 2, 4, 32, -1).transpose(2, 1, 0, 3, 4)
    return split.reshape(512, -1)


def gains_of(column, other, y):
    small = [part[:, :2, 1536:1664].reshape(4, 2, 2, 64) for part in (column, other)]
    pair = [jnp.where(y == at, small[0], small[1]) for at in range(2)]
    return jnp.stack(pair, axis=3).transpose(1, 2, 0, 3, 4).reshape(2, 2, 512).astype(f32)


def body(inputs, cotangent, segments, observed, q_weight, k_weight, v_weight, o_weight,
         gate_weight, up_weight, down_weight, gains, position_table):
    section = lax.axis_index("section")
    dp = lax.axis_index("dp")
    micro_count, row_count, seq_count, width = inputs.shape
    layers = q_weight.shape[0]
    heads = position_table.shape[1]
    tokens = row_count * seq_count
    shards = (q_weight, k_weight, v_weight, o_weight, gate_weight, up_weight, down_weight)
    eight = lax.axis_size("dp") == 8
    own_ids = jnp.stack([dp // 2, dp % 2, section % 2, section]).astype(jnp.int32)
    ids = own_ids if eight else jnp.stack([0 * dp, 0 * dp, 0 * dp, section]).astype(jnp.int32)

    weights = [None] * 4
    if eight:
        pieces = pack_weights(own_ids, shards, gains)
    else:
        whole = [lax.all_gather(w, "dp", axis=1, tiled=True) for w in shards]
        for layer in range(layers):
            weights[2 * layer], weights[2 * layer + 1] = (
                parts_of(w) for w in to_packed(*(w[layer] for w in whole)))
        gains_all = lax.all_gather(gains, "dp", axis=2, tiled=True).astype(f32)

    x = inputs.reshape(micro_count, tokens, width)
    grad = cotangent.reshape(micro_count, tokens, width)
    seg = lax.dynamic_index_in_dim(segments, section, 0, keepdims=False)
    obs = lax.dynamic_index_in_dim(observed, section, 0, keepdims=False)
    allowed = (seg[:, :, None] == seg[:, None, :]) & (obs[:, :, None] == 1)
    mask = jnp.where(allowed, 0.0, masked).astype(f32)
    mask = jnp.concatenate([mask, mask], axis=2)
    position = jnp.arange(seq_count, dtype=jnp.int32)
    bucket = bucket_of(position[:, None], position[None, :])
    onehot = (bucket[:, :, None] == jnp.arange(position_table.shape[0])[None, None, :]).astype(f32)
    bias = jnp.einsum("jib,bh->jhi", onehot, position_table.astype(f32), precision=lax.Precision.HIGHEST)
    bias = bias.reshape(seq_count, heads * seq_count)

    chip = section // 2

    def across(value, pairs):
        return lax.ppermute(value, "section", pairs)

    arrived = [()] * 4
    if eight:
        previous = None
        for s in range(4):
            weights[s], previous = gather_part(pieces[s], dp // 2, previous)
            arrived[s] = previous
            if s == 1:
                previous = previous + [weights[0][1]]
            if s == 1:
                previous = previous + [weights[0][1]]
            if s == 1:
                previous = previous + [weights[0][1]]
        gains_all = gains_of(*weights[0], dp % 2)

    chip = section // 2

    def both_ways(first, second):
        return swapped(jnp.where(chip == 0, first, second), "section", 2)

    def wait(value, *names):
        others = [steps[s][name] for s, name in names] if eight else []
        return after(value, *others) if others else value

    chip = section // 2

    def both_ways(first, second):
        return swapped(jnp.where(chip == 0, first, second), "section", 2)

    moved = {}

    def wait(value, *names):
        others = [moved[name] for name in names if name in moved]
        return after(value, *others) if others else value

    def gain_of(s):
        return gains_all[s // 2, s % 2][None]

    packed, steps = [None] * 4, [None] * 4

    def passed(s, parts):
        if eight:
            if s == 2:
                parts = list(parts)
                parts[1] = wait(parts[1], *("y3", ))
            for at, names in ((1, ("far3", "y2", "x2", )), (0, ("near3", ))):
                if s == at:
                    parts[3] = wait(parts[3], *names)
            hold = [moved[name] for name in () if s == 0 and name in moved]
            steps[s] = reduce_first(*parts, s in (), *hold)
            moved.update({f"{name}{s}": steps[s][name] for name in ("first", "core", "y", "far") if name in steps[s]})
        else:
            packed[s] = whole_of(parts)

    states, kept = [x], []
    outs, grads, out_far, grad_far = [None] * 4, [None] * 4, [None] * 4, [None] * 4
    for s in range(4):
        feed = states[s]
        if eight:
            if s < 3:
                feed = after(feed, *arrived[s + 1])
            holds = [states[s]] if s in (1, 3) else []
            holds += [weights[at][1] for to, at in ((1, 2),) if to == s]
            weights[s] = gather_core(*weights[s], *holds)
        if s == 3:
            outs[3], last_back, *parts = ffn_both(ids, feed, grad, gain_of(3), weights[3])
            break
        if s % 2 == 0:
            out, *saved = attn_fwd(ids, feed, mask, bias, gain_of(s), weights[s])
        else:
            out, *saved = ffn_fwd(ids, feed, gain_of(s), weights[s])
        states.append(out)
        kept.append(saved)
        outs[s] = out
    out_far[0] = out_far[2] = moved["x1"] = both_ways(outs[2], outs[0])
    passed(3, parts)

    bias_sum = jnp.zeros((seq_count, heads * seq_count), f32)
    grads[3] = grad = input_grad(ids, states[3], last_back, grad, gain_of(3), weights[3], 20)
    out_far[1] = grad_far[3] = moved["x2"] = both_ways(grad, outs[1])
    back, *parts, bias_sum = attn_bwd(
        ids, states[2], *kept[2], wait(grad, "first3", "x1"), gain_of(2), weights[2], bias_sum, False)
    passed(2, parts)
    grads[2] = grad = input_grad(
        ids, states[2], back, grad, gain_of(2), weights[2], 20)
    grads[1], *parts = ffn_bwd(
        ids, states[1], *kept[1], wait(grad, "first2", "y3"), gain_of(1), weights[1])
    passed(1, parts)
    grad = grads[1]
    if eight and 3 in (3,):
        steps[3]["near"] = moved["near3"] = reduce_near(steps[3])
    out_far[3] = grad_far[1] = moved["x3"] = both_ways(outs[3], grad)
    grads[0], *parts, bias_sum = attn_bwd(
        ids, states[0], *kept[0], wait(grad, "first1", "y2", "x2"), gain_of(0), weights[0], bias_sum, True)
    passed(0, parts)
    moved["g0"] = grads[0]
    grad_far[0] = grad_far[2] = moved["x4"] = both_ways(grads[2], wait(grads[0], "x3", "y1"))

    shape = (1, micro_count, row_count, seq_count, width)
    out_relay = relay(ids, outs, out_far[:3] + [wait(out_far[3], "y0")])
    section_outputs = moved["placed"] = place(ids, outs, out_relay, out_far)
    if eight:
        for s, names in ((3, ("y1", )), (2, ("y0", )), (1, ()), (0, ())):
            if "near" in steps[s]:
                continue
            if s in ():
                terms = steps[s]["terms"]
                steps[s]["near"] = [
                    xor_shift(wait(terms[by], *names), z_order[by]) for by in (1, 2, 3)]
                moved[f"near{s}"] = steps[s]["near"][-1]
                continue
            steps[s]["far"] = wait(steps[s]["far"], *names)
            steps[s]["near"] = moved[f"near{s}"] = reduce_near(steps[s])
    grad_relay = moved["relayed"] = relay(ids, grads, grad_far)
    grad_pieces = (*grads, grad_relay, *grad_far)
    section_outputs = section_outputs.reshape(shape)

    if eight:
        own = []
        for group in ((3, 2), (1, 0)):
            both = jnp.concatenate([reduce_last(steps[s]) for s in group], axis=1)
            own.append(added(both, swapped(both, "section", 2)))
        own = jnp.concatenate(own, axis=1)
        shapes = [w.shape for w in shards] + [gains.shape, position_table.shape[::-1]]
        peer = swapped(own, "section", 1)
        *final, table, section_grads = finish(ids, own, peer, shards, gains, shapes, grad_pieces)
        return (section_outputs, section_grads.reshape(shape)) + tuple(final) + (table.T,)

    section_grads = place(ids, grads, grad_relay, grad_far).reshape(shape)
    dense = [from_packed(packed[2 * layer], packed[2 * layer + 1]) for layer in range(layers)]
    final = []
    for at in range(7):
        both = jnp.stack([d[at] for d in dense])
        part = lax.psum_scatter(both, "dp", scatter_dimension=1, tiled=True)
        final.append(lax.psum(part, "section").astype(f32))
    terms = [w.astype(f32) * final[at] for at, w in enumerate(shards)]
    gain_sums = [sum(jnp.sum(terms[at], axis=2) for at in group) for group in ((0, 1, 2), (4, 5))]
    gains_grad = jnp.stack(gain_sums, axis=1) / gains.astype(f32)
    bias_sum = bias_sum.reshape(seq_count, heads, seq_count)
    table = jnp.einsum("jib,jhi->bh", onehot, bias_sum, precision=lax.Precision.HIGHEST)
    return (section_outputs, section_grads) + tuple(final) + (gains_grad, lax.psum(table, ("section", "dp")))


def solution(mesh):
    rows4 = P(None, "dp", None, None)
    rows3 = P(None, "dp", None)
    staged = P("section", None, "dp", None, None)
    return jax.shard_map(
        body,
        mesh=mesh,
        in_specs=(rows4, rows4) + (rows3,) * 9 + (P(None, None, "dp"), P()),
        out_specs=(staged, staged) + (rows3,) * 7 + (P(None, None, "dp"), P()),
        check_vma=False,
    )
```

```python
from functools import partial
import jax
import jax.numpy as jnp
from jax import lax
from jax.experimental import pallas as pl
from jax.experimental.pallas import tpu as pltpu
from jax.sharding import PartitionSpec as P

eps_norm = 1e-06
limits = (12, 16, 23, 32, 46, 64, 91)
masked = -1e30
bf = jnp.bfloat16
f32 = jnp.float32
vmem_mib = dict(
    attn_fwd=56, ffn_fwd=40, ffn_both=38, ffn_bwd=33, attn_front=34,
    attn_whole=28, attn_bwd=22, input_grad=12, pack_weights=56, finish=20, place=9, relay=6)


def dot_nn(a, b):
    return lax.dot_general(a, b, (((1,), (0,)), ((), ())), preferred_element_type=f32)


def dot_nt(a, b):
    return lax.dot_general(a, b, (((1,), (1,)), ((), ())), preferred_element_type=f32)


def dot_tn(a, b):
    return lax.dot_general(a, b, (((0,), (0,)), ((), ())), preferred_element_type=f32)


def row_scale(x):
    return lax.rsqrt(jnp.mean(x * x, axis=-1, keepdims=True) + eps_norm)


def pair_parts(values):
    lane = lax.broadcasted_iota(jnp.int32, values.shape, 1)
    zero = jnp.zeros_like(values)
    return jnp.concatenate(
        [jnp.where(lane < 64, values, zero), jnp.where(lane < 64, zero, values)], axis=0
    )


def pair_pick(values):
    half = values.shape[0] // 2
    lane = lax.broadcasted_iota(jnp.int32, (half, values.shape[1]), 1)
    return jnp.where(lane < 64, values[:half], values[half:])


blocks = 16
block_rows = 32


def order_of(ids, z, other_y, other_core):
    return (z * 2 + (ids[1] ^ other_y)) * 2 + (ids[2] ^ other_core)


def open_attn(ids, parts, wqkv, wo):
    for at, ref in enumerate(parts):
        other_y, other_core = at % 2, at // 2
        for z in range(4):
            place = order_of(ids, z, other_y, other_core)
            if wqkv is not None:
                wqkv[pl.ds(pl.multiple_of(place * 32, 32), 32), :] = ref[z, :, :1152]
            shard = z * 2 + (ids[1] ^ other_y)
            core = ids[2] ^ other_core
            for i in range(3):
                rows = pl.ds(pl.multiple_of(shard * 48 + i * 16, 16), 16)
                for j in range(2):
                    columns = pl.ds(pl.multiple_of(core * 256 + j * 128, 128), 128)
                    wo[rows, columns] = ref[z, j * 16:j * 16 + 16, 1152 + i * 128:1280 + i * 128]


def open_ffn(ids, parts, wgu, wd):
    for at, ref in enumerate(parts):
        other_y, other_core = at % 2, at // 2
        for z in range(4):
            place = order_of(ids, z, other_y, other_core)
            if wgu is not None:
                wgu[pl.ds(pl.multiple_of(place * 32, 32), 32), :] = ref[z, :, :2048]
            for i in range(2):
                wd[pl.ds(pl.multiple_of(place * 64 + i * 32, 32), 32), :] = (
                    ref[z, :, 2048 + i * 512:2560 + i * 512])


def open_columns(ids, parts, matrix):
    for at, ref in enumerate(parts):
        for z in range(4):
            place = order_of(ids, z, at % 2, at // 2)
            matrix[pl.ds(pl.multiple_of(place * 32, 32), 32), :] = ref[z, :, :matrix.shape[1]]


z_order = (0, 2, 1, 3)


def hand_out(ids, packed, refs):
    for at, ref in enumerate(refs):
        for by in range(4):
            place = order_of(ids, ids[0] ^ z_order[by], at % 2, at // 2)
            ref[by] = packed[pl.ds(pl.multiple_of(place * 32, 32), 32), :]


def attn_fwd_kernel(ids, x_ref, mask_ref, bias_ref, gain_ref, w0, w1, w2, w3,
                    out_ref, q_ref, k_ref, v_ref, p_ref, att_ref, wqkv, wo):
    @pl.when(pl.program_id(0) == 0)
    def _():
        open_attn(ids, (w0, w1, w2, w3), wqkv, wo)

    x = x_ref[...].astype(f32)
    a = (x * row_scale(x) * gain_ref[...]).astype(bf)
    q = dot_nn(a, wqkv[:, :384]).astype(bf)
    k = dot_nn(a, wqkv[:, 384:768]).astype(bf)
    v = dot_nn(a, wqkv[:, 768:]).astype(bf)
    q_ref[...] = q
    k_ref[...] = k
    v_ref[...] = v
    rows = x.shape[0] // 64
    units = [(r, h) for r in range(rows) for h in range(3)]
    at = lambda arr, r, h: arr[r * 64:r * 64 + 64, h * 128:h * 128 + 128]
    scores = [dot_nt(at(k, r, h), pair_parts(at(q, r, h))) for r, h in units]
    probs = []
    for (r, h), s in zip(units, scores):
        s = s + (bias_ref[:, h * 128:h * 128 + 128] + mask_ref[r])
        e = jnp.exp(s - jnp.max(s, axis=0, keepdims=True))
        p = (e * (1.0 / jnp.sum(e, axis=0, keepdims=True))).astype(bf)
        p_ref[r * 64:r * 64 + 64, h * 128:h * 128 + 128] = p
        probs.append(p)
    full_att = [dot_tn(p, at(v, r, h)) for (r, h), p in zip(units, probs)]
    att = {unit: pair_pick(part).astype(bf) for unit, part in zip(units, full_att)}
    att = jnp.concatenate(
        [jnp.concatenate([att[r, h] for h in range(3)], axis=1) for r in range(rows)], axis=0)
    att_ref[...] = att
    out_ref[...] = (x + dot_nn(att, wo[...])).astype(bf)


def normed(x_ref, gain_ref):
    x = x_ref[...].astype(f32)
    return (x * row_scale(x) * gain_ref[...]).astype(bf)


def norm_back(x_ref, gain_ref, gx, g_low):
    x = x_ref[...].astype(f32)
    scale = row_scale(x)
    n = x * scale
    e = gx * gain_ref[...]
    dx = scale * (e - n * jnp.mean(e * n, axis=-1, keepdims=True))
    return (g_low.astype(f32) + dx).astype(bf), (n * gain_ref[...]).astype(bf)


def input_grad_kernel(ids, x_ref, back_ref, g_ref, gain_ref, w0, w1, w2, w3, gin_ref, w_s):
    @pl.when(pl.program_id(0) == 0)
    def _():
        open_columns(ids, (w0, w1, w2, w3), w_s)

    gin_ref[...] = norm_back(x_ref, gain_ref, dot_nt(back_ref[...], w_s[...]), g_ref[...])[0]


def bucket_of(key, query):
    offset = key - query
    distance = jnp.abs(offset)
    far = jnp.full(distance.shape, 8, jnp.int32)
    for threshold in limits:
        far = far + (distance >= threshold).astype(jnp.int32)
    near = jnp.where(distance < 8, distance, jnp.minimum(far, 15))
    return near + 16 * (offset > 0).astype(jnp.int32)


def table_terms(bias_grad):
    key = lax.broadcasted_iota(jnp.int32, (64, 128), 0)
    query = lax.broadcasted_iota(jnp.int32, (64, 128), 1) & 63
    bucket = bucket_of(key, query)
    pieces = [bias_grad[:, h * 128:h * 128 + 128] for h in range(3)]
    sums = [[], [], []]
    for b in range(32):
        hit = bucket == b
        for h in range(3):
            sums[h].append(jnp.sum(jnp.where(hit, pieces[h], 0.0), axis=0, keepdims=True))
    lane = lax.broadcasted_iota(jnp.int32, (32, 128), 1)
    table = jnp.zeros((32, 128), f32)
    for h in range(3):
        part = jnp.concatenate(sums[h], axis=0)
        low = jnp.sum(jnp.where(lane < 64, part, 0.0), axis=1, keepdims=True)
        high = jnp.sum(jnp.where(lane < 64, 0.0, part), axis=1, keepdims=True)
        table = jnp.where(lane == 2 * h, low, jnp.where(lane == 2 * h + 1, high, table))
    return table


def attn_bwd_kernel(front, whole, ids, x_ref, q_ref, k_ref, v_ref, p_ref, att_ref, g_ref, gain_ref,
                    w0, w1, w2, w3, bias_in, *refs):
    refs = list(refs)
    if front:
        next_x, next_back, next_gain, n0, n1, n2, n3, *refs = refs
        grad_ref, *refs = refs
        next_w = refs.pop()
    if whole:
        wqkv = refs.pop()
    back_ref, r0, r1, r2, r3, dbias_ref, wo, a_s, dqkv_s, att_s, g_s, dbias_s, packed = refs
    step = pl.program_id(0)
    last = pl.num_programs(0) - 1
    block = x_ref.shape[0]
    with_table = r0.shape[2] > 1536

    @pl.when(step == 0)
    def _():
        open_attn(ids, (w0, w1, w2, w3), wqkv if whole else None, wo)
        if front:
            open_columns(ids, (n0, n1, n2, n3), next_w)
        dbias_s[...] = bias_in[...]

    here = pl.ds(pl.multiple_of(step * block, block), block)
    g_low = g_ref[...]
    if front:
        g_low = norm_back(next_x, next_gain, dot_nt(next_back[...], next_w[...]), g_low)[0]
        grad_ref[...] = g_low
    da = dot_nt(g_low, wo[...]).astype(bf)
    att_s[here, :] = att_ref[...]
    g_s[here, :] = g_low
    rows = block // 64
    units = [(r, h) for r in range(rows) for h in range(3)]
    at = lambda arr, r, h: arr[r * 64:r * 64 + 64, h * 128:h * 128 + 128]
    db = [None] * 3
    da_bds = [pair_parts(at(da, r, h)) for r, h in units]
    dps = [dot_nt(at(v_ref, r, h), da_bd) for (r, h), da_bd in zip(units, da_bds)]
    dv_u = {(r, h): dot_nn(at(p_ref, r, h), da_bd).astype(bf) for (r, h), da_bd in zip(units, da_bds)}
    dss = []
    for (r, h), dp in zip(units, dps):
        pf = at(p_ref, r, h).astype(f32)
        ds = pf * (dp - jnp.sum(pf * dp, axis=0, keepdims=True))
        db[h] = ds if db[h] is None else db[h] + ds
        dss.append(ds.astype(bf))
    dk_u = {(r, h): dot_nn(ds, pair_parts(at(q_ref, r, h))).astype(bf) for (r, h), ds in zip(units, dss)}
    full_dq = [dot_tn(ds, at(k_ref, r, h)) for (r, h), ds in zip(units, dss)]
    dq_u = {unit: pair_pick(part).astype(bf) for unit, part in zip(units, full_dq)}
    dqkv = jnp.concatenate(
        [jnp.concatenate([u[r, h] for u in (dq_u, dk_u, dv_u) for h in range(3)], axis=1)
         for r in range(rows)], axis=0)
    dqkv_s[here, :] = dqkv
    for h in range(3):
        dbias_s[:, h * 128:h * 128 + 128] += db[h]
    if whole:
        back_ref[...], a_s[here, :] = norm_back(x_ref, gain_ref, dot_nt(dqkv, wqkv[...]), g_low)
    else:
        back_ref[...] = dqkv
        a_s[here, :] = normed(x_ref, gain_ref)

    @pl.when(step == last)
    def _():
        for h in range(3):
            columns = slice(h * 384, h * 384 + 384)
            packed[:, columns] = dot_tn(a_s[...], dqkv_s[:, columns]).astype(bf)
        dwo = dot_tn(att_s[...], g_s[...]).astype(bf)
        for shard in range(8):
            for core in range(2):
                for i in range(3):
                    for j in range(2):
                        packed[(shard * 2 + core) * 32 + j * 16:(shard * 2 + core) * 32 + j * 16 + 16,
                               1152 + i * 128:1280 + i * 128] = (
                            dwo[shard * 48 + i * 16:shard * 48 + i * 16 + 16,
                                core * 256 + j * 128:core * 256 + j * 128 + 128])
        dbias_ref[...] = dbias_s[...]
        if with_table:
            table = table_terms(dbias_s[...]).astype(bf)
            for at in range(16):
                packed[at * 32:at * 32 + 32, 1536:1664] = table
        hand_out(ids, packed, (r0, r1, r2, r3))


def gelu_parts(u):
    c = 0.7978845608028654
    u2 = u * u
    t = jnp.tanh(u * (c + (c * 0.044715) * u2))
    half = 0.5 + 0.5 * t
    act = u * half
    slope = half + (0.5 * u) * (1.0 - t * t) * (c + (3.0 * c * 0.044715) * u2)
    return act, slope


def gelu(u):
    c = 0.7978845608028654
    t = jnp.tanh(u * (c + (c * 0.044715) * (u * u)))
    return u * (0.5 + 0.5 * t)


def ffn_fwd_kernel(ids, x_ref, gain_ref, w0, w1, w2, w3, out_ref, gate_ref, up_ref, wgu, wd):
    @pl.when(pl.program_id(0) == 0)
    def _():
        open_ffn(ids, (w0, w1, w2, w3), wgu, wd)

    x = x_ref[...].astype(f32)
    a = (x * row_scale(x) * gain_ref[...]).astype(bf)
    gate = dot_nn(a, wgu[:, :1024])
    up = dot_nn(a, wgu[:, 1024:])
    gate_ref[...] = gate.astype(bf)
    up_ref[...] = up.astype(bf)
    hidden = (gelu(gate) * up).astype(bf)
    out_ref[...] = (x + dot_nn(hidden, wd[...])).astype(bf)


def ffn_weight_grads(ids, a_s, gub_s, hid_s, g_s, packed, refs):
    for h in range(4):
        columns = slice(h * 512, h * 512 + 512)
        packed[:, columns] = dot_tn(a_s[...], gub_s[:, columns]).astype(bf)
    for h in range(2):
        dwd = dot_tn(hid_s[:, h * 512:h * 512 + 512], g_s[...]).astype(bf)
        for at in range(8):
            for i in range(2):
                packed[(h * 8 + at) * 32:(h * 8 + at) * 32 + 32, 2048 + i * 512:2560 + i * 512] = (
                    dwd[at * 64 + i * 32:at * 64 + i * 32 + 32])
    hand_out(ids, packed, refs)


def ffn_bwd_kernel(ids, x_ref, gate_ref, up_ref, g_ref, gain_ref, w0, w1, w2, w3,
                   gin_ref, r0, r1, r2, r3, wgu, wd, a_s, gub_s, hid_s, g_s, packed):
    step = pl.program_id(0)
    block = x_ref.shape[0]

    @pl.when(step == 0)
    def _():
        open_ffn(ids, (w0, w1, w2, w3), wgu, wd)

    here = pl.ds(pl.multiple_of(step * block, block), block)
    g_low = g_ref[...]
    g_s[here, :] = g_low
    hg = dot_nt(g_low, wd[...])
    gate = gate_ref[...].astype(f32)
    up = up_ref[...].astype(f32)
    act, slope = gelu_parts(gate)
    hid_s[here, :] = (act * up).astype(bf)
    gb = (hg * up * slope).astype(bf)
    ub = (hg * act).astype(bf)
    gub_s[here, :1024] = gb
    gub_s[here, 1024:] = ub
    gx = dot_nt(gb, wgu[:, :1024]) + dot_nt(ub, wgu[:, 1024:])
    gin_ref[...], a_s[here, :] = norm_back(x_ref, gain_ref, gx, g_low)

    @pl.when(step == pl.num_programs(0) - 1)
    def _():
        ffn_weight_grads(ids, a_s, gub_s, hid_s, g_s, packed, (r0, r1, r2, r3))


def ffn_both_kernel(ids, x_ref, g_ref, gain_ref, w0, w1, w2, w3,
                    out_ref, back_ref, r0, r1, r2, r3, wgu, wd, a_s, gub_s, hid_s, g_s, packed):
    step = pl.program_id(0)
    block = x_ref.shape[0]

    @pl.when(step == 0)
    def _():
        open_ffn(ids, (w0, w1, w2, w3), wgu, wd)

    here = pl.ds(pl.multiple_of(step * block, block), block)
    x = x_ref[...].astype(f32)
    a = (x * row_scale(x) * gain_ref[...]).astype(bf)
    gate = dot_nn(a, wgu[:, :1024])
    up = dot_nn(a, wgu[:, 1024:])
    g_low = g_ref[...]
    g_s[here, :] = g_low
    hg = dot_nt(g_low, wd[...])
    act, slope = gelu_parts(gate)
    hidden = (act * up).astype(bf)
    hid_s[here, :] = hidden
    out_ref[...] = (x + dot_nn(hidden, wd[...])).astype(bf)
    gb = (hg * up * slope).astype(bf)
    ub = (hg * act).astype(bf)
    gub_s[here, :1024] = gb
    gub_s[here, 1024:] = ub
    back_ref[:, :1024] = gb
    back_ref[:, 1024:] = ub
    a_s[here, :] = a

    @pl.when(step == pl.num_programs(0) - 1)
    def _():
        ffn_weight_grads(ids, a_s, gub_s, hid_s, g_s, packed, (r0, r1, r2, r3))


def tok(block, width):
    return pl.BlockSpec((block, width), lambda i, ids: (i, 0))


def picked(block, width):
    return pl.BlockSpec((None, block, width), lambda i, ids: (ids[3], i, 0))


def tokens_of(array, block):
    return (tok if array.ndim == 2 else picked)(block, array.shape[-1])


def full(shape):
    zero = (0,) * len(shape)
    return pl.BlockSpec(shape, lambda i, ids: zero)


def sds(shape, dtype):
    return jax.ShapeDtypeStruct(shape, dtype)


def call(kernel, grid, in_specs, out_specs, out_shape, scratch, micros, name):
    return pl.pallas_call(
        kernel,
        grid_spec=pltpu.PrefetchScalarGridSpec(
            num_scalar_prefetch=1, grid=(grid,), in_specs=in_specs, out_specs=out_specs,
            scratch_shapes=scratch),
        out_shape=out_shape, name=name,
        compiler_params=pltpu.CompilerParams(vmem_limit_bytes=vmem_mib[name] << 20),
        cost_estimate=pl.CostEstimate(flops=int(micros * 1.1e9), bytes_accessed=0, transcendentals=0),
    )


token_block = 512


def attn_fwd(ids, x, mask, bias, gain, parts):
    t, d = x.shape[-2:]
    block = token_block
    return call(
        attn_fwd_kernel, t // block,
        [tokens_of(x, block), pl.BlockSpec((block // 64, 64, 128), lambda i, ids: (i, 0, 0)),
         full(bias.shape), full((1, d))] + [full(parts[0].shape)] * 4,
        [tok(block, d)] + [tok(block, 384)] * 5,
        [sds((t, d), bf)] + [sds((t, 384), bf)] * 5,
        [pltpu.VMEM((512, 1152), bf), pltpu.VMEM((384, 512), bf)],
        15, "attn_fwd")(ids, x, mask, bias, gain, *parts)


def attn_bwd(ids, x, q, k, v, p, att, g, gain, parts, bias_in, whole, ahead=None, table=False):
    t, d = x.shape[-2:]
    block = token_block
    packed = (4, 32, 1664 if whole or table else 1536)
    width = d if whole else 1152
    args = [x, q, k, v, p, att, g, gain, *parts, bias_in]
    specs = ([tokens_of(x, block)] + [tok(block, 384)] * 5 + [tokens_of(g, block), full((1, d))]
             + [full(parts[0].shape)] * 4 + [full(bias_in.shape)])
    out_specs = [tok(block, width)] + [full(packed)] * 4 + [full((64, 384))]
    sizes = [sds((t, width), bf)] + [sds(packed, bf)] * 4 + [sds((64, 384), f32)]
    scratch = [pltpu.VMEM((384, 512), bf), pltpu.VMEM((t, d), bf), pltpu.VMEM((t, 1152), bf),
               pltpu.VMEM((t, 384), bf), pltpu.VMEM((t, d), bf), pltpu.VMEM((64, 384), f32),
               pltpu.VMEM((512, packed[2]), bf)]
    if whole:
        scratch.append(pltpu.VMEM((512, 1152), bf))
    if ahead is not None:
        next_x, next_back, next_gain, next_parts = ahead
        args += [next_x, next_back, next_gain, *next_parts]
        specs += [tok(block, d), tok(block, 2048), full((1, d))] + [columns_of(next_parts[0], 2048)] * 4
        out_specs.insert(0, tok(block, d))
        sizes.insert(0, sds((t, d), bf))
        scratch.append(pltpu.VMEM((512, 2048), bf))
    kernel = partial(attn_bwd_kernel, ahead is not None, whole)
    return call(kernel, t // block, specs, out_specs, sizes, scratch,
                15 if ahead is not None else 20 if whole else 9, "attn_front" if ahead is not None else "attn_whole" if whole else "attn_bwd")(ids, *args)


def columns_of(part, width):
    return pl.BlockSpec((4, part.shape[1], width), lambda i, ids: (0, 0, 0))


def input_grad(ids, x, back, g, gain, parts, micros):
    t, d = x.shape[-2:]
    block = token_block
    width = back.shape[1]
    part = columns_of(parts[0], width)
    return call(
        input_grad_kernel, t // block,
        [tokens_of(x, block), tok(block, width), tokens_of(g, block), full((1, d))] + [part] * 4,
        [tok(block, d)], [sds((t, d), bf)], [pltpu.VMEM((512, width), bf)],
        micros, "input_grad")(ids, x, back, g, gain, *parts)[0]


def ffn_fwd(ids, x, gain, parts):
    t, d = x.shape
    block = token_block
    return call(
        ffn_fwd_kernel, t // block,
        [tok(block, d), full((1, d))] + [full(parts[0].shape)] * 4,
        [tok(block, d), tok(block, 1024), tok(block, 1024)],
        [sds((t, d), bf), sds((t, 1024), bf), sds((t, 1024), bf)],
        [pltpu.VMEM((512, 2048), bf), pltpu.VMEM((1024, 512), bf)],
        0.3, "ffn_fwd")(ids, x, gain, *parts)


def ffn_scratch(t, d):
    return [pltpu.VMEM((1024, 512), bf), pltpu.VMEM((t, d), bf),
            pltpu.VMEM((t, 2048), bf), pltpu.VMEM((t, 1024), bf), pltpu.VMEM((t, d), bf),
            pltpu.VMEM((512, 3072), bf)]


def ffn_bwd(ids, x, gate, up, g, gain, parts):
    t, d = x.shape
    block = token_block
    packed = (4, 32, 3072)
    return call(
        ffn_bwd_kernel, t // block,
        [tok(block, d), tok(block, 1024), tok(block, 1024), tok(block, d), full((1, d))]
        + [full(parts[0].shape)] * 4,
        [tok(block, d)] + [full(packed)] * 4,
        [sds((t, d), bf)] + [sds(packed, bf)] * 4,
        [pltpu.VMEM((512, 2048), bf)] + ffn_scratch(t, d), 12, "ffn_bwd")(ids, x, gate, up, g, gain, *parts)


def ffn_both(ids, x, g, gain, parts):
    t, d = x.shape
    block = token_block
    packed = (4, 32, 3072)
    return call(
        ffn_both_kernel, t // block,
        [tok(block, d), tokens_of(g, block), full((1, d))] + [full(parts[0].shape)] * 4,
        [tok(block, d), tok(block, 2048)] + [full(packed)] * 4,
        [sds((t, d), bf), sds((t, 2048), bf)] + [sds(packed, bf)] * 4,
        [pltpu.VMEM((512, 2048), bf)] + ffn_scratch(t, d), 15, "ffn_both")(ids, x, g, gain, *parts)


def pack_attn_kernel(ids, q, k, v, o, *refs):
    core = ids[2]
    rows = pl.ds(pl.multiple_of(core * 32, 32), 32)
    out = refs[-1]
    layer = 1
    if len(refs) == 2:
        layer, gains = 0, refs[0]
        pair = [jnp.concatenate([gains[l, 0:1, :], gains[l, 1:2, :]], axis=1).astype(f32) for l in range(2)]
        row = lax.broadcasted_iota(jnp.int32, (32, 128), 0)
        out[:, 1536:] = jnp.where(row == 0, pair[0], jnp.where(row == 1, pair[1], 0.0)).astype(bf)
    for at, w in enumerate((q, k, v)):
        out[:, at * 384:at * 384 + 384] = w[layer, rows, :]
    for i in range(3):
        for j in range(2):
            columns = pl.ds(pl.multiple_of(core * 256 + j * 128, 128), 128)
            out[j * 16:j * 16 + 16, 1152 + i * 128:1280 + i * 128] = o[layer, i * 16:i * 16 + 16, columns]


def pack_ffn_kernel(ids, gate, up, down, *outs):
    core = ids[2]
    rows = pl.ds(pl.multiple_of(core * 32, 32), 32)
    for layer, out in enumerate(outs):
        out[:, :1024] = gate[layer, rows, :]
        out[:, 1024:2048] = up[layer, rows, :]
        for i in range(2):
            out[:, 2048 + i * 512:2560 + i * 512] = (
                down[layer, pl.ds(pl.multiple_of(core * 64 + i * 32, 32), 32), :])


def pack_weights(ids, shards, gains):
    attn, ffn = shards[:4], shards[4:]
    specs = [full(w.shape) for w in attn]
    first = call(pack_attn_kernel, 1, specs + [full(gains.shape)], [full((32, 1664))],
                 [sds((32, 1664), bf)], [], 2, "pack_weights")(ids, *attn, gains)[0]
    third = call(pack_attn_kernel, 1, specs, [full((32, 1536))],
                 [sds((32, 1536), bf)], [], 2, "pack_weights")(ids, *attn)[0]
    second, fourth = call(pack_ffn_kernel, 1, [full(w.shape) for w in ffn], [full((32, 3072))] * 2,
                          [sds((32, 3072), bf)] * 2, [], 2, "pack_weights")(ids, *ffn)
    return first, second, third, fourth


def finish_kernel(ids, own, peer, qw, kw, vw, gw, uw, gain, *refs):
    with_moves = len(refs) > 9
    if with_moves:
        moved, refs, moving_refs = refs[:9], refs[9:18], refs[18:]
        arrive, pass_on, leave = place_moves(ids, moved, *moving_refs)
        arrive()
    q, k, v, o, gate, up, down, gains, table = refs
    first = ids[2] == 0
    base = 0

    def row_sums(*pairs):
        total = None
        for weight, grad in pairs:
            term = weight.astype(f32) * grad
            total = term if total is None else total + term
        ones = jnp.ones((8, total.shape[1]), f32)
        sums = lax.dot_general(ones, total, (((1,), (1,)), ((), ())), preferred_element_type=f32,
                               precision=lax.Precision.HIGHEST)
        return sums[0:1, :]

    for s in (3, 2, 1, 0):
        layer = s // 2
        for core in range(2):
            def part(start, width, rows=slice(0, 32)):
                columns = slice(base + start, base + start + width)
                one, two = own[rows, columns].astype(f32), peer[rows, columns].astype(f32)
                return jnp.where(first, one, two) if core == 0 else jnp.where(first, two, one)

            rows = slice(core * 32, core * 32 + 32)
            if s % 2 == 0:
                for at, w in enumerate((q, k, v)):
                    w[layer, rows, :] = part(at * 384, 384)
                for i in range(3):
                    for j in range(2):
                        o[layer, i * 16:i * 16 + 16, core * 256 + j * 128:core * 256 + j * 128 + 128] = (
                            part(1152 + i * 128, 128, slice(j * 16, j * 16 + 16)))
            else:
                gate[layer, rows, :] = part(0, 1024)
                up[layer, rows, :] = part(1024, 1024)
                for i in range(2):
                    down[layer, core * 64 + i * 32:core * 64 + i * 32 + 32, :] = part(2048 + i * 512, 512)
            if s == 0 and core == 1:
                table[...] = part(1536, 128).T[:6, :]
        if s % 2 == 0:
            sums = row_sums(*((w[layer], grad[layer]) for w, grad in ((qw, q), (kw, k), (vw, v))))
        else:
            sums = row_sums(*((w[layer], grad[layer]) for w, grad in ((gw, gate), (uw, up))))
        gains[layer, s % 2:s % 2 + 1, :] = sums / gain[layer, s % 2:s % 2 + 1, :].astype(f32)
        base += 1536 if s % 2 == 0 else 3072
        if s == 3 and with_moves:
            pass_on()
    if with_moves:
        leave()


def finish(ids, own, peer, shards, gains, shapes, moved=()):
    q, k, v, o, gate, up, down = shards
    args = (own, peer, q, k, v, gate, up, gains)
    anywhere = pl.BlockSpec(memory_space=pl.ANY)
    specs, sizes = [full(array.shape) for array in args], [sds(shape, f32) for shape in shapes]
    out_specs, scratch = [full(shape) for shape in shapes], []
    if moved:
        t, d = moved[0].shape
        specs += [anywhere] * len(moved)
        out_specs.append(anywhere)
        sizes.append(sds((4, t, d), bf))
        scratch = [pltpu.VMEM((4, t, d), bf), pltpu.SemaphoreType.DMA((2, 4))]
    return call(finish_kernel, 1, specs, out_specs, sizes, scratch, 3, "finish")(ids, *args, *moved)


def move(sources, scratch, targets, sems):
    def fetch(ref, at):
        return pltpu.make_async_copy(ref, scratch.at[at], sems.at[0, at])

    def store(at):
        return pltpu.make_async_copy(scratch.at[at], targets[at], sems.at[1, at])

    def arrive():
        for at, options in enumerate(sources):
            for condition, ref in options:
                if condition is None:
                    fetch(ref, at).start()
                else:
                    @pl.when(condition)
                    def _(ref=ref, at=at):
                        fetch(ref, at).start()

    def pass_on():
        for at in range(len(targets)):
            fetch(sources[at][0][1], at).wait()
            store(at).start()

    def leave():
        for at in range(len(targets)):
            store(at).wait()

    return arrive, pass_on, leave


def place_moves(ids, refs, out, scratch, sems):
    own, relay, far = refs[:4], refs[4], refs[5:]
    section = ids[3]
    pick = lambda group: [(section == at, ref) for at, ref in enumerate(group)]
    return move([pick(own), [(None, relay.at[0])], pick(far), [(None, relay.at[1])]], scratch,
                [out.at[section ^ bit] for bit in range(4)], sems)


def place_kernel(ids, *refs):
    for part in place_moves(ids, refs[:9], *refs[9:]):
        part()


def moving(kernel, ids, arrays, out_shape, slots, micros, name):
    anywhere = pl.BlockSpec(memory_space=pl.ANY)
    t, d = arrays[0].shape[-2:]
    return pl.pallas_call(
        kernel,
        grid_spec=pltpu.PrefetchScalarGridSpec(
            num_scalar_prefetch=1, grid=(1,), in_specs=[anywhere] * len(arrays), out_specs=anywhere,
            scratch_shapes=[pltpu.VMEM((slots, t, d), bf), pltpu.SemaphoreType.DMA((2, slots))]),
        out_shape=out_shape, name=name,
        compiler_params=pltpu.CompilerParams(vmem_limit_bytes=vmem_mib[name] << 20),
        cost_estimate=pl.CostEstimate(flops=int(micros * 1.1e9), bytes_accessed=0, transcendentals=0),
    )(ids, *arrays)


def place(ids, own, relay, far):
    return moving(place_kernel, ids, (*own, relay, *far), sds((4,) + own[0].shape, bf), 4, 3, "place")


def relay_kernel(ids, *refs):
    own, far = refs[:4], refs[4:8]
    out, scratch, sems = refs[8:]
    pick = lambda group: [((ids[3] ^ 1) == at, ref) for at, ref in enumerate(group)]
    for part in move([pick(own), pick(far)], scratch, [out.at[0], out.at[1]], sems):
        part()


def relay(ids, own, far):
    t, d = own[0].shape
    both = moving(relay_kernel, ids, (*own, *far), sds((2, t, d), bf), 2, 2, "relay")
    return swapped(both, "section", 1)


def z_shift(values, by):
    half = lax.axis_size("dp") // 2
    pairs = [(z * 2 + y, ((z + by) % half) * 2 + y) for z in range(half) for y in range(2)]
    return lax.ppermute(values, "dp", pairs)


def swapped(values, axis, bit):
    return lax.ppermute(values, axis, [(i, i ^ bit) for i in range(lax.axis_size(axis))])


def after(values, *others):
    return lax.optimization_barrier((values,) + others)[0]


def added(*terms):
    total = terms[0].astype(f32)
    for term in terms[1:]:
        total = total + term.astype(f32)
    return total.astype(bf)


def gather_part(piece, z, previous):
    if previous is not None:
        piece = after(piece, *previous)
    got = [z_shift(piece, by) for by in range(1, 4)]
    column = jnp.stack([lax.select_n((z - at) % 4, piece, *got) for at in range(4)])
    return (column, swapped(column, "dp", 1)), got


def gather_core(column, other, *holds):
    if holds:
        column, other = lax.optimization_barrier((column, other) + holds)[:2]
    return column, other, swapped(column, "section", 1), swapped(other, "section", 1)


def reduce_first(own, other, give_own, give_other, straight, hold=None):
    first = swapped(give_other, "section", 1)
    sent = swapped(added(other, first), "dp", 1)
    got = swapped(give_own, "section", 1)
    step = dict(keep=own, first=first, core=got, y=sent)
    if straight:
        step["terms"] = [added(own[by], got[by], sent[by]) for by in range(4)]
    else:
        step["far"] = swapped(added(own[2:], got[2:], sent[2:] if hold is None else after(sent[2:], hold)), "dp", 2)
    return step


def xor_shift(values, z_bits):
    return swapped(values, "dp", 2 * z_bits)


def reduce_near(step):
    terms = (step["keep"][1], step["core"][1], step["y"][1], step["far"][1])
    return swapped(added(*terms), "dp", 4)


def reduce_last(step):
    if "terms" in step:
        return added(step["terms"][0], *step["near"])
    return added(step["keep"][0], step["core"][0], step["y"][0], step["far"][0], step["near"])


def to_packed(q, k, v, o, gate, up, down):
    o_part = o.reshape(8, 3, 16, 2, 2, 128).transpose(0, 3, 4, 2, 1, 5).reshape(512, 384)
    d_part = down.reshape(16, 2, 32, 512).transpose(0, 2, 1, 3).reshape(512, 1024)
    return jnp.concatenate([q, k, v, o_part], axis=1), jnp.concatenate([gate, up, d_part], axis=1)


def from_packed(attn, ffn):
    q, k, v = (attn[:, at * 384:at * 384 + 384] for at in range(3))
    o = attn[:, 1152:1536].reshape(8, 2, 2, 16, 3, 128).transpose(0, 4, 3, 1, 2, 5).reshape(384, 512)
    down = ffn[:, 2048:].reshape(16, 32, 2, 512).transpose(0, 2, 1, 3).reshape(1024, 512)
    return q, k, v, o, ffn[:, :1024], ffn[:, 1024:2048], down


def parts_of(whole):
    split = whole.reshape(4, 2, 2, 32, whole.shape[1])
    return tuple(split[:, y, core] for core in range(2) for y in range(2))


def whole_of(parts):
    parts = [part[..., :1536] if part.shape[2] == 1664 else part for part in parts]
    parts = [jnp.stack([part[by] for by in z_order]) for part in parts]
    split = jnp.stack(parts).reshape(2, 2, 4, 32, -1).transpose(2, 1, 0, 3, 4)
    return split.reshape(512, -1)


def gains_of(column, other, y):
    small = [part[:, :2, 1536:1664].reshape(4, 2, 2, 64) for part in (column, other)]
    pair = [jnp.where(y == at, small[0], small[1]) for at in range(2)]
    return jnp.stack(pair, axis=3).transpose(1, 2, 0, 3, 4).reshape(2, 2, 512).astype(f32)


def body(inputs, cotangent, segments, observed, q_weight, k_weight, v_weight, o_weight,
         gate_weight, up_weight, down_weight, gains, position_table):
    section = lax.axis_index("section")
    dp = lax.axis_index("dp")
    micro_count, row_count, seq_count, width = inputs.shape
    layers = q_weight.shape[0]
    heads = position_table.shape[1]
    tokens = row_count * seq_count
    shards = (q_weight, k_weight, v_weight, o_weight, gate_weight, up_weight, down_weight)
    eight = lax.axis_size("dp") == 8
    own_ids = jnp.stack([dp // 2, dp % 2, section % 2, section]).astype(jnp.int32)
    ids = own_ids if eight else jnp.stack([0 * dp, 0 * dp, 0 * dp, section]).astype(jnp.int32)

    weights = [None] * 4
    if eight:
        pieces = pack_weights(own_ids, shards, gains)
    else:
        whole = [lax.all_gather(w, "dp", axis=1, tiled=True) for w in shards]
        for layer in range(layers):
            weights[2 * layer], weights[2 * layer + 1] = (
                parts_of(w) for w in to_packed(*(w[layer] for w in whole)))
        gains_all = lax.all_gather(gains, "dp", axis=2, tiled=True).astype(f32)

    x = inputs.reshape(micro_count, tokens, width)
    grad = cotangent.reshape(micro_count, tokens, width)
    seg = lax.dynamic_index_in_dim(segments, section, 0, keepdims=False)
    obs = lax.dynamic_index_in_dim(observed, section, 0, keepdims=False)
    allowed = (seg[:, :, None] == seg[:, None, :]) & (obs[:, :, None] == 1)
    mask = jnp.where(allowed, 0.0, masked).astype(f32)
    mask = jnp.concatenate([mask, mask], axis=2)
    position = jnp.arange(seq_count, dtype=jnp.int32)
    bucket = bucket_of(position[:, None], position[None, :])
    onehot = (bucket[:, :, None] == jnp.arange(position_table.shape[0])[None, None, :]).astype(f32)
    bias = jnp.einsum("jib,bh->jhi", onehot, position_table.astype(f32), precision=lax.Precision.HIGHEST)
    bias = bias.reshape(seq_count, heads * seq_count)

    chip = section // 2

    def across(value, pairs):
        return lax.ppermute(value, "section", pairs)

    arrived = [()] * 4
    if eight:
        previous = None
        for s in range(4):
            weights[s], previous = gather_part(pieces[s], dp // 2, previous)
            arrived[s] = previous
            if s == 1:
                previous = previous + [weights[0][1]]
            if s == 1:
                previous = previous + [weights[0][1]]
            if s == 1:
                previous = previous + [weights[0][1]]
        gains_all = gains_of(*weights[0], dp % 2)

    chip = section // 2

    def both_ways(first, second):
        return swapped(jnp.where(chip == 0, first, second), "section", 2)

    def wait(value, *names):
        others = [steps[s][name] for s, name in names] if eight else []
        return after(value, *others) if others else value

    chip = section // 2

    def both_ways(first, second):
        return swapped(jnp.where(chip == 0, first, second), "section", 2)

    moved = {}

    def wait(value, *names):
        others = [moved[name] for name in names if name in moved]
        return after(value, *others) if others else value

    def gain_of(s):
        return gains_all[s // 2, s % 2][None]

    packed, steps = [None] * 4, [None] * 4

    def passed(s, parts):
        if eight:
            if s == 2:
                parts = list(parts)
                parts[1] = wait(parts[1], *("y3", ))
            for at, names in ((1, ("far3", "core2", "x2", )), (0, ("near3", ))):
                if s == at:
                    parts[3] = wait(parts[3], *names)
            hold = [moved[name] for name in () if s == 0 and name in moved]
            steps[s] = reduce_first(*parts, s in (), *hold)
            moved.update({f"{name}{s}": steps[s][name] for name in ("first", "core", "y", "far") if name in steps[s]})
        else:
            packed[s] = whole_of(parts)

    states, kept = [x], []
    outs, grads, out_far, grad_far = [None] * 4, [None] * 4, [None] * 4, [None] * 4
    for s in range(4):
        feed = states[s]
        if eight:
            if s < 3:
                feed = after(feed, *arrived[s + 1])
            holds = [states[s]] if s in (1, 3) else []
            holds += [weights[at][1] for to, at in ((1, 2),) if to == s]
            weights[s] = gather_core(*weights[s], *holds)
        if s == 3:
            outs[3], last_back, *parts = ffn_both(ids, feed, grad, gain_of(3), weights[3])
            break
        if s % 2 == 0:
            out, *saved = attn_fwd(ids, feed, mask, bias, gain_of(s), weights[s])
        else:
            out, *saved = ffn_fwd(ids, feed, gain_of(s), weights[s])
        states.append(out)
        kept.append(saved)
        outs[s] = out
    out_far[0] = out_far[2] = moved["x1"] = both_ways(outs[2], outs[0])
    passed(3, parts)

    bias_sum = jnp.zeros((seq_count, heads * seq_count), f32)
    grads[3] = grad = input_grad(ids, states[3], last_back, grad, gain_of(3), weights[3], 20)
    out_far[1] = grad_far[3] = moved["x2"] = both_ways(grad, outs[1])
    back, *parts, bias_sum = attn_bwd(
        ids, states[2], *kept[2], wait(grad, "first3", "x1"), gain_of(2), weights[2], bias_sum, False)
    passed(2, parts)
    grads[2] = grad = input_grad(
        ids, states[2], back, grad, gain_of(2), weights[2], 20)
    grads[1], *parts = ffn_bwd(
        ids, states[1], *kept[1], wait(grad, "first2", "y3"), gain_of(1), weights[1])
    passed(1, parts)
    grad = grads[1]
    if eight and 3 in (3,):
        steps[3]["near"] = moved["near3"] = reduce_near(steps[3])
    out_far[3] = grad_far[1] = moved["x3"] = both_ways(outs[3], grad)
    grads[0], *parts, bias_sum = attn_bwd(
        ids, states[0], *kept[0], wait(grad, "first1", "y2", "x2"), gain_of(0), weights[0], bias_sum, True)
    passed(0, parts)
    moved["g0"] = grads[0]
    grad_far[0] = grad_far[2] = moved["x4"] = both_ways(grads[2], wait(grads[0], "x3", "y1"))

    shape = (1, micro_count, row_count, seq_count, width)
    out_relay = relay(ids, outs, out_far[:3] + [wait(out_far[3], "y0")])
    section_outputs = moved["placed"] = place(ids, outs, out_relay, out_far)
    if eight:
        for s, names in ((3, ("y1", )), (2, ("y0", )), (1, ()), (0, ())):
            if "near" in steps[s]:
                continue
            if s in ():
                terms = steps[s]["terms"]
                steps[s]["near"] = [
                    xor_shift(wait(terms[by], *names), z_order[by]) for by in (1, 2, 3)]
                moved[f"near{s}"] = steps[s]["near"][-1]
                continue
            steps[s]["far"] = wait(steps[s]["far"], *names)
            steps[s]["near"] = moved[f"near{s}"] = reduce_near(steps[s])
    grad_relay = moved["relayed"] = relay(ids, grads, grad_far)
    grad_pieces = (*grads, grad_relay, *grad_far)
    section_outputs = section_outputs.reshape(shape)

    if eight:
        own = []
        for group in ((3, 2), (1, 0)):
            both = jnp.concatenate([reduce_last(steps[s]) for s in group], axis=1)
            own.append(added(both, swapped(both, "section", 2)))
        own = jnp.concatenate(own, axis=1)
        shapes = [w.shape for w in shards] + [gains.shape, position_table.shape[::-1]]
        peer = swapped(own, "section", 1)
        *final, table, section_grads = finish(ids, own, peer, shards, gains, shapes, grad_pieces)
        return (section_outputs, section_grads.reshape(shape)) + tuple(final) + (table.T,)

    section_grads = place(ids, grads, grad_relay, grad_far).reshape(shape)
    dense = [from_packed(packed[2 * layer], packed[2 * layer + 1]) for layer in range(layers)]
    final = []
    for at in range(7):
        both = jnp.stack([d[at] for d in dense])
        part = lax.psum_scatter(both, "dp", scatter_dimension=1, tiled=True)
        final.append(lax.psum(part, "section").astype(f32))
    terms = [w.astype(f32) * final[at] for at, w in enumerate(shards)]
    gain_sums = [sum(jnp.sum(terms[at], axis=2) for at in group) for group in ((0, 1, 2), (4, 5))]
    gains_grad = jnp.stack(gain_sums, axis=1) / gains.astype(f32)
    bias_sum = bias_sum.reshape(seq_count, heads, seq_count)
    table = jnp.einsum("jib,jhi->bh", onehot, bias_sum, precision=lax.Precision.HIGHEST)
    return (section_outputs, section_grads) + tuple(final) + (gains_grad, lax.psum(table, ("section", "dp")))


def solution(mesh):
    rows4 = P(None, "dp", None, None)
    rows3 = P(None, "dp", None)
    staged = P("section", None, "dp", None, None)
    return jax.shard_map(
        body,
        mesh=mesh,
        in_specs=(rows4, rows4) + (rows3,) * 9 + (P(None, None, "dp"), P()),
        out_specs=(staged, staged) + (rows3,) * 7 + (P(None, None, "dp"), P()),
        check_vma=False,
    )
```
